128 devices in a mesh: row: 16 (over y_hi, z, core), col: 8 (over y_lo, x).
Axes of the slice: x: 4, y: 4 (y_hi: 2, y_lo: 2; y = y_hi * 2 + y_lo), z: 4, core: 2. Of those that a mesh axis runs over, the one named last changes fastest.
Arguments:
- vectors: bfloat16 [2, 8, 32768], P(None, 'col', 'row'), may hold values from -6 to 6
- lr_left: bfloat16 [16, 8, 32, 8, 4096], P('row', 'col'), may hold values from -0.75 to 0.75
- lr_right: bfloat16 [16, 8, 32, 8, 4096], P('row', 'col'), may hold values from -0.09375 to 0.09375
- tile_rank: int32 [16, 8, 32], P('row', 'col'), may hold values from 0 to 8, as said below
- leaf_values: bfloat16 [16, 8, 8, 512, 512], P('row', 'col'), may hold values from -0.25 to 0.25
- leaf_places: int32 [16, 8, 8, 2], P('row', 'col'), may hold values from 0 to 63, as said below
- cluster_perm: int32 [16, 16384], P('row'), may hold values from 0 to 262143, as said below
- kappa: float32 [64, 32, 128], P('row', 'col'), may hold values from 0.25 to 4
Outputs:
- prior_action: float32 [2, 64, 32, 128], P(None, 'row', 'col')
The draws below stay inside these ranges and needn't reach their ends.
Inputs may be any that keep to these rules, and one draw needn't show every extreme that they name: `tile_rank`: 0 exactly on the tiles that contain a leaf, 1 to 8 on the others. `leaf_places`: the 8 leaves of a block are distinct; entry 0 indexes rows and entry 1 column of the block in units of 512. `cluster_perm`: a permutation of all brick indices; within each aligned block of 2048 entries, every value of entry // 2048 occurs exactly 32 times or not at all.
All inputs are finite; a program needn't handle non-finite values.
Results may differ from the reference program's by a relative error of at most 0.0023.
Values may be sent and summed in bfloat16 or wider, within the bound.
No kernel may reach another device: no remote copies, remote signals or barrier semaphores. Data moves between devices by JAX's collectives and lax.ppermute only.
A program may use at most 64 MiB of HBM per device.

```python
import math
import jax
import jax.numpy as jnp
from jax import lax

NVEC = 2
CX = 4
CY = 4
NZ = 128
TILE_ROWS = 4
TILE_COLS = 8
KMAX = 8
LEAF = 512
NLEAF = 8
PTS_DEV = 2048
BLOCK_ROWS = 16
BLOCK_COLS = 8
ROWS_CL = 16384
COLS_CL = 32768
TS = 4096
NX = 64
NY = 32
POINTS = 262144
CAP = 32
DEVICES = 128


def leaf_layout(key):
    base = jax.random.fold_in(key, 11)
    row_count = ROWS_CL // LEAF
    col_count = COLS_CL // LEAF
    every_key = jax.random.split(base, BLOCK_ROWS * BLOCK_COLS)

    def one_block(single):
        chosen = jax.random.permutation(single, row_count * col_count)[:NLEAF]
        return jnp.stack([chosen // col_count, chosen % col_count], axis=1)
    places = jax.vmap(one_block)(every_key)
    return places.reshape(BLOCK_ROWS, BLOCK_COLS, NLEAF, 2).astype(jnp.int32)


def draw_leaf_places(key, part):
    return leaf_layout(key)


def draw_tile_rank(key, part):
    places = leaf_layout(key)
    tile_ranks = jax.random.randint(jax.random.fold_in(key, 12), (BLOCK_ROWS, BLOCK_COLS, TILE_ROWS * TILE_COLS), 1, KMAX + 1)
    tile_of = places[..., 0] * LEAF // TS * TILE_COLS + places[..., 1] * LEAF // TS
    near_tile = jnp.any(tile_of[..., :, None] == jnp.arange(TILE_ROWS * TILE_COLS)[None, None, None, :], axis=2)
    return jnp.where(near_tile, 0, tile_ranks).astype(jnp.int32)


def draw_cluster_perm(key, part):
    base = jax.random.fold_in(key, 21)
    keys_a, keys_b, keys_c = jax.random.split(base, 3)
    group_total = PTS_DEV // CAP
    offsets = jax.random.permutation(keys_a, DEVICES)[:group_total]
    shuffle = jax.vmap(lambda single: jax.random.permutation(single, PTS_DEV))(jax.random.split(keys_b, DEVICES))
    landing = jax.vmap(lambda single: jax.random.permutation(single, PTS_DEV))(jax.random.split(keys_c, DEVICES))
    source = jnp.arange(DEVICES)[:, None]
    group_id = shuffle // CAP
    target = (source + offsets[group_id]) % DEVICES
    landing_spot = landing[target, shuffle]
    return (target * PTS_DEV + landing_spot).reshape(BLOCK_ROWS, ROWS_CL).astype(jnp.int32)


def levels(own_key, shape, shards, least, largest):
    gain, own = 1.0, jax.random.fold_in(own_key, 6)
    for axis_at, blocks in shards:
        heights = jnp.exp(jax.random.uniform(jax.random.fold_in(own, axis_at), (blocks,), jnp.float32, least / len(shards), largest / len(shards)))
        gain = gain * jnp.repeat(heights, shape[axis_at] // blocks).reshape([-1 if axis == axis_at else 1 for axis in range(len(shape))])
    return gain


def noise(rng, dims, scale, limit, shards=(), held_as=jnp.bfloat16):
    drawn = scale * jax.random.normal(rng, dims, jnp.float32)
    if shards:
        drawn = drawn * levels(rng, dims, shards, -0.22, 0.18)
    return jnp.clip(drawn, -limit, limit).astype(held_as)


def setup_inputs(seed: int = 0) -> dict:
    key_list = jax.random.split(jax.random.key(seed), 9)
    return {
        "vectors": noise(key_list[0], (NVEC, BLOCK_COLS, COLS_CL), 1.0, 6.0, ((1, 8), (2, 16))),
        "lr_left": noise(key_list[1], (BLOCK_ROWS, BLOCK_COLS, TILE_ROWS * TILE_COLS, KMAX, TS), (KMAX * TILE_COLS) ** -0.5, 0.75, ((0, 16), (1, 8))),
        "lr_right": noise(key_list[2], (BLOCK_ROWS, BLOCK_COLS, TILE_ROWS * TILE_COLS, KMAX, TS), TS ** -0.5, 0.09375, ((0, 16), (1, 8))),
        "tile_rank": draw_tile_rank(jax.random.fold_in(key_list[8], 71), 0),
        "leaf_values": noise(key_list[4], (BLOCK_ROWS, BLOCK_COLS, NLEAF, LEAF, LEAF), LEAF ** -0.5, 0.25, ((0, 16), (1, 8))),
        "leaf_places": draw_leaf_places(jax.random.fold_in(key_list[8], 71), 0),
        "cluster_perm": draw_cluster_perm(jax.random.fold_in(key_list[8], 71), 0),
        "kappa": jnp.clip(jnp.exp(math.log(4.0) - 2.7725887 * jax.random.uniform(key_list[7], (NX, NY, NZ), jnp.float32) ** levels(key_list[7], (NX, NY, NZ), ((0, 16), (1, 8)), -0.2, 0.2)), 0.25, 4.0),
    }


def prior_step(padded, stiffness):
    center = padded[:, 1:-1, 1:-1, :]
    flat_pad = jnp.pad(center, ((0, 0), (0, 0), (0, 0), (1, 1)))
    beside = padded[:, 2:, 1:-1, :] + padded[:, :-2, 1:-1, :]
    beside = beside + padded[:, 1:-1, 2:, :] + padded[:, 1:-1, :-2, :]
    beside = beside + flat_pad[..., 2:] + flat_pad[..., :-2]
    return ((6.0 + stiffness) * center - beside) * 0.125


def block_product(far_left, far_right, tile_ranks, leaf_vals, leaf_pos, x_column):
    x_tiles = x_column.reshape(NVEC, TILE_COLS, TS).astype(jnp.float32)
    right_tiles = far_right.reshape(TILE_ROWS, TILE_COLS, KMAX, TS).astype(jnp.float32)
    projected = jnp.einsum('abkp,vbp->abvk', right_tiles, x_tiles)
    rank_mask = (jnp.arange(KMAX)[None, None, :] < tile_ranks.reshape(TILE_ROWS, TILE_COLS)[:, :, None]).astype(jnp.float32)
    projected = lax.optimization_barrier((projected * rank_mask[:, :, None, :]).astype(jnp.bfloat16)).astype(jnp.float32)
    left_tiles = far_left.reshape(TILE_ROWS, TILE_COLS, KMAX, TS).astype(jnp.float32)
    far_part = jnp.einsum('abkp,abvk->vap', left_tiles, projected).reshape(NVEC, ROWS_CL)
    x_sub = x_column.reshape(NVEC, COLS_CL // LEAF, LEAF).astype(jnp.float32)
    picked = x_sub[:, leaf_pos[:, 1], :]
    near_out = jnp.einsum('lqp,vlp->vlq', leaf_vals.astype(jnp.float32), picked)
    near_part = jnp.zeros((NVEC, ROWS_CL // LEAF, LEAF), jnp.float32).at[:, leaf_pos[:, 0], :].add(near_out)
    return far_part + near_part.reshape(NVEC, ROWS_CL)


def reference(vectors, lr_left, lr_right, tile_rank, leaf_values, leaf_places, cluster_perm, kappa):
    columns = jnp.transpose(vectors, (1, 0, 2))

    def one_row(inputs):
        left_row, right_row, rank_row, vals_row, pos_row = inputs

        def add_block(carry, column):
            left_one, right_one, rank_one, vals_one, pos_one, x_one = column
            return carry + block_product(left_one, right_one, rank_one, vals_one, pos_one, x_one), None

        summed, unused = lax.scan(add_block, jnp.zeros((NVEC, ROWS_CL), jnp.float32),
                                  (left_row, right_row, rank_row, vals_row, pos_row, columns))
        return summed

    sums = lax.map(one_row, (lr_left, lr_right, tile_rank, leaf_values, leaf_places))
    action = jnp.transpose(sums, (1, 0, 2)).reshape(NVEC, POINTS)
    bricks = jnp.zeros((NVEC, POINTS), jnp.float32).at[:, cluster_perm.reshape(-1)].set(action)
    field = bricks.reshape(NVEC, BLOCK_ROWS, BLOCK_COLS, CX, CY, NZ)
    field = jnp.transpose(field, (0, 1, 3, 2, 4, 5)).reshape(NVEC, NX, NY, NZ)
    for repeat in range(4):
        padded = jnp.pad(field, ((0, 0), (1, 1), (1, 1), (0, 0)))
        field = prior_step(padded, kappa)
    return field
```

```python
import jax
import jax.numpy as jnp
from jax import lax
from jax.experimental import pallas as pl
from jax.experimental.pallas import tpu as pltpu
from jax.sharding import PartitionSpec as P

NVEC = 2
CX = 4
CY = 4
NZ = 128
TILE_ROWS = 4
TILE_COLS = 8
KMAX = 8
LEAF = 512
NLEAF = 8
PTS = 2048
ROWS = 16
COLS = 8
TS = 4096
CAP = 32
DEV = ROWS * COLS
SLAB = 16
F32 = jnp.float32
BF16 = jnp.bfloat16
NT = (((1,), (1,)), ((), ()))
MIB = 1 << 20


def iota(shape, dim):
    return lax.broadcasted_iota(jnp.int32, shape, dim)


def rank_kernel(perm_ref, rank_ref, place_ref):
    chunk = 256
    upto = jnp.where(iota((chunk, chunk), 0) <= iota((chunk, chunk), 1), 1.0, 0.0).astype(BF16)
    brick = iota((DEV, chunk), 0)
    carry = jnp.zeros((COLS * DEV, 1), F32)
    for j in range(PTS // chunk):
        masks = [
            (perm_ref[0:1, k * PTS + j * chunk : k * PTS + (j + 1) * chunk] >> 11) == brick
            for k in range(COLS)
        ]
        hot = jnp.concatenate([jnp.where(m, 1.0, 0.0).astype(BF16) for m in masks], axis=0)
        count = jnp.dot(hot, upto, preferred_element_type=F32)
        total = count + carry
        for k in range(COLS):
            at = jnp.where(masks[k], total[k * DEV : (k + 1) * DEV], 0.0)
            rank_ref[0:1, k * PTS + j * chunk : k * PTS + (j + 1) * chunk] = (
                jnp.sum(at, axis=0, keepdims=True) - 1.0
            ).astype(jnp.int32)
        carry = total[:, chunk - 1 : chunk]
    col = lax.axis_index("col")
    start = pl.multiple_of(col * PTS, PTS)
    own = perm_ref[0:1, pl.ds(start, PTS)]
    slot = rank_ref[0:1, pl.ds(start, PTS)] + (col % 4) * CAP
    inside = own & (PTS - 1)
    code = ((NZ + (inside & (NZ - 1))) << (inside >> 7)).astype(F32)
    spread = jnp.where(slot == iota((128, PTS), 0), code, 0.0).astype(BF16)
    hot = jnp.where((own >> 11) == iota((DEV, PTS), 0), 1.0, 0.0).astype(BF16)
    place_ref[...] = lax.dot_general(hot, spread, NT, preferred_element_type=F32)


def send_kernel(
    leaf_at,
    x_ref,
    tile_rank_ref,
    perm_ref,
    rank_ref,
    place_ref,
    right_hbm,
    left_hbm,
    leaf_hbm,
    out_ref,
    right,
    left,
    leaves,
    x_rows,
    sums,
    stage,
    sems,
):
    copies = [
        pltpu.make_async_copy(right_hbm, right, sems.at[0]),
        pltpu.make_async_copy(left_hbm, left, sems.at[1]),
        pltpu.make_async_copy(leaf_hbm, leaves, sems.at[2]),
    ]
    for copy in copies:
        copy.start()
    half = TS // PTS
    for s in range(ROWS):
        b, h = divmod(s, half)
        block = x_ref[s].astype(F32)
        x_rows[b : b + 1, h * PTS : (h + 1) * PTS] = block[0:1]
        x_rows[8 + b : 9 + b, h * PTS : (h + 1) * PTS] = block[1:2]
    terms = TILE_ROWS * TILE_COLS * KMAX
    lane = iota((16, terms), 1)
    sub = iota((16, terms), 0)
    widen = jnp.where(
        iota((TILE_ROWS * TILE_COLS, terms), 1) // KMAX
        == iota((TILE_ROWS * TILE_COLS, terms), 0),
        1.0,
        0.0,
    ).astype(BF16)
    ranks = jnp.broadcast_to(tile_rank_ref[...].astype(F32), (16, TILE_ROWS * TILE_COLS))
    rank_lane = jnp.dot(ranks.astype(BF16), widen, preferred_element_type=F32)
    keep = (sub % 8 == (lane // KMAX) % TILE_COLS) & ((lane % KMAX).astype(F32) < rank_lane)
    x_all = x_rows[...].astype(BF16)
    copies[0].wait()
    projected = lax.dot_general(x_all, right[...], NT, preferred_element_type=F32)
    projected = jnp.where(keep, projected, 0.0)
    first = jnp.sum(projected[0:8], axis=0, keepdims=True)
    second = jnp.sum(projected[8:16], axis=0, keepdims=True)
    by_row = jnp.where(sub < 8, first, second)
    by_row = jnp.where(sub % 8 == lane // (TILE_COLS * KMAX), by_row, 0.0).astype(BF16)
    copies[1].wait()
    sums[...] = jnp.dot(by_row, left[...], preferred_element_type=F32)
    copies[2].wait()
    per_tile = TS // LEAF
    for l in range(NLEAF):
        i, j = leaf_at[l, 0], leaf_at[l, 1]
        from_lane = pl.multiple_of((j % per_tile) * LEAF, LEAF)
        to_lane = pl.multiple_of((i % per_tile) * LEAF, LEAF)
        picked = jnp.concatenate(
            [x_rows[pl.ds(8 * v + j // per_tile, 1), pl.ds(from_lane, LEAF)] for v in range(NVEC)],
            axis=0,
        ).astype(BF16)
        near = lax.dot_general(picked, leaves[l], NT, preferred_element_type=F32)
        for v in range(NVEC):
            at = (pl.ds(8 * v + i // per_tile, 1), pl.ds(to_lane, LEAF))
            sums[at] = sums[at] + near[v : v + 1]
    row = iota((DEV, 128), 0) % COLS

    def put(values, first_row, step):
        below = jnp.where(row != 0, pltpu.roll(values, 1, 0), 0.0)
        above = jnp.where(row != COLS - 1, pltpu.roll(values, DEV - 1, 0), 0.0)
        for j, v in enumerate((below, values, above)):
            stage[pl.ds(first_row + j * step, DEV, stride=SLAB), :] = v

    put(place_ref[...], 12, 1)
    stage[pl.ds(15, DEV, stride=SLAB), :] = jnp.zeros((DEV, 128), F32)
    brick = iota((DEV, PTS), 0)
    slots = iota((CAP, PTS), 0)
    for group in range(2):
        parts = []
        for kk in range(4):
            k = group * 4 + kk
            a, h = divmod(k, half)
            at = slice(k * PTS, (k + 1) * PTS)
            hot = jnp.where((perm_ref[0:1, at] >> 11) == brick, 1.0, 0.0).astype(BF16)
            mask = rank_ref[0:1, at] == slots
            spread = jnp.concatenate(
                [
                    jnp.where(mask, sums[8 * v + a : 8 * v + a + 1, h * PTS : (h + 1) * PTS], 0.0)
                    for v in range(NVEC)
                ],
                axis=0,
            ).astype(BF16)
            parts.append(lax.dot_general(hot, spread, NT, preferred_element_type=F32))
        for v in range(NVEC):
            put(
                jnp.concatenate([p[:, v * CAP : (v + 1) * CAP] for p in parts], axis=1),
                group * 2 + v,
                4,
            )
    out_ref[...] = stage[...].astype(BF16)


def receive_kernel(got_ref, field_ref, first, second, values, where, hots):
    for r in range(ROWS):
        base = r * COLS * SLAB
        halves = []
        for g in range(2):
            total = got_ref[base + g * 64 : base + g * 64 + SLAB, :].astype(F32)
            for c in range(1, 4):
                at = base + g * 64 + c * SLAB
                total = total + got_ref[at : at + SLAB, :].astype(F32)
            halves.append(total)
        first[r * SLAB : (r + 1) * SLAB, :] = halves[0]
        second[r * SLAB : (r + 1) * SLAB, :] = halves[1]
    code_a, code_b = first[...], second[...]
    for code, ref in ((code_a, first), (code_b, second)):
        cell = jnp.zeros_like(code)
        for bits in (8, 4, 2, 1):
            big = code >= float(NZ << bits)
            code = jnp.where(big, code * (0.5**bits), code)
            cell = jnp.where(big, cell + float(bits), cell)
        cell = jnp.where(code > 0.0, cell, -1.0)
        ref[...] = code - float(NZ)
        where[0 if ref is first else 1] = cell
    total = code_a + code_b
    total_ref = values.at[0]
    total_ref[...] = total
    sub = iota((8, 128), 0)
    z_row = iota((NZ, 128), 0).astype(F32)
    for j in range(3):
        for r in range(ROWS):
            for g in range(2):
                lanes = slice((r * 2 + g) * 128, (r * 2 + g + 1) * 128)
                at = r * SLAB + j * 4 + g * 2
                pair = jnp.where(sub < 4, total_ref[at : at + 1, :], total_ref[at + 1 : at + 2, :])
                high = pair.astype(BF16).astype(F32)
                low = pair - high
                p = r * SLAB + 12 + j
                cell = where[g, p : p + 1, :]
                z_at = (first if g == 0 else second)[p : p + 1, :]
                wanted = [cell == ((sub % 4) * CY + y).astype(F32) for y in range(CY)]
                rows = jnp.concatenate(
                    [jnp.where(w, part, 0.0) for part in (high, low) for w in wanted], axis=0
                )
                values_at = hots.at[0]
                values_at[0:64, lanes] = rows.astype(BF16)
                hots[1, :, lanes] = jnp.where(z_at == z_row, 1.0, 0.0).astype(BF16)
        both = lax.dot_general(hots[0, 0:64, :], hots[1], NT, preferred_element_type=F32)
        field_ref[j * 32 : (j + 1) * 32, :] = both[0:32] + both[32:64]


def prior_kernel(field_ref, before_ref, after_ref, kappa_ref, kappa_before, kappa_after, out_ref):
    my_row, my_col = lax.axis_index("row"), lax.axis_index("col")
    wide = 3 * CY
    inside_x = [
        jnp.where(my_row > 0, 1.0, 0.0),
        jnp.float32(1.0),
        jnp.where(my_row < ROWS - 1, 1.0, 0.0),
    ]
    inside_y = [
        jnp.where(my_col > 0, 1.0, 0.0),
        jnp.float32(1.0),
        jnp.where(my_col < COLS - 1, 1.0, 0.0),
    ]
    x_at = iota((8, NZ), 0) % CX
    z_at = iota((8, NZ), 1)
    us = [[ref[y] for y in range(wide)] for ref in (before_ref, field_ref, after_ref)]
    ks = [kappa_before, kappa_ref, kappa_after]
    for step in range(1, 5):
        new = [[None] * wide for _ in range(3)]
        up = [[None if u is None else pltpu.roll(u, 1, 0) for u in us[x]] for x in range(3)]
        down = [[None if u is None else pltpu.roll(u, 7, 0) for u in us[x]] for x in range(3)]
        up4 = [[None if u is None else pltpu.roll(u, 5, 0) for u in us[x]] for x in range(3)]
        down4 = [[None if u is None else pltpu.roll(u, 3, 0) for u in us[x]] for x in range(3)]
        for x in range(3):
            if step == 4 and x != 1:
                continue
            for y in range(step, wide - step):
                u = us[x][y]
                lower = up4[x - 1][y] if x > 0 else jnp.zeros_like(u)
                upper = down4[x + 1][y] if x < 2 else jnp.zeros_like(u)
                beside = us[x][y - 1] + us[x][y + 1]
                beside = beside + jnp.where(x_at == 0, lower, up[x][y])
                beside = beside + jnp.where(x_at == CX - 1, upper, down[x][y])
                beside = beside + jnp.where(z_at == 0, 0.0, pltpu.roll(u, 1, 1))
                beside = beside + jnp.where(z_at == NZ - 1, 0.0, pltpu.roll(u, NZ - 1, 1))
                result = ((6.0 + ks[x][y]) * u - beside) * 0.125
                if step < 4:
                    if x != 1 and y // CY != 1:
                        result = result * (inside_x[x] * inside_y[y // CY])
                    elif x != 1:
                        result = result * inside_x[x]
                    elif y // CY != 1:
                        result = result * inside_y[y // CY]
                new[x][y] = result
        us = new
    for y in range(CY):
        out_ref[y] = us[1][CY + y]


def to_both_sides(array, axis):
    size = lax.axis_size(axis)
    before = lax.ppermute(array, axis, [(i, i + 1) for i in range(size - 1)])
    after = lax.ppermute(array, axis, [(i + 1, i) for i in range(size - 1)])
    return before, after


def cost(flops, size):
    return pl.CostEstimate(flops=flops, bytes_accessed=size, transcendentals=0)


def per_device(
    vectors, lr_left, lr_right, tile_rank, leaf_values, leaf_places, cluster_perm, kappa
):
    vmem = pl.BlockSpec(memory_space=pltpu.VMEM)
    smem = pl.BlockSpec(memory_space=pltpu.SMEM)
    anywhere = pl.BlockSpec(memory_space=pl.ANY)
    points = ROWS // 2 * PTS
    x_all = lax.all_to_all(
        jnp.broadcast_to(vectors[:, 0][None], (ROWS, NVEC, PTS)), "row", 0, 0, tiled=True
    )
    rank, place = pl.pallas_call(
        rank_kernel,
        out_shape=(
            jax.ShapeDtypeStruct((1, points), jnp.int32),
            jax.ShapeDtypeStruct((DEV, 128), F32),
        ),
        in_specs=[vmem],
        out_specs=(vmem, vmem),
        compiler_params=pltpu.CompilerParams(vmem_limit_bytes=24 * MIB),
        cost_estimate=cost(1 << 31, 1 << 20),
        name="slots",
    )(cluster_perm)
    kappa_own = jnp.transpose(kappa, (1, 0, 2))
    kappa_own = jnp.concatenate([kappa_own, kappa_own], axis=1)
    low, high = to_both_sides(kappa_own, "col")
    kappa_own = jnp.concatenate([low, kappa_own, high], axis=0)
    kappa_before, kappa_after = to_both_sides(kappa_own, "row")
    terms = TILE_ROWS * TILE_COLS * KMAX
    send = pl.pallas_call(
        send_kernel,
        out_shape=jax.ShapeDtypeStruct((DEV * SLAB, 128), BF16),
        in_specs=[smem, vmem, vmem, vmem, vmem, vmem, anywhere, anywhere, anywhere],
        out_specs=vmem,
        scratch_shapes=[
            pltpu.VMEM((terms, TS), BF16),
            pltpu.VMEM((terms, TS), BF16),
            pltpu.VMEM((NLEAF, LEAF, LEAF), BF16),
            pltpu.VMEM((16, TS), F32),
            pltpu.VMEM((16, TS), F32),
            pltpu.VMEM((DEV * SLAB, 128), F32),
            pltpu.SemaphoreType.DMA((3,)),
        ],
        compiler_params=pltpu.CompilerParams(vmem_limit_bytes=32 * MIB),
        cost_estimate=cost(1 << 31, 8 << 20),
        name="partial_sums",
    )(
        leaf_places[0, 0],
        x_all,
        tile_rank[0],
        cluster_perm,
        rank,
        place,
        lr_right.reshape(terms, TS),
        lr_left.reshape(terms, TS),
        leaf_values[0, 0],
    )
    got = lax.all_to_all(send.reshape(DEV, SLAB, 128), ("row", "col"), 0, 0, tiled=True)
    field = pl.pallas_call(
        receive_kernel,
        out_shape=jax.ShapeDtypeStruct((3 * CY * NVEC * CX, NZ), F32),
        in_specs=[vmem],
        out_specs=vmem,
        scratch_shapes=[
            pltpu.VMEM((ROWS * SLAB, 128), F32),
            pltpu.VMEM((ROWS * SLAB, 128), F32),
            pltpu.VMEM((1, ROWS * SLAB, 128), F32),
            pltpu.VMEM((2, ROWS * SLAB, 128), F32),
            pltpu.VMEM((2, NZ, 4096), BF16),
        ],
        compiler_params=pltpu.CompilerParams(vmem_limit_bytes=24 * MIB),
        cost_estimate=cost(1 << 30, 1 << 20),
        name="bricks",
    )(got.reshape(DEV * SLAB, 128))
    field = field.reshape(3 * CY, NVEC * CX, NZ)
    before, after = to_both_sides(field, "row")
    out = pl.pallas_call(
        prior_kernel,
        out_shape=jax.ShapeDtypeStruct((CY, NVEC * CX, NZ), F32),
        in_specs=[vmem] * 6,
        out_specs=vmem,
        cost_estimate=cost(1 << 24, 1 << 20),
        name="prior",
    )(field, before, after, kappa_own, kappa_before, kappa_after)
    return jnp.transpose(out.reshape(CY, NVEC, CX, NZ), (1, 2, 0, 3))


def solution(mesh):
    in_specs = (
        P(None, "col", "row"),
        P("row", "col", None, None, None),
        P("row", "col", None, None, None),
        P("row", "col", None),
        P("row", "col", None, None, None),
        P("row", "col", None, None),
        P("row", None),
        P("row", "col", None),
    )
    out_specs = P(None, "row", "col", None)
    return jax.shard_map(
        per_device, mesh=mesh, in_specs=in_specs, out_specs=out_specs, check_vma=False
    )
```

```python
import jax
import jax.numpy as jnp
from jax import lax
from jax.experimental import pallas as pl
from jax.experimental.pallas import tpu as pltpu
from jax.sharding import PartitionSpec as P

NVEC = 2
CX = 4
CY = 4
NZ = 128
TILE_ROWS = 4
TILE_COLS = 8
KMAX = 8
LEAF = 512
NLEAF = 8
PTS = 2048
ROWS = 16
COLS = 8
TS = 4096
CAP = 32
DEV = ROWS * COLS
SLAB = 16
F32 = jnp.float32
BF16 = jnp.bfloat16
NT = (((1,), (1,)), ((), ()))
MIB = 1 << 20
LEVELS = 64.0
STEPS = 32000.0
FIELD = 3 * CX * NVEC * CY


def iota(shape, dim):
    return lax.broadcasted_iota(jnp.int32, shape, dim)


def pack_kernel(vectors_ref, kappa_ref, out_ref):
    rows = [kappa_ref[q // CY, q % CY : q % CY + 1, :] for q in range(CX * CY)]
    half = CX * CY // NVEC
    for s in range(ROWS):
        out_ref[s, :, 0:PTS] = vectors_ref[...]
    for q in range(half):
        pair = jnp.concatenate([rows[q], rows[half + q]], axis=0).astype(BF16)
        for s in range(ROWS):
            out_ref[s, :, PTS + q * NZ : PTS + (q + 1) * NZ] = pair


def slots_kernel(
    perm_ref, right_hbm, left_hbm, leaf_hbm, rank_ref, place_ref, right, left, leaves, sems
):
    copies = [
        pltpu.make_async_copy(right_hbm, right, sems.at[0]),
        pltpu.make_async_copy(leaf_hbm, leaves, sems.at[1]),
        pltpu.make_async_copy(left_hbm, left, sems.at[2]),
    ]
    for copy in copies:
        copy.start()
    chunk = 256
    upto = jnp.where(iota((chunk, chunk), 0) <= iota((chunk, chunk), 1), 1.0, 0.0).astype(BF16)
    brick = iota((DEV, chunk), 0)
    carry = jnp.zeros((COLS * DEV, 1), F32)
    for j in range(PTS // chunk):
        masks = [
            (perm_ref[0:1, k * PTS + j * chunk : k * PTS + (j + 1) * chunk] >> 11) == brick
            for k in range(COLS)
        ]
        hot = jnp.concatenate([jnp.where(m, 1.0, 0.0).astype(BF16) for m in masks], axis=0)
        count = jnp.dot(hot, upto, preferred_element_type=F32)
        total = count + carry
        for k in range(COLS):
            at = jnp.where(masks[k], total[k * DEV : (k + 1) * DEV], 0.0)
            rank_ref[0:1, k * PTS + j * chunk : k * PTS + (j + 1) * chunk] = (
                jnp.sum(at, axis=0, keepdims=True) - 1.0
            ).astype(jnp.int32)
        carry = total[:, chunk - 1 : chunk]
    col = lax.axis_index("col")
    start = pl.multiple_of(col * PTS, PTS)
    own = perm_ref[0:1, pl.ds(start, PTS)]
    slot = rank_ref[0:1, pl.ds(start, PTS)] + (col % 4) * CAP
    here = slot == iota((128, PTS), 0)
    inside = own & (PTS - 1)
    coarse = jnp.where(here, (inside & ~(NZ - 1)).astype(F32), 0.0).astype(BF16)
    fine = jnp.where(here, (inside & (NZ - 1)).astype(F32) + 1.0, 0.0).astype(BF16)
    hot = jnp.where((own >> 11) == iota((DEV, PTS), 0), 1.0, 0.0).astype(BF16)
    place_ref[...] = lax.dot_general(
        hot, coarse, NT, preferred_element_type=F32
    ) + lax.dot_general(hot, fine, NT, preferred_element_type=F32)
    for copy in copies:
        copy.wait()


def send_kernel(
    leaf_at,
    x_ref,
    tile_rank_ref,
    perm_ref,
    rank_ref,
    place_ref,
    right,
    left,
    leaves,
    out_ref,
    x_rows,
    sums,
    stage,
):
    half = TS // PTS
    for s in range(ROWS):
        b, h = divmod(s, half)
        block = x_ref[s, :, 0:PTS].astype(F32)
        x_rows[b : b + 1, h * PTS : (h + 1) * PTS] = block[0:1]
        x_rows[8 + b : 9 + b, h * PTS : (h + 1) * PTS] = block[1:2]
    terms = TILE_ROWS * TILE_COLS * KMAX
    lane = iota((16, terms), 1)
    sub = iota((16, terms), 0)
    widen = jnp.where(
        iota((TILE_ROWS * TILE_COLS, terms), 1) // KMAX
        == iota((TILE_ROWS * TILE_COLS, terms), 0),
        1.0,
        0.0,
    ).astype(BF16)
    ranks = jnp.broadcast_to(tile_rank_ref[...].astype(F32), (16, TILE_ROWS * TILE_COLS))
    rank_lane = jnp.dot(ranks.astype(BF16), widen, preferred_element_type=F32)
    keep = (sub % 8 == (lane // KMAX) % TILE_COLS) & ((lane % KMAX).astype(F32) < rank_lane)
    x_all = x_rows[...].astype(BF16)
    projected = lax.dot_general(x_all, right[...], NT, preferred_element_type=F32)
    projected = jnp.where(keep, projected, 0.0)
    first = jnp.sum(projected[0:8], axis=0, keepdims=True)
    second = jnp.sum(projected[8:16], axis=0, keepdims=True)
    by_row = jnp.where(sub < 8, first, second)
    by_row = jnp.where(sub % 8 == lane // (TILE_COLS * KMAX), by_row, 0.0).astype(BF16)
    sums[...] = jnp.dot(by_row, left[...], preferred_element_type=F32)
    per_tile = TS // LEAF
    for l in range(NLEAF):
        i, j = leaf_at[0, 0, l, 0], leaf_at[0, 0, l, 1]
        from_lane = pl.multiple_of((j % per_tile) * LEAF, LEAF)
        to_lane = pl.multiple_of((i % per_tile) * LEAF, LEAF)
        picked = jnp.concatenate(
            [x_rows[pl.ds(8 * v + j // per_tile, 1), pl.ds(from_lane, LEAF)] for v in range(NVEC)],
            axis=0,
        ).astype(BF16)
        near = lax.dot_general(picked, leaves[l], NT, preferred_element_type=F32)
        for v in range(NVEC):
            at = (pl.ds(8 * v + i // per_tile, 1), pl.ds(to_lane, LEAF))
            sums[at] = sums[at] + near[v : v + 1]
    largest = jnp.max(jnp.abs(sums[...]), axis=0, keepdims=True)
    largest = jnp.broadcast_to(jnp.max(largest, axis=1, keepdims=True), (8, 128))
    level = jnp.ceil(jnp.maximum(jnp.log2(largest), -100.0) * LEVELS)
    inverse = (STEPS * jnp.exp2(level * (-1.0 / LEVELS)))[0:1]

    def put(values, first_row, step):
        none = jnp.zeros((COLS, 128), F32)
        stage[pl.ds(first_row, COLS, stride=SLAB), :] = none
        stage[pl.ds(first_row + COLS * SLAB, DEV - COLS, stride=SLAB), :] = values[: DEV - COLS]
        stage[pl.ds(first_row + step, DEV, stride=SLAB), :] = values
        at = first_row + 2 * step
        stage[pl.ds(at, DEV - COLS, stride=SLAB), :] = values[COLS:]
        stage[pl.ds(at + (DEV - COLS) * SLAB, COLS, stride=SLAB), :] = none

    put(place_ref[...], 12, 1)
    stage[pl.ds(15, DEV, stride=SLAB), :] = jnp.broadcast_to(level[0:1], (DEV, 128))
    brick = iota((DEV, PTS), 0)
    slots = iota((CAP, PTS), 0)
    for group in range(2):
        parts = []
        for kk in range(4):
            k = group * 4 + kk
            a, h = divmod(k, half)
            at = slice(k * PTS, (k + 1) * PTS)
            hot = jnp.where((perm_ref[0:1, at] >> 11) == brick, 1.0, 0.0).astype(BF16)
            mask = rank_ref[0:1, at] == slots
            rows = [sums[8 * v + a : 8 * v + a + 1, h * PTS : (h + 1) * PTS] for v in range(NVEC)]
            highs = [row.astype(BF16).astype(F32) for row in rows]
            lows = [row - high for row, high in zip(rows, highs)]
            spread = jnp.concatenate(
                [jnp.where(mask, row, 0.0).astype(BF16) for row in highs + lows], axis=0
            )
            part = lax.dot_general(hot, spread, NT, preferred_element_type=F32)
            parts.append(part + pltpu.roll(part, NVEC * CAP, 1))
        for v in range(NVEC):
            values = jnp.concatenate([p[:, v * CAP : (v + 1) * CAP] for p in parts], axis=1)
            put(jnp.round(values * inverse), group * 2 + v, 4)
    out_ref[...] = stage[...].astype(jnp.int32).astype(jnp.int16)


def bricks_kernel(got_ref, packed_ref, kappa_ref, out_ref, sums, wheres, at_cells, hots):
    for r in range(ROWS):
        for g in range(2):
            total = None
            for c in range(4):
                at = ((r * 2 + g) * 4 + c) * SLAB
                one = got_ref[at : at + SLAB, :].astype(jnp.int32).astype(F32)
                size = jnp.exp2(one[15:16] * (1.0 / LEVELS)) * (1.0 / STEPS)
                one = jnp.where(iota((SLAB, 128), 0) < 12, one * size, one)
                total = one if total is None else total + one
            wheres[g, r * SLAB : (r + 1) * SLAB, :] = total
    sums[...] = wheres[0] + wheres[1]
    for g in range(2):
        place = wheres[g] - 1.0
        cell = jnp.floor(place * (1.0 / NZ))
        at_cells[g] = cell
        wheres[g] = place - cell * NZ
    sub = iota((8, 128), 0)
    z_row = iota((NZ, 128), 0).astype(F32)
    for j in range(3):
        for r in range(ROWS):
            for g in range(2):
                lanes = slice((r * 2 + g) * 128, (r * 2 + g + 1) * 128)
                at = r * SLAB + j * 4 + g * 2
                pair = jnp.where(sub < 4, sums[at : at + 1, :], sums[at + 1 : at + 2, :])
                high = pair.astype(BF16).astype(F32)
                low = pair - high
                p = r * SLAB + 12 + j
                cell = at_cells[g, p : p + 1, :]
                z_at = wheres[g, p : p + 1, :]
                wanted = [cell == (x * CY + sub % CY).astype(F32) for x in range(CX)]
                rows = jnp.concatenate(
                    [jnp.where(w, part, 0.0) for part in (high, low) for w in wanted], axis=0
                )
                hots[0, 0:64, lanes] = rows.astype(BF16)
                hots[1, :, lanes] = jnp.where(z_at == z_row, 1.0, 0.0).astype(BF16)
        both = lax.dot_general(hots[0, 0:64, :], hots[1], NT, preferred_element_type=F32)
        out_ref[j * 32 : (j + 1) * 32, :] = both[0:32] + both[32:64]
    my_row = lax.axis_index("row")
    half = CX * CY // NVEC
    for j, r in ((0, jnp.maximum(my_row - 1, 0)), (2, jnp.minimum(my_row + 1, ROWS - 1))):
        block = packed_ref[r, :, PTS:].astype(F32)
        for q in range(half):
            for v in range(NVEC):
                at = FIELD + j * CX * CY + v * half + q
                out_ref[at : at + 1, :] = block[v : v + 1, q * NZ : (q + 1) * NZ]
    for x in range(CX):
        at = FIELD + CX * CY + x * CY
        out_ref[at : at + CY, :] = kappa_ref[x]


def prior_kernel(own_ref, before_ref, after_ref, out_ref):
    my_row, my_col = lax.axis_index("row"), lax.axis_index("col")
    wide = 3 * CX
    inside_x = [
        jnp.where(my_row > 0, 1.0, 0.0),
        jnp.float32(1.0),
        jnp.where(my_row < ROWS - 1, 1.0, 0.0),
    ]
    inside_y = [
        jnp.where(my_col > 0, 1.0, 0.0),
        jnp.float32(1.0),
        jnp.where(my_col < COLS - 1, 1.0, 0.0),
    ]
    y_at = iota((8, NZ), 0) % CY
    z_at = iota((8, NZ), 1)
    refs = (before_ref, own_ref, after_ref)
    us = [[ref[8 * x : 8 * x + 8, :] for x in range(wide)] for ref in refs]
    ks = []
    for ref in refs:
        rows = [ref[FIELD + CY * x : FIELD + CY * (x + 1), :] for x in range(wide)]
        ks.append([6.0 + jnp.concatenate([row, row], axis=0) for row in rows])
    for step in range(1, 5):
        new = [[None] * wide for _ in range(3)]
        for b in range(3):
            if step == 4 and b != 1:
                continue
            for x in range(step, wide - step):
                u = us[b][x]
                lower = pltpu.roll(us[b - 1][x], 5, 0) if b > 0 else 0.0
                upper = pltpu.roll(us[b + 1][x], 3, 0) if b < 2 else 0.0
                beside = us[b][x - 1] + us[b][x + 1]
                beside = beside + jnp.where(y_at == 0, lower, pltpu.roll(u, 1, 0))
                beside = beside + jnp.where(y_at == CY - 1, upper, pltpu.roll(u, 7, 0))
                beside = beside + jnp.where(z_at == 0, 0.0, pltpu.roll(u, 1, 1))
                beside = beside + jnp.where(z_at == NZ - 1, 0.0, pltpu.roll(u, NZ - 1, 1))
                result = (ks[b][x] * u - beside) * 0.125
                if step < 4:
                    if b != 1 and x // CX != 1:
                        result = result * (inside_y[b] * inside_x[x // CX])
                    elif b != 1:
                        result = result * inside_y[b]
                    elif x // CX != 1:
                        result = result * inside_x[x // CX]
                new[b][x] = result
        us = new
    for x in range(CX):
        for v in range(NVEC):
            out_ref[v, x] = us[1][CX + x][v * CY : (v + 1) * CY]


def to_both_sides(array, axis):
    size = lax.axis_size(axis)
    before = lax.ppermute(array, axis, [(i, i + 1) for i in range(size - 1)])
    after = lax.ppermute(array, axis, [(i + 1, i) for i in range(size - 1)])
    return before, after


def cost(flops, size):
    return pl.CostEstimate(flops=flops, bytes_accessed=size, transcendentals=0)


def params(mib):
    return pltpu.CompilerParams(vmem_limit_bytes=mib * MIB)


def per_device(
    vectors, lr_left, lr_right, tile_rank, leaf_values, leaf_places, cluster_perm, kappa
):
    vmem = pl.BlockSpec(memory_space=pltpu.VMEM)
    smem = pl.BlockSpec(memory_space=pltpu.SMEM)
    hbm = pl.BlockSpec(memory_space=pltpu.HBM)
    points = COLS * PTS
    terms = TILE_ROWS * TILE_COLS * KMAX
    shape = jax.ShapeDtypeStruct
    packed = pl.pallas_call(
        pack_kernel,
        out_shape=shape((ROWS, NVEC, PTS + PTS // NVEC), BF16),
        in_specs=[vmem] * 2,
        out_specs=vmem,
        compiler_params=params(8),
        name="pack",
    )(vectors[:, 0], kappa)
    packed = lax.all_to_all(packed, "row", 0, 0, tiled=True)
    rank, place, right, left, leaves = pl.pallas_call(
        slots_kernel,
        out_shape=(
            shape((1, points), jnp.int32),
            shape((DEV, 128), F32),
            shape((terms, TS), BF16),
            shape((terms, TS), BF16),
            shape((NLEAF, LEAF, LEAF), BF16),
        ),
        in_specs=[vmem, hbm, hbm, hbm],
        out_specs=(vmem,) * 5,
        scratch_shapes=[pltpu.SemaphoreType.DMA((3,))],
        compiler_params=params(20),
        cost_estimate=cost(1 << 31, 1 << 20),
        name="slots",
    )(
        cluster_perm,
        lr_right.reshape(terms, TS),
        lr_left.reshape(terms, TS),
        leaf_values[0, 0],
    )
    send = pl.pallas_call(
        send_kernel,
        out_shape=shape((DEV * SLAB, 128), jnp.int16),
        in_specs=[smem] + [vmem] * 8,
        out_specs=vmem,
        scratch_shapes=[
            pltpu.VMEM((16, TS), F32),
            pltpu.VMEM((16, TS), F32),
            pltpu.VMEM((DEV * SLAB, 128), F32),
        ],
        compiler_params=params(20),
        cost_estimate=cost(1 << 31, 8 << 20),
        name="partial_sums",
    )(leaf_places, packed, tile_rank[0], cluster_perm, rank, place, right, left, leaves)
    got = lax.all_to_all(send.reshape(DEV, SLAB, 128), ("row", "col"), 0, 0, tiled=True)
    own = pl.pallas_call(
        bricks_kernel,
        out_shape=shape((FIELD + 3 * CX * CY, NZ), F32),
        in_specs=[vmem] * 3,
        out_specs=vmem,
        scratch_shapes=[
            pltpu.VMEM((ROWS * SLAB, 128), F32),
            pltpu.VMEM((2, ROWS * SLAB, 128), F32),
            pltpu.VMEM((2, ROWS * SLAB, 128), F32),
            pltpu.VMEM((2, NZ, 4096), BF16),
        ],
        compiler_params=params(16),
        cost_estimate=cost(1 << 30, 1 << 20),
        name="bricks",
    )(got.reshape(DEV * SLAB, 128), packed, kappa)
    before, after = to_both_sides(own, "col")
    return pl.pallas_call(
        prior_kernel,
        out_shape=shape((NVEC, CX, CY, NZ), F32),
        in_specs=[vmem] * 3,
        out_specs=vmem,
        compiler_params=params(8),
        cost_estimate=cost(1 << 24, 1 << 20),
        name="prior",
    )(own, before, after)


def solution(mesh):
    in_specs = (
        P(None, "col", "row"),
        P("row", "col", None, None, None),
        P("row", "col", None, None, None),
        P("row", "col", None),
        P("row", "col", None, None, None),
        P("row", "col", None, None),
        P("row", None),
        P("row", "col", None),
    )
    out_specs = P(None, "row", "col", None)
    return jax.shard_map(
        per_device, mesh=mesh, in_specs=in_specs, out_specs=out_specs, check_vma=False
    )
```

```python
import jax
import jax.numpy as jnp
from jax import lax
from jax.experimental import pallas as pl
from jax.experimental.pallas import tpu as pltpu
from jax.sharding import PartitionSpec as P

NVEC = 2
CX = 4
CY = 4
NZ = 128
TILE_ROWS = 4
TILE_COLS = 8
KMAX = 8
LEAF = 512
NLEAF = 8
PTS = 2048
ROWS = 16
COLS = 8
TS = 4096
CAP = 32
DEV = ROWS * COLS
SLAB = 16
F32 = jnp.float32
BF16 = jnp.bfloat16
NT = (((1,), (1,)), ((), ()))
MIB = 1 << 20
LEVELS = 64.0
STEPS = 32000.0
KAPPA_STEPS = 8000.0
FIELD = 3 * CX * NVEC * CY
HALO = FIELD - 2 * NVEC * CY


def iota(shape, dim):
    return lax.broadcasted_iota(jnp.int32, shape, dim)


def pack_kernel(
    vectors_hbm, kappa_hbm, perm_hbm, rank_hbm, out_ref, kappa_ref, perm_ref, rank_ref, vectors, sems
):
    pairs = (
        (vectors_hbm, vectors),
        (kappa_hbm, kappa_ref),
        (perm_hbm, perm_ref),
        (rank_hbm, rank_ref),
    )
    copies = [pltpu.make_async_copy(a, b, sems.at[i]) for i, (a, b) in enumerate(pairs)]
    for copy in copies:
        copy.start()
    copies[0].wait()
    for s in range(ROWS):
        out_ref[s, :, 0:PTS] = vectors[...]
    copies[1].wait()
    rows = [kappa_ref[q // CY, q % CY : q % CY + 1, :] for q in range(CX * CY)]
    half = CX * CY // NVEC
    for q in range(half):
        pair = jnp.concatenate([rows[q], rows[half + q]], axis=0).astype(BF16)
        for s in range(ROWS):
            out_ref[s, :, PTS + q * NZ : PTS + (q + 1) * NZ] = pair
    copies[2].wait()
    copies[3].wait()


def slots_kernel(
    perm_ref,
    right_hbm,
    left_hbm,
    leaf_hbm,
    hot_ref,
    slot_ref,
    place_ref,
    right,
    left,
    leaves,
    sems,
):
    copies = [
        pltpu.make_async_copy(right_hbm, right, sems.at[0]),
        pltpu.make_async_copy(left_hbm, left, sems.at[1]),
        pltpu.make_async_copy(leaf_hbm, leaves, sems.at[2]),
    ]
    for copy in copies:
        copy.start()
    chunk = 256
    upto = jnp.where(iota((chunk, chunk), 0) <= iota((chunk, chunk), 1), 1.0, 0.0).astype(BF16)
    brick = iota((DEV, chunk), 0)
    slots = iota((CAP, chunk), 0).astype(F32)
    carry = jnp.zeros((COLS * DEV, 1), F32)
    for j in range(PTS // chunk):
        lanes = slice(j * chunk, (j + 1) * chunk)
        masks = [
            (perm_ref[0:1, k * PTS + j * chunk : k * PTS + (j + 1) * chunk] >> 11) == brick
            for k in range(COLS)
        ]
        hot = jnp.concatenate([jnp.where(m, 1.0, 0.0).astype(BF16) for m in masks], axis=0)
        hot_ref[:, lanes] = hot
        total = jnp.dot(hot, upto, preferred_element_type=F32) + carry
        for k in range(COLS):
            at = jnp.where(masks[k], total[k * DEV : (k + 1) * DEV], 0.0)
            rank = jnp.sum(at, axis=0, keepdims=True) - 1.0
            slot_ref[k * CAP : (k + 1) * CAP, lanes] = jnp.where(rank == slots, 1.0, 0.0).astype(
                BF16
            )
        carry = total[:, chunk - 1 : chunk]
    col = lax.axis_index("col")
    own = perm_ref[0:1, pl.ds(pl.multiple_of(col * PTS, PTS), PTS)]
    here = slot_ref[pl.ds(pl.multiple_of(col * CAP, CAP), CAP), :]
    hot = hot_ref[pl.ds(pl.multiple_of(col * DEV, DEV), DEV), :]
    inside = own & (PTS - 1)
    place = jnp.zeros((DEV, 128), F32)
    for part in (inside & ~(NZ - 1), (inside & (NZ - 1)) + 1):
        spread = here * part.astype(F32).astype(BF16)
        spread = jnp.concatenate(
            [spread * jnp.where(col % 4 == g, 1.0, 0.0).astype(BF16) for g in range(4)], axis=0
        )
        place = place + lax.dot_general(hot, spread, NT, preferred_element_type=F32)
    place_ref[...] = place
    for copy in copies:
        copy.wait()


def level_of(values):
    largest = jnp.max(jnp.abs(values), axis=0, keepdims=True)
    largest = jnp.broadcast_to(jnp.max(largest, axis=1, keepdims=True), (8, 128))
    level = jnp.ceil(jnp.maximum(jnp.log2(largest), -100.0) * LEVELS)
    return level[0:1], (STEPS * jnp.exp2(level * (-1.0 / LEVELS)))[0:1]


def step_at(level):
    return jnp.exp2(level * (1.0 / LEVELS)) * (1.0 / STEPS)


def send_kernel(
    leaf_hbm,
    x_ref,
    tile_rank_ref,
    hot_ref,
    slot_ref,
    place_ref,
    right,
    left,
    leaves,
    out_ref,
    x_rows,
    sums,
    stage,
    leaf_at,
    sem,
):
    leaf_copy = pltpu.make_async_copy(leaf_hbm, leaf_at, sem)
    leaf_copy.start()
    half = TS // PTS
    for s in range(ROWS):
        b, h = divmod(s, half)
        block = x_ref[s, :, 0:PTS].astype(F32)
        x_rows[b : b + 1, h * PTS : (h + 1) * PTS] = block[0:1]
        x_rows[8 + b : 9 + b, h * PTS : (h + 1) * PTS] = block[1:2]
    terms = TILE_ROWS * TILE_COLS * KMAX
    lane = iota((16, terms), 1)
    sub = iota((16, terms), 0)
    widen = jnp.where(
        iota((TILE_ROWS * TILE_COLS, terms), 1) // KMAX
        == iota((TILE_ROWS * TILE_COLS, terms), 0),
        1.0,
        0.0,
    ).astype(BF16)
    ranks = jnp.broadcast_to(tile_rank_ref[...].astype(F32), (16, TILE_ROWS * TILE_COLS))
    rank_lane = jnp.dot(ranks.astype(BF16), widen, preferred_element_type=F32)
    keep = (sub % 8 == (lane // KMAX) % TILE_COLS) & ((lane % KMAX).astype(F32) < rank_lane)
    x_all = x_rows[...].astype(BF16)
    projected = lax.dot_general(x_all, right[...], NT, preferred_element_type=F32)
    projected = jnp.where(keep, projected, 0.0)
    first = jnp.sum(projected[0:8], axis=0, keepdims=True)
    second = jnp.sum(projected[8:16], axis=0, keepdims=True)
    by_row = jnp.where(sub < 8, first, second)
    by_row = jnp.where(sub % 8 == lane // (TILE_COLS * KMAX), by_row, 0.0).astype(BF16)
    sums[...] = jnp.dot(by_row, left[...], preferred_element_type=F32)
    leaf_copy.wait()
    per_tile = TS // LEAF
    for l in range(NLEAF):
        i, j = leaf_at[0, l], leaf_at[1, l]
        from_lane = pl.multiple_of((j % per_tile) * LEAF, LEAF)
        to_lane = pl.multiple_of((i % per_tile) * LEAF, LEAF)
        picked = jnp.concatenate(
            [x_rows[pl.ds(8 * v + j // per_tile, 1), pl.ds(from_lane, LEAF)] for v in range(NVEC)],
            axis=0,
        ).astype(BF16)
        near = lax.dot_general(picked, leaves[l], NT, preferred_element_type=F32)
        for v in range(NVEC):
            at = (pl.ds(8 * v + i // per_tile, 1), pl.ds(to_lane, LEAF))
            sums[at] = sums[at] + near[v : v + 1]
    level, inverse = level_of(sums[...])

    def put(values, first_row, step):
        none = jnp.zeros((COLS, 128), F32)
        stage[pl.ds(first_row, COLS, stride=SLAB), :] = none
        stage[pl.ds(first_row + COLS * SLAB, DEV - COLS, stride=SLAB), :] = values[: DEV - COLS]
        stage[pl.ds(first_row + step, DEV, stride=SLAB), :] = values
        at = first_row + 2 * step
        stage[pl.ds(at, DEV - COLS, stride=SLAB), :] = values[COLS:]
        stage[pl.ds(at + (DEV - COLS) * SLAB, COLS, stride=SLAB), :] = none

    put(place_ref[...], 12, 1)
    stage[pl.ds(15, DEV, stride=SLAB), :] = jnp.broadcast_to(level, (DEV, 128))
    for group in range(2):
        parts = []
        for kk in range(4):
            k = group * 4 + kk
            a, h = divmod(k, half)
            slot = slot_ref[k * CAP : (k + 1) * CAP, :]
            rows = [sums[8 * v + a : 8 * v + a + 1, h * PTS : (h + 1) * PTS] for v in range(NVEC)]
            highs = [row.astype(BF16) for row in rows]
            lows = [(row - high.astype(F32)).astype(BF16) for row, high in zip(rows, highs)]
            spread = jnp.concatenate([slot * row for row in highs + lows], axis=0)
            hot = hot_ref[k * DEV : (k + 1) * DEV, :]
            part = lax.dot_general(hot, spread, NT, preferred_element_type=F32)
            parts.append(part + pltpu.roll(part, NVEC * CAP, 1))
        for v in range(NVEC):
            values = jnp.concatenate([p[:, v * CAP : (v + 1) * CAP] for p in parts], axis=1)
            put(jnp.round(values * inverse), group * 2 + v, 4)
    out_ref[...] = stage[...].astype(jnp.int32).astype(jnp.int16)


def bricks_kernel(
    got_ref, packed_ref, kappa_ref, out_ref, halo_ref, sums, wheres, at_cells, hots
):
    for r in range(ROWS):
        for g in range(2):
            total = None
            for c in range(4):
                at = ((r * 2 + g) * 4 + c) * SLAB
                one = got_ref[at : at + SLAB, :].astype(jnp.int32).astype(F32)
                one = jnp.where(iota((SLAB, 128), 0) < 12, one * step_at(one[15:16]), one)
                total = one if total is None else total + one
            wheres[g, r * SLAB : (r + 1) * SLAB, :] = total
    sums[...] = wheres[0] + wheres[1]
    for g in range(2):
        place = wheres[g] - 1.0
        cell = jnp.floor(place * (1.0 / NZ))
        at_cells[g] = cell
        wheres[g] = place - cell * NZ
    sub = iota((8, 128), 0)
    z_row = iota((NZ, 128), 0).astype(F32)
    for j in range(3):
        for r in range(ROWS):
            for g in range(2):
                lanes = slice((r * 2 + g) * 128, (r * 2 + g + 1) * 128)
                at = r * SLAB + j * 4 + g * 2
                pair = jnp.where(sub < 4, sums[at : at + 1, :], sums[at + 1 : at + 2, :])
                high = pair.astype(BF16).astype(F32)
                low = pair - high
                p = r * SLAB + 12 + j
                cell = at_cells[g, p : p + 1, :]
                z_at = wheres[g, p : p + 1, :]
                wanted = [cell == (x * CY + sub % CY).astype(F32) for x in range(CX)]
                rows = jnp.concatenate(
                    [jnp.where(w, part, 0.0) for part in (high, low) for w in wanted], axis=0
                )
                hots[0, 0:64, lanes] = rows.astype(BF16)
                hots[1, :, lanes] = jnp.where(z_at == z_row, 1.0, 0.0).astype(BF16)
        both = lax.dot_general(hots[0, 0:64, :], hots[1], NT, preferred_element_type=F32)
        out_ref[j * 32 : (j + 1) * 32, :] = both[0:32] + both[32:64]
    my_row = lax.axis_index("row")
    half = CX * CY // NVEC
    for j, r in ((0, jnp.maximum(my_row - 1, 0)), (2, jnp.minimum(my_row + 1, ROWS - 1))):
        block = packed_ref[r, :, PTS:].astype(F32)
        for q in range(half):
            for v in range(NVEC):
                at = FIELD + j * CX * CY + v * half + q
                out_ref[at : at + 1, :] = block[v : v + 1, q * NZ : (q + 1) * NZ]
    for x in range(CX):
        at = FIELD + CX * CY + x * CY
        out_ref[at : at + CY, :] = kappa_ref[x]
    level, inverse = level_of(out_ref[0:FIELD, :])

    def store(at, values):
        halo_ref[at : at + values.shape[0], :] = (
            jnp.round(values).astype(jnp.int32).astype(jnp.int16)
        )

    store(0, out_ref[8 : FIELD - 8, :] * inverse)
    store(HALO, out_ref[FIELD + 2 * CY : FIELD + 10 * CY, :] * KAPPA_STEPS)
    store(HALO + 8 * CY, jnp.broadcast_to(level, (16, 128)))


def prior_kernel(own_ref, before_ref, after_ref, out_ref):
    my_row, my_col = lax.axis_index("row"), lax.axis_index("col")
    wide = 3 * CX
    inside_x = [
        jnp.where(my_row > 0, 1.0, 0.0),
        jnp.float32(1.0),
        jnp.where(my_row < ROWS - 1, 1.0, 0.0),
    ]
    inside_y = [
        jnp.where(my_col > 0, 1.0, 0.0),
        jnp.float32(1.0),
        jnp.where(my_col < COLS - 1, 1.0, 0.0),
    ]
    y_at = iota((8, NZ), 0) % CY
    z_at = iota((8, NZ), 1)
    none = jnp.zeros((8, NZ), F32)
    us, ks = [], []
    for ref in (before_ref, own_ref, after_ref):
        if ref is own_ref:
            field = [ref[8 * x : 8 * x + 8, :] for x in range(wide)]
            rows = [ref[FIELD + CY * x : FIELD + CY * (x + 1), :] for x in range(wide)]
            kappas = [6.0 + jnp.concatenate([row, row], axis=0) for row in rows]
        else:
            got = ref[...].astype(jnp.int32).astype(F32)
            values = got[0:HALO] * step_at(got[HALO + 8 * CY : HALO + 8 * CY + 1])
            field = [values[8 * x : 8 * x + 8] for x in range(wide - 2)]
            field = [none] + field + [none]
            values = got[HALO : HALO + 8 * CY] * (1.0 / KAPPA_STEPS) + 6.0
            rows = [values[CY * x : CY * (x + 1)] for x in range(8)]
            kappas = [none] * 2 + [jnp.concatenate([row, row], axis=0) for row in rows] + [none] * 2
        us.append(field)
        ks.append(kappas)
    for step in range(1, 5):
        new = [[None] * wide for _ in range(3)]
        for b in range(3):
            if step == 4 and b != 1:
                continue
            edge = step if b == 1 else step + 1
            for x in range(edge, wide - edge):
                u = us[b][x]
                lower = pltpu.roll(us[b - 1][x], 5, 0) if b > 0 and us[b - 1][x] is not None else 0.0
                upper = pltpu.roll(us[b + 1][x], 3, 0) if b < 2 and us[b + 1][x] is not None else 0.0
                beside = us[b][x - 1] + us[b][x + 1]
                beside = beside + jnp.where(y_at == 0, lower, pltpu.roll(u, 1, 0))
                beside = beside + jnp.where(y_at == CY - 1, upper, pltpu.roll(u, 7, 0))
                beside = beside + jnp.where(z_at == 0, 0.0, pltpu.roll(u, 1, 1))
                beside = beside + jnp.where(z_at == NZ - 1, 0.0, pltpu.roll(u, NZ - 1, 1))
                result = (ks[b][x] * u - beside) * 0.125
                if step < 4:
                    if b != 1 and x // CX != 1:
                        result = result * (inside_y[b] * inside_x[x // CX])
                    elif b != 1:
                        result = result * inside_y[b]
                    elif x // CX != 1:
                        result = result * inside_x[x // CX]
                new[b][x] = result
        us = new
    for x in range(CX):
        for v in range(NVEC):
            out_ref[v, x] = us[1][CX + x][v * CY : (v + 1) * CY]


def to_both_sides(array, axis):
    size = lax.axis_size(axis)
    before = lax.ppermute(array, axis, [(i, i + 1) for i in range(size - 1)])
    after = lax.ppermute(array, axis, [(i + 1, i) for i in range(size - 1)])
    return before, after


def cost(flops, size):
    return pl.CostEstimate(flops=flops, bytes_accessed=size, transcendentals=0)


def in_hbm(*arrays):
    return [pltpu.with_memory_space_constraint(a, pltpu.HBM) for a in arrays]


def in_vmem(*arrays):
    return [pltpu.with_memory_space_constraint(a, pltpu.VMEM) for a in arrays]


def params(mib):
    return pltpu.CompilerParams(vmem_limit_bytes=mib * MIB)


def per_device(
    vectors, lr_left, lr_right, tile_rank, leaf_values, leaf_places, cluster_perm, kappa
):
    vmem = pl.BlockSpec(memory_space=pltpu.VMEM)
    hbm = pl.BlockSpec(memory_space=pltpu.HBM)
    points = COLS * PTS
    terms = TILE_ROWS * TILE_COLS * KMAX
    packed_shape = (ROWS, NVEC, PTS + PTS // NVEC)
    packed, kappa_own, perm, ranks = pl.pallas_call(
        pack_kernel,
        out_shape=(
            pltpu.VMEM(packed_shape, BF16),
            pltpu.VMEM((CX, CY, NZ), F32),
            pltpu.VMEM((1, points), jnp.int32),
            pltpu.VMEM((1, TILE_ROWS * TILE_COLS), jnp.int32),
        ),
        in_specs=[hbm] * 4,
        out_specs=(vmem,) * 4,
        scratch_shapes=[pltpu.VMEM((NVEC, PTS), BF16), pltpu.SemaphoreType.DMA((4,))],
        compiler_params=params(8),
        name="pack",
    )(*in_hbm(vectors[:, 0], kappa, cluster_perm, tile_rank[0]))
    packed = lax.all_to_all(packed, "row", 0, 0, tiled=True)
    hot, slot, place, right, left, leaves = pl.pallas_call(
        slots_kernel,
        out_shape=(
            pltpu.VMEM((COLS * DEV, PTS), BF16),
            pltpu.VMEM((COLS * CAP, PTS), BF16),
            pltpu.VMEM((DEV, 128), F32),
            pltpu.VMEM((terms, TS), BF16),
            pltpu.VMEM((terms, TS), BF16),
            pltpu.VMEM((NLEAF, LEAF, LEAF), BF16),
        ),
        in_specs=[vmem, hbm, hbm, hbm],
        out_specs=(vmem,) * 6,
        scratch_shapes=[pltpu.SemaphoreType.DMA((3,))],
        compiler_params=params(16),
        cost_estimate=cost(1 << 31, 1 << 20),
        name="slots",
    )(
        perm,
        *in_hbm(
            lr_right.reshape(terms, TS), lr_left.reshape(terms, TS), leaf_values[0, 0]
        ),
    )
    send = pl.pallas_call(
        send_kernel,
        out_shape=jax.ShapeDtypeStruct((DEV * SLAB, 128), jnp.int16),
        in_specs=[hbm] + [vmem] * 8,
        out_specs=vmem,
        scratch_shapes=[
            pltpu.VMEM((16, TS), F32),
            pltpu.VMEM((16, TS), F32),
            pltpu.VMEM((DEV * SLAB, 128), F32),
            pltpu.SMEM((2, NLEAF), jnp.int32),
            pltpu.SemaphoreType.DMA,
        ],
        compiler_params=params(16),
        cost_estimate=cost(1 << 31, 8 << 20),
        name="partial_sums",
    )(
        *in_hbm(leaf_places[0, 0].T),
        *in_vmem(packed, ranks, hot, slot, place, right, left, leaves),
    )
    got = lax.all_to_all(send.reshape(DEV, SLAB, 128), ("row", "col"), 0, 0, tiled=True)
    own, halo = pl.pallas_call(
        bricks_kernel,
        out_shape=(
            pltpu.VMEM((FIELD + 3 * CX * CY, NZ), F32),
            pltpu.VMEM((HALO + 8 * CY + 16, NZ), jnp.int16),
        ),
        in_specs=[vmem] * 3,
        out_specs=(vmem,) * 2,
        scratch_shapes=[
            pltpu.VMEM((ROWS * SLAB, 128), F32),
            pltpu.VMEM((2, ROWS * SLAB, 128), F32),
            pltpu.VMEM((2, ROWS * SLAB, 128), F32),
            pltpu.VMEM((2, NZ, 4096), BF16),
        ],
        compiler_params=params(16),
        cost_estimate=cost(1 << 30, 1 << 20),
        name="bricks",
    )(got.reshape(DEV * SLAB, 128), packed, kappa_own)
    before, after = to_both_sides(halo, "col")
    return pl.pallas_call(
        prior_kernel,
        out_shape=jax.ShapeDtypeStruct((NVEC, CX, CY, NZ), F32),
        in_specs=[vmem] * 3,
        out_specs=vmem,
        compiler_params=params(8),
        cost_estimate=cost(1 << 24, 1 << 20),
        name="prior",
    )(own, before, after)


def solution(mesh):
    in_specs = (
        P(None, "col", "row"),
        P("row", "col", None, None, None),
        P("row", "col", None, None, None),
        P("row", "col", None),
        P("row", "col", None, None, None),
        P("row", "col", None, None),
        P("row", None),
        P("row", "col", None),
    )
    out_specs = P(None, "row", "col", None)
    return jax.shard_map(
        per_device, mesh=mesh, in_specs=in_specs, out_specs=out_specs, check_vma=False
    )
```

```python
import jax
import jax.numpy as jnp
from jax import lax
from jax.experimental import pallas as pl
from jax.experimental.pallas import tpu as pltpu
from jax.sharding import PartitionSpec as P

NVEC = 2
CX = 4
CY = 4
NZ = 128
TILE_ROWS = 4
TILE_COLS = 8
KMAX = 8
LEAF = 512
NLEAF = 8
PTS = 2048
ROWS = 16
COLS = 8
TS = 4096
CAP = 32
DEV = ROWS * COLS
SLAB = 16
F32 = jnp.float32
BF16 = jnp.bfloat16
NT = (((1,), (1,)), ((), ()))
MIB = 1 << 20
LEVELS = 64.0
STEPS = 32000.0
KAPPA_STEPS = 8000.0
FIELD = 3 * CX * NVEC * CY
HALO = FIELD - 2 * NVEC * CY


def iota(shape, dim):
    return lax.broadcasted_iota(jnp.int32, shape, dim)


def pack_kernel(
    vectors_hbm, kappa_hbm, perm_hbm, rank_hbm, out_ref, kappa_ref, perm_ref, rank_ref, vectors, sems
):
    pairs = (
        (vectors_hbm, vectors),
        (kappa_hbm, kappa_ref),
        (perm_hbm, perm_ref),
        (rank_hbm, rank_ref),
    )
    copies = [pltpu.make_async_copy(a, b, sems.at[i]) for i, (a, b) in enumerate(pairs)]
    for copy in copies:
        copy.start()
    copies[0].wait()
    for s in range(ROWS):
        out_ref[s, :, 0:PTS] = vectors[...]
    copies[1].wait()
    rows = [kappa_ref[q // CY, q % CY : q % CY + 1, :] for q in range(CX * CY)]
    half = CX * CY // NVEC
    for q in range(half):
        pair = jnp.concatenate([rows[q], rows[half + q]], axis=0).astype(BF16)
        for s in range(ROWS):
            out_ref[s, :, PTS + q * NZ : PTS + (q + 1) * NZ] = pair
    copies[2].wait()
    copies[3].wait()


def slots_kernel(perm_ref, right_hbm, rank_ref, place_ref, right, sem):
    copy = pltpu.make_async_copy(right_hbm, right, sem)
    copy.start()
    chunk = 256
    upto = jnp.where(iota((chunk, chunk), 0) <= iota((chunk, chunk), 1), 1.0, 0.0).astype(BF16)
    brick = iota((DEV, chunk), 0)
    carry = jnp.zeros((COLS * DEV, 1), F32)
    for j in range(PTS // chunk):
        lanes = [slice(k * PTS + j * chunk, k * PTS + (j + 1) * chunk) for k in range(COLS)]
        masks = [(perm_ref[0:1, at] >> 11) == brick for at in lanes]
        hot = jnp.concatenate([jnp.where(m, 1.0, 0.0).astype(BF16) for m in masks], axis=0)
        total = jnp.dot(hot, upto, preferred_element_type=F32) + carry
        for k in range(COLS):
            at = jnp.where(masks[k], total[k * DEV : (k + 1) * DEV], 0.0)
            rank_ref[0:1, lanes[k]] = jnp.sum(at, axis=0, keepdims=True) - 1.0
        carry = total[:, chunk - 1 : chunk]
    col = lax.axis_index("col")
    start = pl.multiple_of(col * PTS, PTS)
    own = perm_ref[0:1, pl.ds(start, PTS)]
    slot = rank_ref[0:1, pl.ds(start, PTS)] + ((col % 4) * CAP).astype(F32)
    here = jnp.where(slot == iota((128, PTS), 0).astype(F32), 1.0, 0.0).astype(BF16)
    hot = jnp.where((own >> 11) == iota((DEV, PTS), 0), 1.0, 0.0).astype(BF16)
    inside = own & (PTS - 1)
    place = jnp.zeros((DEV, 128), F32)
    for part in (inside & ~(NZ - 1), (inside & (NZ - 1)) + 1):
        spread = here * part.astype(F32).astype(BF16)
        place = place + lax.dot_general(hot, spread, NT, preferred_element_type=F32)
    place_ref[...] = place
    copy.wait()


def level_of(values):
    largest = jnp.max(jnp.abs(values), axis=0, keepdims=True)
    largest = jnp.broadcast_to(jnp.max(largest, axis=1, keepdims=True), (8, 128))
    level = jnp.ceil(jnp.maximum(jnp.log2(largest), -100.0) * LEVELS)
    return level[0:1], (STEPS * jnp.exp2(level * (-1.0 / LEVELS)))[0:1]


def step_at(level):
    return jnp.exp2(level * (1.0 / LEVELS)) * (1.0 / STEPS)


def send_kernel(
    leaf_at_hbm,
    left_hbm,
    leaf_hbm,
    x_ref,
    tile_rank_ref,
    perm_ref,
    rank_ref,
    place_ref,
    right,
    out_ref,
    left,
    leaves,
    x_rows,
    sums,
    stage,
    hots,
    slots,
    leaf_at,
    sems,
):
    pairs = ((left_hbm, left), (leaf_hbm, leaves), (leaf_at_hbm, leaf_at))
    copies = [pltpu.make_async_copy(a, b, sems.at[i]) for i, (a, b) in enumerate(pairs)]
    for copy in copies:
        copy.start()
    half = TS // PTS
    for s in range(ROWS):
        b, h = divmod(s, half)
        block = x_ref[s, :, 0:PTS].astype(F32)
        x_rows[b : b + 1, h * PTS : (h + 1) * PTS] = block[0:1]
        x_rows[8 + b : 9 + b, h * PTS : (h + 1) * PTS] = block[1:2]
    terms = TILE_ROWS * TILE_COLS * KMAX
    lane = iota((16, terms), 1)
    sub = iota((16, terms), 0)
    widen = jnp.where(
        iota((TILE_ROWS * TILE_COLS, terms), 1) // KMAX
        == iota((TILE_ROWS * TILE_COLS, terms), 0),
        1.0,
        0.0,
    ).astype(BF16)
    ranks = jnp.broadcast_to(tile_rank_ref[...].astype(F32), (16, TILE_ROWS * TILE_COLS))
    rank_lane = jnp.dot(ranks.astype(BF16), widen, preferred_element_type=F32)
    keep = (sub % 8 == (lane // KMAX) % TILE_COLS) & ((lane % KMAX).astype(F32) < rank_lane)
    x_all = x_rows[...].astype(BF16)
    projected = lax.dot_general(x_all, right[...], NT, preferred_element_type=F32)
    projected = jnp.where(keep, projected, 0.0)
    first = jnp.sum(projected[0:8], axis=0, keepdims=True)
    second = jnp.sum(projected[8:16], axis=0, keepdims=True)
    by_row = jnp.where(sub < 8, first, second)
    by_row = jnp.where(sub % 8 == lane // (TILE_COLS * KMAX), by_row, 0.0).astype(BF16)
    for k in range(COLS):
        at = slice(k * PTS, (k + 1) * PTS)
        hot = (perm_ref[0:1, at] >> 11) == iota((DEV, PTS), 0)
        hots[k * DEV : (k + 1) * DEV, :] = jnp.where(hot, 1.0, 0.0).astype(BF16)
        slot = rank_ref[0:1, at] == iota((CAP, PTS), 0).astype(F32)
        slots[k * CAP : (k + 1) * CAP, :] = jnp.where(slot, 1.0, 0.0).astype(BF16)
    copies[0].wait()
    sums[...] = jnp.dot(by_row, left[...], preferred_element_type=F32)
    copies[1].wait()
    copies[2].wait()
    per_tile = TS // LEAF
    for l in range(NLEAF):
        i, j = leaf_at[0, l], leaf_at[1, l]
        from_lane = pl.multiple_of((j % per_tile) * LEAF, LEAF)
        to_lane = pl.multiple_of((i % per_tile) * LEAF, LEAF)
        picked = jnp.concatenate(
            [x_rows[pl.ds(8 * v + j // per_tile, 1), pl.ds(from_lane, LEAF)] for v in range(NVEC)],
            axis=0,
        ).astype(BF16)
        near = lax.dot_general(picked, leaves[l], NT, preferred_element_type=F32)
        for v in range(NVEC):
            at = (pl.ds(8 * v + i // per_tile, 1), pl.ds(to_lane, LEAF))
            sums[at] = sums[at] + near[v : v + 1]
    level, inverse = level_of(sums[...])

    def put(values, first_row, step):
        none = jnp.zeros((COLS, 128), F32)
        stage[pl.ds(first_row, COLS, stride=SLAB), :] = none
        stage[pl.ds(first_row + COLS * SLAB, DEV - COLS, stride=SLAB), :] = values[: DEV - COLS]
        stage[pl.ds(first_row + step, DEV, stride=SLAB), :] = values
        at = first_row + 2 * step
        stage[pl.ds(at, DEV - COLS, stride=SLAB), :] = values[COLS:]
        stage[pl.ds(at + (DEV - COLS) * SLAB, COLS, stride=SLAB), :] = none

    put(place_ref[...], 12, 1)
    stage[pl.ds(15, DEV, stride=SLAB), :] = jnp.broadcast_to(level, (DEV, 128))
    for group in range(2):
        parts = []
        for kk in range(4):
            k = group * 4 + kk
            a, h = divmod(k, half)
            slot = slots[k * CAP : (k + 1) * CAP, :]
            rows = [sums[8 * v + a : 8 * v + a + 1, h * PTS : (h + 1) * PTS] for v in range(NVEC)]
            highs = [row.astype(BF16) for row in rows]
            lows = [(row - high.astype(F32)).astype(BF16) for row, high in zip(rows, highs)]
            spread = jnp.concatenate([slot * row for row in highs + lows], axis=0)
            hot = hots[k * DEV : (k + 1) * DEV, :]
            part = lax.dot_general(hot, spread, NT, preferred_element_type=F32)
            parts.append(part + pltpu.roll(part, NVEC * CAP, 1))
        for v in range(NVEC):
            values = jnp.concatenate([p[:, v * CAP : (v + 1) * CAP] for p in parts], axis=1)
            put(jnp.round(values * inverse), group * 2 + v, 4)
    out_ref[...] = stage[...].astype(jnp.int32).astype(jnp.int16)


def bricks_kernel(
    got_ref, packed_ref, kappa_ref, out_ref, halo_ref, sums, wheres, at_cells, hots
):
    for r in range(ROWS):
        for g in range(2):
            total = None
            for c in range(4):
                at = ((r * 2 + g) * 4 + c) * SLAB
                one = got_ref[at : at + SLAB, :].astype(jnp.int32).astype(F32)
                one = jnp.where(iota((SLAB, 128), 0) < 12, one * step_at(one[15:16]), one)
                total = one if total is None else total + one
            wheres[g, r * SLAB : (r + 1) * SLAB, :] = total
    sums[...] = wheres[0] + wheres[1]
    for g in range(2):
        place = wheres[g] - 1.0
        cell = jnp.floor(place * (1.0 / NZ))
        at_cells[g] = cell
        wheres[g] = place - cell * NZ
    sub = iota((8, 128), 0)
    z_row = iota((NZ, 128), 0).astype(F32)
    for j in range(3):
        for r in range(ROWS):
            for g in range(2):
                lanes = slice((r * 2 + g) * 128, (r * 2 + g + 1) * 128)
                at = r * SLAB + j * 4 + g * 2
                pair = jnp.where(sub < 4, sums[at : at + 1, :], sums[at + 1 : at + 2, :])
                high = pair.astype(BF16).astype(F32)
                low = pair - high
                p = r * SLAB + 12 + j
                cell = at_cells[g, p : p + 1, :]
                z_at = wheres[g, p : p + 1, :]
                wanted = [cell == (x * CY + sub % CY).astype(F32) for x in range(CX)]
                rows = jnp.concatenate(
                    [jnp.where(w, part, 0.0) for part in (high, low) for w in wanted], axis=0
                )
                hots[0, 0:64, lanes] = rows.astype(BF16)
                hots[1, :, lanes] = jnp.where(z_at == z_row, 1.0, 0.0).astype(BF16)
        both = lax.dot_general(hots[0, 0:64, :], hots[1], NT, preferred_element_type=F32)
        out_ref[j * 32 : (j + 1) * 32, :] = both[0:32] + both[32:64]
    my_row = lax.axis_index("row")
    half = CX * CY // NVEC
    for j, r in ((0, jnp.maximum(my_row - 1, 0)), (2, jnp.minimum(my_row + 1, ROWS - 1))):
        block = packed_ref[r, :, PTS:].astype(F32)
        for q in range(half):
            for v in range(NVEC):
                at = FIELD + j * CX * CY + v * half + q
                out_ref[at : at + 1, :] = block[v : v + 1, q * NZ : (q + 1) * NZ]
    for x in range(CX):
        at = FIELD + CX * CY + x * CY
        out_ref[at : at + CY, :] = kappa_ref[x]
    level, inverse = level_of(out_ref[0:FIELD, :])

    def store(at, values):
        halo_ref[at : at + values.shape[0], :] = (
            jnp.round(values).astype(jnp.int32).astype(jnp.int16)
        )

    store(0, out_ref[8 : FIELD - 8, :] * inverse)
    store(HALO, out_ref[FIELD + 2 * CY : FIELD + 10 * CY, :] * KAPPA_STEPS)
    store(HALO + 8 * CY, jnp.broadcast_to(level, (16, 128)))


def prior_kernel(own_ref, before_ref, after_ref, out_ref):
    my_row, my_col = lax.axis_index("row"), lax.axis_index("col")
    wide = 3 * CX
    inside_x = [
        jnp.where(my_row > 0, 1.0, 0.0),
        jnp.float32(1.0),
        jnp.where(my_row < ROWS - 1, 1.0, 0.0),
    ]
    inside_y = [
        jnp.where(my_col > 0, 1.0, 0.0),
        jnp.float32(1.0),
        jnp.where(my_col < COLS - 1, 1.0, 0.0),
    ]
    y_at = iota((8, NZ), 0) % CY
    z_at = iota((8, NZ), 1)
    none = jnp.zeros((8, NZ), F32)
    us, ks = [], []
    for ref in (before_ref, own_ref, after_ref):
        if ref is own_ref:
            field = [ref[8 * x : 8 * x + 8, :] for x in range(wide)]
            rows = [ref[FIELD + CY * x : FIELD + CY * (x + 1), :] for x in range(wide)]
            kappas = [6.0 + jnp.concatenate([row, row], axis=0) for row in rows]
        else:
            got = ref[...].astype(jnp.int32).astype(F32)
            values = got[0:HALO] * step_at(got[HALO + 8 * CY : HALO + 8 * CY + 1])
            field = [values[8 * x : 8 * x + 8] for x in range(wide - 2)]
            field = [none] + field + [none]
            values = got[HALO : HALO + 8 * CY] * (1.0 / KAPPA_STEPS) + 6.0
            rows = [values[CY * x : CY * (x + 1)] for x in range(8)]
            kappas = [none] * 2 + [jnp.concatenate([row, row], axis=0) for row in rows] + [none] * 2
        us.append(field)
        ks.append(kappas)
    for step in range(1, 5):
        new = [[None] * wide for _ in range(3)]
        for b in range(3):
            if step == 4 and b != 1:
                continue
            edge = step if b == 1 else step + 1
            for x in range(edge, wide - edge):
                u = us[b][x]
                lower = pltpu.roll(us[b - 1][x], 5, 0) if b > 0 and us[b - 1][x] is not None else 0.0
                upper = pltpu.roll(us[b + 1][x], 3, 0) if b < 2 and us[b + 1][x] is not None else 0.0
                beside = us[b][x - 1] + us[b][x + 1]
                beside = beside + jnp.where(y_at == 0, lower, pltpu.roll(u, 1, 0))
                beside = beside + jnp.where(y_at == CY - 1, upper, pltpu.roll(u, 7, 0))
                beside = beside + jnp.where(z_at == 0, 0.0, pltpu.roll(u, 1, 1))
                beside = beside + jnp.where(z_at == NZ - 1, 0.0, pltpu.roll(u, NZ - 1, 1))
                result = (ks[b][x] * u - beside) * 0.125
                if step < 4:
                    if b != 1 and x // CX != 1:
                        result = result * (inside_y[b] * inside_x[x // CX])
                    elif b != 1:
                        result = result * inside_y[b]
                    elif x // CX != 1:
                        result = result * inside_x[x // CX]
                new[b][x] = result
        us = new
    for x in range(CX):
        for v in range(NVEC):
            out_ref[v, x] = us[1][CX + x][v * CY : (v + 1) * CY]


def to_both_sides(array, axis):
    size = lax.axis_size(axis)
    before = lax.ppermute(array, axis, [(i, i + 1) for i in range(size - 1)])
    after = lax.ppermute(array, axis, [(i + 1, i) for i in range(size - 1)])
    return before, after


def cost(flops, size):
    return pl.CostEstimate(flops=flops, bytes_accessed=size, transcendentals=0)


def in_hbm(*arrays):
    return [pltpu.with_memory_space_constraint(a, pltpu.HBM) for a in arrays]


def in_vmem(*arrays):
    return [pltpu.with_memory_space_constraint(a, pltpu.VMEM) for a in arrays]


def params(mib):
    return pltpu.CompilerParams(vmem_limit_bytes=mib * MIB)


def per_device(
    vectors, lr_left, lr_right, tile_rank, leaf_values, leaf_places, cluster_perm, kappa
):
    vmem = pl.BlockSpec(memory_space=pltpu.VMEM)
    hbm = pl.BlockSpec(memory_space=pltpu.HBM)
    points = COLS * PTS
    terms = TILE_ROWS * TILE_COLS * KMAX
    packed_shape = (ROWS, NVEC, PTS + PTS // NVEC)
    packed, kappa_own, perm, ranks = pl.pallas_call(
        pack_kernel,
        out_shape=(
            pltpu.VMEM(packed_shape, BF16),
            pltpu.VMEM((CX, CY, NZ), F32),
            pltpu.VMEM((1, points), jnp.int32),
            pltpu.VMEM((1, TILE_ROWS * TILE_COLS), jnp.int32),
        ),
        in_specs=[hbm] * 4,
        out_specs=(vmem,) * 4,
        scratch_shapes=[pltpu.VMEM((NVEC, PTS), BF16), pltpu.SemaphoreType.DMA((4,))],
        compiler_params=params(8),
        name="pack",
    )(*in_hbm(vectors[:, 0], kappa, cluster_perm, tile_rank[0]))
    packed = lax.all_to_all(packed, "row", 0, 0, tiled=True)
    rank, place, right = pl.pallas_call(
        slots_kernel,
        out_shape=(
            pltpu.VMEM((1, points), F32),
            pltpu.VMEM((DEV, 128), F32),
            pltpu.VMEM((terms, TS), BF16),
        ),
        in_specs=[vmem, hbm],
        out_specs=(vmem,) * 3,
        scratch_shapes=[pltpu.SemaphoreType.DMA],
        compiler_params=params(16),
        cost_estimate=cost(1 << 31, 1 << 20),
        name="slots",
    )(perm, *in_hbm(lr_right.reshape(terms, TS)))
    send = pl.pallas_call(
        send_kernel,
        out_shape=jax.ShapeDtypeStruct((DEV * SLAB, 128), jnp.int16),
        in_specs=[hbm] * 3 + [vmem] * 6,
        out_specs=vmem,
        scratch_shapes=[
            pltpu.VMEM((terms, TS), BF16),
            pltpu.VMEM((NLEAF, LEAF, LEAF), BF16),
            pltpu.VMEM((16, TS), F32),
            pltpu.VMEM((16, TS), F32),
            pltpu.VMEM((DEV * SLAB, 128), F32),
            pltpu.VMEM((COLS * DEV, PTS), BF16),
            pltpu.VMEM((COLS * CAP, PTS), BF16),
            pltpu.SMEM((2, NLEAF), jnp.int32),
            pltpu.SemaphoreType.DMA((3,)),
        ],
        compiler_params=params(32),
        cost_estimate=cost(1 << 31, 8 << 20),
        name="partial_sums",
    )(
        *in_hbm(leaf_places[0, 0].T, lr_left.reshape(terms, TS), leaf_values[0, 0]),
        *in_vmem(packed, ranks, perm, rank, place, right),
    )
    got = lax.all_to_all(send.reshape(DEV, SLAB, 128), ("row", "col"), 0, 0, tiled=True)
    own, halo = pl.pallas_call(
        bricks_kernel,
        out_shape=(
            pltpu.VMEM((FIELD + 3 * CX * CY, NZ), F32),
            pltpu.VMEM((HALO + 8 * CY + 16, NZ), jnp.int16),
        ),
        in_specs=[vmem] * 3,
        out_specs=(vmem,) * 2,
        scratch_shapes=[
            pltpu.VMEM((ROWS * SLAB, 128), F32),
            pltpu.VMEM((2, ROWS * SLAB, 128), F32),
            pltpu.VMEM((2, ROWS * SLAB, 128), F32),
            pltpu.VMEM((2, NZ, 4096), BF16),
        ],
        compiler_params=params(16),
        cost_estimate=cost(1 << 30, 1 << 20),
        name="bricks",
    )(got.reshape(DEV * SLAB, 128), packed, kappa_own)
    before, after = to_both_sides(halo, "col")
    return pl.pallas_call(
        prior_kernel,
        out_shape=jax.ShapeDtypeStruct((NVEC, CX, CY, NZ), F32),
        in_specs=[vmem] * 3,
        out_specs=vmem,
        compiler_params=params(8),
        cost_estimate=cost(1 << 24, 1 << 20),
        name="prior",
    )(own, before, after)


def solution(mesh):
    in_specs = (
        P(None, "col", "row"),
        P("row", "col", None, None, None),
        P("row", "col", None, None, None),
        P("row", "col", None),
        P("row", "col", None, None, None),
        P("row", "col", None, None),
        P("row", None),
        P("row", "col", None),
    )
    out_specs = P(None, "row", "col", None)
    return jax.shard_map(
        per_device, mesh=mesh, in_specs=in_specs, out_specs=out_specs, check_vma=False
    )
```

```python
import jax
import jax.numpy as jnp
from jax import lax
from jax.experimental import pallas as pl
from jax.experimental.pallas import tpu as pltpu
from jax.sharding import PartitionSpec as P

NVEC = 2
CX = 4
CY = 4
NZ = 128
TILE_ROWS = 4
TILE_COLS = 8
KMAX = 8
LEAF = 512
NLEAF = 8
PTS = 2048
ROWS = 16
COLS = 8
TS = 4096
CAP = 32
DEV = ROWS * COLS
PIECES = 2
SLAB = 16
F32 = jnp.float32
BF16 = jnp.bfloat16
NT = (((1,), (1,)), ((), ()))
MIB = 1 << 20
LEVELS = 64.0
STEPS = 32000.0
KAPPA_STEPS = 8000.0
FIELD = 3 * CX * NVEC * CY
HALO = FIELD - 2 * NVEC * CY
MESSAGE = HALO + 8 * CY + 16


def iota(shape, dim):
    return lax.broadcasted_iota(jnp.int32, shape, dim)


def pack_kernel(
    vectors_hbm, kappa_hbm, perm_hbm, rank_hbm, out_ref, kappa_ref, perm_ref, rank_ref, vectors, sems
):
    pairs = (
        (vectors_hbm, vectors),
        (kappa_hbm, kappa_ref),
        (perm_hbm, perm_ref),
        (rank_hbm, rank_ref),
    )
    copies = [pltpu.make_async_copy(a, b, sems.at[i]) for i, (a, b) in enumerate(pairs)]
    for copy in copies:
        copy.start()
    copies[0].wait()
    for s in range(ROWS):
        out_ref[s, :, 0:PTS] = vectors[...]
    copies[1].wait()
    rows = [kappa_ref[q // CY, q % CY : q % CY + 1, :] for q in range(CX * CY)]
    half = CX * CY // NVEC
    for q in range(half):
        pair = jnp.concatenate([rows[q], rows[half + q]], axis=0).astype(BF16)
        for s in range(ROWS):
            out_ref[s, :, PTS + q * NZ : PTS + (q + 1) * NZ] = pair
    copies[2].wait()
    copies[3].wait()


def slots_kernel(perm_ref, right_hbm, rank_ref, place_ref, right, sem):
    copy = pltpu.make_async_copy(right_hbm, right, sem)
    copy.start()
    chunk = 256
    upto = jnp.where(iota((chunk, chunk), 0) <= iota((chunk, chunk), 1), 1.0, 0.0).astype(BF16)
    brick = iota((DEV, chunk), 0)
    carry = jnp.zeros((COLS * DEV, 1), F32)
    for j in range(PTS // chunk):
        lanes = [slice(k * PTS + j * chunk, k * PTS + (j + 1) * chunk) for k in range(COLS)]
        masks = [(perm_ref[0:1, at] >> 11) == brick for at in lanes]
        hot = jnp.concatenate([jnp.where(m, 1.0, 0.0).astype(BF16) for m in masks], axis=0)
        total = jnp.dot(hot, upto, preferred_element_type=F32) + carry
        for k in range(COLS):
            at = jnp.where(masks[k], total[k * DEV : (k + 1) * DEV], 0.0)
            rank_ref[0:1, lanes[k]] = jnp.sum(at, axis=0, keepdims=True) - 1.0
        carry = total[:, chunk - 1 : chunk]
    col = lax.axis_index("col")
    start = pl.multiple_of(col * PTS, PTS)
    own = perm_ref[0:1, pl.ds(start, PTS)]
    slot = rank_ref[0:1, pl.ds(start, PTS)] + ((col % 4) * CAP).astype(F32)
    here = jnp.where(slot == iota((128, PTS), 0).astype(F32), 1.0, 0.0).astype(BF16)
    hot = jnp.where((own >> 11) == iota((DEV, PTS), 0), 1.0, 0.0).astype(BF16)
    inside = own & (PTS - 1)
    place = jnp.zeros((DEV, 128), F32)
    for part in (inside & ~(NZ - 1), (inside & (NZ - 1)) + 1):
        spread = here * part.astype(F32).astype(BF16)
        place = place + lax.dot_general(hot, spread, NT, preferred_element_type=F32)
    place_ref[...] = place
    copy.wait()


def level_of(values):
    largest = jnp.max(jnp.abs(values), axis=0, keepdims=True)
    largest = jnp.broadcast_to(jnp.max(largest, axis=1, keepdims=True), (8, 128))
    level = jnp.ceil(jnp.maximum(jnp.log2(largest), -100.0) * LEVELS)
    return level[0:1], (STEPS * jnp.exp2(level * (-1.0 / LEVELS)))[0:1]


def step_at(level):
    return jnp.exp2(level * (1.0 / LEVELS)) * (1.0 / STEPS)


def send_kernel(
    leaf_at_hbm,
    left_hbm,
    leaf_hbm,
    x_ref,
    tile_rank_ref,
    perm_ref,
    rank_ref,
    place_ref,
    right,
    out_ref,
    left,
    leaves,
    x_rows,
    sums,
    stage,
    leaf_at,
    sems,
):
    pairs = [(leaf_at_hbm, leaf_at)]
    each, wide = NLEAF // PIECES, TS // PIECES
    for i in range(PIECES):
        at = pl.ds(i * wide, wide)
        pairs.append((left_hbm.at[:, at], left.at[:, at]))
    for i in range(PIECES):
        at = pl.ds(i * each, each)
        pairs.append((leaf_hbm.at[at], leaves.at[at]))
    copies = [pltpu.make_async_copy(a, b, sems.at[i]) for i, (a, b) in enumerate(pairs)]
    for copy in copies:
        copy.start()

    def put(values, first_row, step):
        none = jnp.zeros((COLS, 128), F32)
        stage[pl.ds(first_row, COLS, stride=SLAB), :] = none
        stage[pl.ds(first_row + COLS * SLAB, DEV - COLS, stride=SLAB), :] = values[: DEV - COLS]
        stage[pl.ds(first_row + step, DEV, stride=SLAB), :] = values
        at = first_row + 2 * step
        stage[pl.ds(at, DEV - COLS, stride=SLAB), :] = values[COLS:]
        stage[pl.ds(at + (DEV - COLS) * SLAB, COLS, stride=SLAB), :] = none

    put(place_ref[...], 12, 1)
    half = TS // PTS
    for s in range(ROWS):
        b, h = divmod(s, half)
        block = x_ref[s, :, 0:PTS].astype(F32)
        x_rows[b : b + 1, h * PTS : (h + 1) * PTS] = block[0:1]
        x_rows[8 + b : 9 + b, h * PTS : (h + 1) * PTS] = block[1:2]
    terms = TILE_ROWS * TILE_COLS * KMAX
    lane = iota((16, terms), 1)
    sub = iota((16, terms), 0)
    widen = jnp.where(
        iota((TILE_ROWS * TILE_COLS, terms), 1) // KMAX
        == iota((TILE_ROWS * TILE_COLS, terms), 0),
        1.0,
        0.0,
    ).astype(BF16)
    ranks = jnp.broadcast_to(tile_rank_ref[...].astype(F32), (16, TILE_ROWS * TILE_COLS))
    rank_lane = jnp.dot(ranks.astype(BF16), widen, preferred_element_type=F32)
    keep = (sub % 8 == (lane // KMAX) % TILE_COLS) & ((lane % KMAX).astype(F32) < rank_lane)
    x_all = x_rows[...].astype(BF16)
    projected = lax.dot_general(x_all, right[...], NT, preferred_element_type=F32)
    projected = jnp.where(keep, projected, 0.0)
    first = jnp.sum(projected[0:8], axis=0, keepdims=True)
    second = jnp.sum(projected[8:16], axis=0, keepdims=True)
    by_row = jnp.where(sub < 8, first, second)
    by_row = jnp.where(sub % 8 == lane // (TILE_COLS * KMAX), by_row, 0.0).astype(BF16)
    for i in range(PIECES):
        copies[1 + i].wait()
        at = (slice(None), slice(i * wide, (i + 1) * wide))
        sums[at] = jnp.dot(by_row, left[at], preferred_element_type=F32)
    copies[0].wait()
    per_tile = TS // LEAF
    for l in range(NLEAF):
        if l % each == 0:
            copies[1 + PIECES + l // each].wait()
        i, j = leaf_at[0, l], leaf_at[1, l]
        from_lane = pl.multiple_of((j % per_tile) * LEAF, LEAF)
        to_lane = pl.multiple_of((i % per_tile) * LEAF, LEAF)
        picked = jnp.concatenate(
            [x_rows[pl.ds(8 * v + j // per_tile, 1), pl.ds(from_lane, LEAF)] for v in range(NVEC)],
            axis=0,
        ).astype(BF16)
        near = lax.dot_general(picked, leaves[l], NT, preferred_element_type=F32)
        for v in range(NVEC):
            at = (pl.ds(8 * v + i // per_tile, 1), pl.ds(to_lane, LEAF))
            sums[at] = sums[at] + near[v : v + 1]
    level, inverse = level_of(sums[...])

    stage[pl.ds(15, DEV, stride=SLAB), :] = jnp.broadcast_to(level, (DEV, 128))
    one, none = jnp.ones((), BF16), jnp.zeros((), BF16)

    def numbers(count):
        return iota((count, PTS), 0).astype(F32).astype(BF16)

    for group in range(2):
        parts = []
        for kk in range(4):
            k = group * 4 + kk
            a, h = divmod(k, half)
            at = slice(k * PTS, (k + 1) * PTS)
            slot = rank_ref[0:1, at].astype(BF16) == numbers(CAP)
            slot = jnp.where(slot, one, none)
            rows = [sums[8 * v + a : 8 * v + a + 1, h * PTS : (h + 1) * PTS] for v in range(NVEC)]
            highs = [row.astype(BF16) for row in rows]
            lows = [(row - high.astype(F32)).astype(BF16) for row, high in zip(rows, highs)]
            spread = jnp.concatenate([slot * row for row in highs + lows], axis=0)
            hot = (perm_ref[0:1, at] >> 11).astype(F32).astype(BF16) == numbers(DEV)
            hot = jnp.where(hot, one, none)
            part = lax.dot_general(hot, spread, NT, preferred_element_type=F32)
            parts.append(part + pltpu.roll(part, NVEC * CAP, 1))
        for v in range(NVEC):
            values = jnp.concatenate([p[:, v * CAP : (v + 1) * CAP] for p in parts], axis=1)
            put(jnp.round(values * inverse), group * 2 + v, 4)
    out_ref[...] = stage[...].astype(jnp.int32).astype(jnp.int16)


def bricks_kernel(
    got_ref, packed_ref, kappa_ref, out_ref, halo_ref, sums, wheres, at_cells, hots
):
    for r in range(ROWS):
        for g in range(2):
            total = None
            for c in range(4):
                at = ((r * 2 + g) * 4 + c) * SLAB
                one = got_ref[at : at + SLAB, :].astype(jnp.int32).astype(F32)
                one = jnp.where(iota((SLAB, 128), 0) < 12, one * step_at(one[15:16]), one)
                total = one if total is None else total + one
            wheres[g, r * SLAB : (r + 1) * SLAB, :] = total
    sums[...] = wheres[0] + wheres[1]
    for g in range(2):
        place = wheres[g] - 1.0
        cell = jnp.floor(place * (1.0 / NZ))
        at_cells[g] = cell
        wheres[g] = place - cell * NZ
    sub = iota((8, 128), 0)
    z_row = iota((NZ, 128), 0).astype(F32)
    for j in range(3):
        for r in range(ROWS):
            for g in range(2):
                lanes = slice((r * 2 + g) * 128, (r * 2 + g + 1) * 128)
                at = r * SLAB + j * 4 + g * 2
                pair = jnp.where(sub < 4, sums[at : at + 1, :], sums[at + 1 : at + 2, :])
                high = pair.astype(BF16).astype(F32)
                low = pair - high
                p = r * SLAB + 12 + j
                cell = at_cells[g, p : p + 1, :]
                z_at = wheres[g, p : p + 1, :]
                wanted = [cell == (x * CY + sub % CY).astype(F32) for x in range(CX)]
                rows = jnp.concatenate(
                    [jnp.where(w, part, 0.0) for part in (high, low) for w in wanted], axis=0
                )
                hots[0, 0:64, lanes] = rows.astype(BF16)
                hots[1, :, lanes] = jnp.where(z_at == z_row, 1.0, 0.0).astype(BF16)
        both = lax.dot_general(hots[0, 0:64, :], hots[1], NT, preferred_element_type=F32)
        out_ref[j * 32 : (j + 1) * 32, :] = both[0:32] + both[32:64]
    my_row = lax.axis_index("row")
    half = CX * CY // NVEC
    for j, r in ((0, jnp.maximum(my_row - 1, 0)), (2, jnp.minimum(my_row + 1, ROWS - 1))):
        block = packed_ref[r, :, PTS:].astype(F32)
        for q in range(half):
            for v in range(NVEC):
                at = FIELD + j * CX * CY + v * half + q
                out_ref[at : at + 1, :] = block[v : v + 1, q * NZ : (q + 1) * NZ]
    for x in range(CX):
        at = FIELD + CX * CY + x * CY
        out_ref[at : at + CY, :] = kappa_ref[x]
    level, inverse = level_of(out_ref[0:FIELD, :])

    def store(at, values):
        values = jnp.round(values).astype(jnp.int32).astype(jnp.int16)
        for c in range(COLS):
            halo_ref[c * MESSAGE + at : c * MESSAGE + at + values.shape[0], :] = values

    store(0, out_ref[8 : FIELD - 8, :] * inverse)
    store(HALO, out_ref[FIELD + 2 * CY : FIELD + 10 * CY, :] * KAPPA_STEPS)
    store(HALO + 8 * CY, jnp.broadcast_to(level, (16, 128)))


def prior_kernel(own_ref, halo_ref, out_ref):
    my_row, my_col = lax.axis_index("row"), lax.axis_index("col")
    wide = 3 * CX
    inside_x = [
        jnp.where(my_row > 0, 1.0, 0.0),
        jnp.float32(1.0),
        jnp.where(my_row < ROWS - 1, 1.0, 0.0),
    ]
    inside_y = [
        jnp.where(my_col > 0, 1.0, 0.0),
        jnp.float32(1.0),
        jnp.where(my_col < COLS - 1, 1.0, 0.0),
    ]
    y_at = iota((8, NZ), 0) % CY
    z_at = iota((8, NZ), 1)
    none = jnp.zeros((8, NZ), F32)
    us, ks = [], []
    before, after = jnp.maximum(my_col - 1, 0), jnp.minimum(my_col + 1, COLS - 1)
    for b, c in enumerate((before, None, after)):
        if c is None:
            field = [own_ref[8 * x : 8 * x + 8, :] for x in range(wide)]
            rows = [own_ref[FIELD + CY * x : FIELD + CY * (x + 1), :] for x in range(wide)]
            kappas = [6.0 + jnp.concatenate([row, row], axis=0) for row in rows]
        else:
            at = pl.multiple_of(c * MESSAGE, MESSAGE)
            got = halo_ref[pl.ds(at, MESSAGE), :].astype(jnp.int32).astype(F32)
            values = got[0:HALO] * (step_at(got[HALO + 8 * CY : HALO + 8 * CY + 1]) * inside_y[b])
            field = [values[8 * x : 8 * x + 8] for x in range(wide - 2)]
            field = [none] + field + [none]
            values = got[HALO : HALO + 8 * CY] * (1.0 / KAPPA_STEPS) + 6.0
            rows = [values[CY * x : CY * (x + 1)] for x in range(8)]
            kappas = [none] * 2 + [jnp.concatenate([row, row], axis=0) for row in rows] + [none] * 2
        us.append(field)
        ks.append(kappas)
    for step in range(1, 5):
        new = [[None] * wide for _ in range(3)]
        for b in range(3):
            if step == 4 and b != 1:
                continue
            edge = step if b == 1 else step + 1
            for x in range(edge, wide - edge):
                u = us[b][x]
                lower = pltpu.roll(us[b - 1][x], 5, 0) if b > 0 and us[b - 1][x] is not None else 0.0
                upper = pltpu.roll(us[b + 1][x], 3, 0) if b < 2 and us[b + 1][x] is not None else 0.0
                beside = us[b][x - 1] + us[b][x + 1]
                beside = beside + jnp.where(y_at == 0, lower, pltpu.roll(u, 1, 0))
                beside = beside + jnp.where(y_at == CY - 1, upper, pltpu.roll(u, 7, 0))
                beside = beside + jnp.where(z_at == 0, 0.0, pltpu.roll(u, 1, 1))
                beside = beside + jnp.where(z_at == NZ - 1, 0.0, pltpu.roll(u, NZ - 1, 1))
                result = (ks[b][x] * u - beside) * 0.125
                if step < 4:
                    if b != 1 and x // CX != 1:
                        result = result * (inside_y[b] * inside_x[x // CX])
                    elif b != 1:
                        result = result * inside_y[b]
                    elif x // CX != 1:
                        result = result * inside_x[x // CX]
                new[b][x] = result
        us = new
    for x in range(CX):
        for v in range(NVEC):
            out_ref[v, x] = us[1][CX + x][v * CY : (v + 1) * CY]


def cost(flops, size):
    return pl.CostEstimate(flops=flops, bytes_accessed=size, transcendentals=0)


def in_hbm(*arrays):
    return [pltpu.with_memory_space_constraint(a, pltpu.HBM) for a in arrays]


def in_vmem(*arrays):
    return [pltpu.with_memory_space_constraint(a, pltpu.VMEM) for a in arrays]


def params(mib):
    return pltpu.CompilerParams(vmem_limit_bytes=mib * MIB)


def per_device(
    vectors, lr_left, lr_right, tile_rank, leaf_values, leaf_places, cluster_perm, kappa
):
    vmem = pl.BlockSpec(memory_space=pltpu.VMEM)
    hbm = pl.BlockSpec(memory_space=pltpu.HBM)
    points = COLS * PTS
    terms = TILE_ROWS * TILE_COLS * KMAX
    packed_shape = (ROWS, NVEC, PTS + PTS // NVEC)
    packed, kappa_own, perm, ranks = pl.pallas_call(
        pack_kernel,
        out_shape=(
            pltpu.VMEM(packed_shape, BF16),
            pltpu.VMEM((CX, CY, NZ), F32),
            pltpu.VMEM((1, points), jnp.int32),
            pltpu.VMEM((1, TILE_ROWS * TILE_COLS), jnp.int32),
        ),
        in_specs=[hbm] * 4,
        out_specs=(vmem,) * 4,
        scratch_shapes=[pltpu.VMEM((NVEC, PTS), BF16), pltpu.SemaphoreType.DMA((4,))],
        compiler_params=params(8),
        name="pack",
    )(*in_hbm(vectors[:, 0], kappa, cluster_perm, tile_rank[0]))
    packed = lax.all_to_all(packed, "row", 0, 0, tiled=True)
    rank, place, right = pl.pallas_call(
        slots_kernel,
        out_shape=(
            pltpu.VMEM((1, points), F32),
            pltpu.VMEM((DEV, 128), F32),
            pltpu.VMEM((terms, TS), BF16),
        ),
        in_specs=[vmem, hbm],
        out_specs=(vmem,) * 3,
        scratch_shapes=[pltpu.SemaphoreType.DMA],
        compiler_params=params(16),
        cost_estimate=cost(1 << 31, 1 << 20),
        name="slots",
    )(perm, *in_hbm(lr_right.reshape(terms, TS)))
    send = pl.pallas_call(
        send_kernel,
        out_shape=jax.ShapeDtypeStruct((DEV * SLAB, 128), jnp.int16),
        in_specs=[hbm] * 3 + [vmem] * 6,
        out_specs=vmem,
        scratch_shapes=[
            pltpu.VMEM((terms, TS), BF16),
            pltpu.VMEM((NLEAF, LEAF, LEAF), BF16),
            pltpu.VMEM((16, TS), F32),
            pltpu.VMEM((16, TS), F32),
            pltpu.VMEM((DEV * SLAB, 128), F32),
            pltpu.SMEM((2, NLEAF), jnp.int32),
            pltpu.SemaphoreType.DMA((1 + 2 * PIECES,)),
        ],
        compiler_params=params(32),
        cost_estimate=cost(1 << 31, 8 << 20),
        name="partial_sums",
    )(
        *in_hbm(leaf_places[0, 0].T, lr_left.reshape(terms, TS), leaf_values[0, 0]),
        *in_vmem(packed, ranks, perm, rank, place, right),
    )
    got = lax.all_to_all(send.reshape(DEV, SLAB, 128), ("row", "col"), 0, 0, tiled=True)
    own, halo = pl.pallas_call(
        bricks_kernel,
        out_shape=(
            pltpu.VMEM((FIELD + 3 * CX * CY, NZ), F32),
            pltpu.VMEM((COLS * MESSAGE, NZ), jnp.int16),
        ),
        in_specs=[vmem] * 3,
        out_specs=(vmem,) * 2,
        scratch_shapes=[
            pltpu.VMEM((ROWS * SLAB, 128), F32),
            pltpu.VMEM((2, ROWS * SLAB, 128), F32),
            pltpu.VMEM((2, ROWS * SLAB, 128), F32),
            pltpu.VMEM((2, NZ, 4096), BF16),
        ],
        compiler_params=params(16),
        cost_estimate=cost(1 << 30, 1 << 20),
        name="bricks",
    )(got.reshape(DEV * SLAB, 128), packed, kappa_own)
    halo = lax.all_to_all(halo.reshape(COLS, MESSAGE, NZ), "col", 0, 0, tiled=True)
    return pl.pallas_call(
        prior_kernel,
        out_shape=jax.ShapeDtypeStruct((NVEC, CX, CY, NZ), F32),
        in_specs=[vmem] * 2,
        out_specs=vmem,
        compiler_params=params(8),
        cost_estimate=cost(1 << 24, 1 << 20),
        name="prior",
    )(own, halo.reshape(COLS * MESSAGE, NZ))


def solution(mesh):
    in_specs = (
        P(None, "col", "row"),
        P("row", "col", None, None, None),
        P("row", "col", None, None, None),
        P("row", "col", None),
        P("row", "col", None, None, None),
        P("row", "col", None, None),
        P("row", None),
        P("row", "col", None),
    )
    out_specs = P(None, "row", "col", None)
    return jax.shard_map(
        per_device, mesh=mesh, in_specs=in_specs, out_specs=out_specs, check_vma=False
    )
```

```python
import jax
import jax.numpy as jnp
from jax import lax
from jax.experimental import pallas as pl
from jax.experimental.pallas import tpu as pltpu
from jax.sharding import PartitionSpec as P

NVEC = 2
CX = 4
CY = 4
NZ = 128
TILE_ROWS = 4
TILE_COLS = 8
KMAX = 8
LEAF = 512
NLEAF = 8
PTS = 2048
ROWS = 16
COLS = 8
TS = 4096
CAP = 32
DEV = ROWS * COLS
PIECES = 2
SLAB = 16
F32 = jnp.float32
BF16 = jnp.bfloat16
NT = (((1,), (1,)), ((), ()))
MIB = 1 << 20
LEVELS = 64.0
STEPS = 32000.0
KAPPA_STEPS = 8000.0
FIELD = 3 * CX * NVEC * CY
HALO = FIELD - 2 * NVEC * CY
MESSAGE = HALO + 8 * CY + 16


def iota(shape, dim):
    return lax.broadcasted_iota(jnp.int32, shape, dim)


def pack_kernel(
    vectors_hbm, kappa_hbm, perm_hbm, rank_hbm, out_ref, kappa_ref, perm_ref, rank_ref, vectors, sems
):
    pairs = (
        (vectors_hbm, vectors),
        (kappa_hbm, kappa_ref),
        (perm_hbm, perm_ref),
        (rank_hbm, rank_ref),
    )
    copies = [pltpu.make_async_copy(a, b, sems.at[i]) for i, (a, b) in enumerate(pairs)]
    for copy in copies:
        copy.start()
    copies[0].wait()
    for s in range(ROWS):
        out_ref[s, :, 0:PTS] = vectors[...]
    copies[1].wait()
    rows = [kappa_ref[q // CY, q % CY : q % CY + 1, :] for q in range(CX * CY)]
    half = CX * CY // NVEC
    for q in range(half):
        pair = jnp.concatenate([rows[q], rows[half + q]], axis=0).astype(BF16)
        for s in range(ROWS):
            out_ref[s, :, PTS + q * NZ : PTS + (q + 1) * NZ] = pair
    copies[2].wait()
    copies[3].wait()


def slots_kernel(perm_ref, right_hbm, rank_ref, place_ref, right, sem):
    copy = pltpu.make_async_copy(right_hbm, right, sem)
    copy.start()
    chunk = 256
    upto = jnp.where(iota((chunk, chunk), 0) <= iota((chunk, chunk), 1), 1.0, 0.0).astype(BF16)
    brick = iota((DEV, chunk), 0)
    carry = jnp.zeros((COLS * DEV, 1), F32)
    for j in range(PTS // chunk):
        lanes = [slice(k * PTS + j * chunk, k * PTS + (j + 1) * chunk) for k in range(COLS)]
        masks = [(perm_ref[0:1, at] >> 11) == brick for at in lanes]
        hot = jnp.concatenate([jnp.where(m, 1.0, 0.0).astype(BF16) for m in masks], axis=0)
        total = jnp.dot(hot, upto, preferred_element_type=F32) + carry
        for k in range(COLS):
            at = jnp.where(masks[k], total[k * DEV : (k + 1) * DEV], 0.0)
            rank_ref[0:1, lanes[k]] = jnp.sum(at, axis=0, keepdims=True) - 1.0
        carry = total[:, chunk - 1 : chunk]
    col = lax.axis_index("col")
    start = pl.multiple_of(col * PTS, PTS)
    own = perm_ref[0:1, pl.ds(start, PTS)]
    slot = rank_ref[0:1, pl.ds(start, PTS)] + ((col % 4) * CAP).astype(F32)
    here = jnp.where(slot == iota((128, PTS), 0).astype(F32), 1.0, 0.0).astype(BF16)
    hot = jnp.where((own >> 11) == iota((DEV, PTS), 0), 1.0, 0.0).astype(BF16)
    inside = own & (PTS - 1)
    place = jnp.zeros((DEV, 128), F32)
    for part in (inside & ~(NZ - 1), (inside & (NZ - 1)) + 1):
        spread = here * part.astype(F32).astype(BF16)
        place = place + lax.dot_general(hot, spread, NT, preferred_element_type=F32)
    place_ref[...] = place
    copy.wait()


def level_of(values):
    largest = jnp.max(jnp.abs(values), axis=0, keepdims=True)
    largest = jnp.broadcast_to(jnp.max(largest, axis=1, keepdims=True), (8, 128))
    level = jnp.ceil(jnp.maximum(jnp.log2(largest), -100.0) * LEVELS)
    return level[0:1], (STEPS * jnp.exp2(level * (-1.0 / LEVELS)))[0:1]


def step_at(level):
    return jnp.exp2(level * (1.0 / LEVELS)) * (1.0 / STEPS)


def send_kernel(
    leaf_at_hbm,
    left_hbm,
    leaf_hbm,
    x_ref,
    tile_rank_ref,
    perm_ref,
    rank_ref,
    place_ref,
    right,
    out_ref,
    left,
    leaves,
    x_rows,
    sums,
    stage,
    leaf_at,
    sems,
):
    pairs = [(leaf_at_hbm, leaf_at)]
    each, wide = NLEAF // PIECES, TS // PIECES
    for i in range(PIECES):
        at = pl.ds(i * wide, wide)
        pairs.append((left_hbm.at[:, at], left.at[:, at]))
    for i in range(PIECES):
        at = pl.ds(i * each, each)
        pairs.append((leaf_hbm.at[at], leaves.at[at]))
    copies = [pltpu.make_async_copy(a, b, sems.at[i]) for i, (a, b) in enumerate(pairs)]
    for copy in copies:
        copy.start()

    def put(values, first_row, step):
        none = jnp.zeros((COLS, 128), F32)
        stage[pl.ds(first_row, COLS, stride=SLAB), :] = none
        stage[pl.ds(first_row + COLS * SLAB, DEV - COLS, stride=SLAB), :] = values[: DEV - COLS]
        stage[pl.ds(first_row + step, DEV, stride=SLAB), :] = values
        at = first_row + 2 * step
        stage[pl.ds(at, DEV - COLS, stride=SLAB), :] = values[COLS:]
        stage[pl.ds(at + (DEV - COLS) * SLAB, COLS, stride=SLAB), :] = none

    put(place_ref[...], 12, 1)
    half = TS // PTS
    for s in range(ROWS):
        b, h = divmod(s, half)
        block = x_ref[s, :, 0:PTS].astype(F32)
        x_rows[b : b + 1, h * PTS : (h + 1) * PTS] = block[0:1]
        x_rows[8 + b : 9 + b, h * PTS : (h + 1) * PTS] = block[1:2]
    terms = TILE_ROWS * TILE_COLS * KMAX
    lane = iota((16, terms), 1)
    sub = iota((16, terms), 0)
    widen = jnp.where(
        iota((TILE_ROWS * TILE_COLS, terms), 1) // KMAX
        == iota((TILE_ROWS * TILE_COLS, terms), 0),
        1.0,
        0.0,
    ).astype(BF16)
    ranks = jnp.broadcast_to(tile_rank_ref[...].astype(F32), (16, TILE_ROWS * TILE_COLS))
    rank_lane = jnp.dot(ranks.astype(BF16), widen, preferred_element_type=F32)
    keep = (sub % 8 == (lane // KMAX) % TILE_COLS) & ((lane % KMAX).astype(F32) < rank_lane)
    x_all = x_rows[...].astype(BF16)
    projected = lax.dot_general(x_all, right[...], NT, preferred_element_type=F32)
    projected = jnp.where(keep, projected, 0.0)
    first = jnp.sum(projected[0:8], axis=0, keepdims=True)
    second = jnp.sum(projected[8:16], axis=0, keepdims=True)
    by_row = jnp.where(sub < 8, first, second)
    by_row = jnp.where(sub % 8 == lane // (TILE_COLS * KMAX), by_row, 0.0).astype(BF16)
    for i in range(PIECES):
        copies[1 + i].wait()
        at = (slice(None), slice(i * wide, (i + 1) * wide))
        sums[at] = jnp.dot(by_row, left[at], preferred_element_type=F32)
    copies[0].wait()
    per_tile = TS // LEAF
    for l in range(NLEAF):
        if l % each == 0:
            copies[1 + PIECES + l // each].wait()
        i, j = leaf_at[0, l], leaf_at[1, l]
        from_lane = pl.multiple_of((j % per_tile) * LEAF, LEAF)
        to_lane = pl.multiple_of((i % per_tile) * LEAF, LEAF)
        picked = jnp.concatenate(
            [x_rows[pl.ds(8 * v + j // per_tile, 1), pl.ds(from_lane, LEAF)] for v in range(NVEC)],
            axis=0,
        ).astype(BF16)
        near = lax.dot_general(picked, leaves[l], NT, preferred_element_type=F32)
        for v in range(NVEC):
            at = (pl.ds(8 * v + i // per_tile, 1), pl.ds(to_lane, LEAF))
            sums[at] = sums[at] + near[v : v + 1]
    level, inverse = level_of(sums[...])

    stage[pl.ds(15, DEV, stride=SLAB), :] = jnp.broadcast_to(level, (DEV, 128))
    one, none = jnp.ones((), BF16), jnp.zeros((), BF16)

    def numbers(count):
        return iota((count, PTS), 0).astype(F32).astype(BF16)

    for group in range(2):
        parts = []
        for kk in range(4):
            k = group * 4 + kk
            a, h = divmod(k, half)
            at = slice(k * PTS, (k + 1) * PTS)
            slot = rank_ref[0:1, at].astype(BF16) == numbers(CAP)
            slot = jnp.where(slot, one, none)
            rows = [sums[8 * v + a : 8 * v + a + 1, h * PTS : (h + 1) * PTS] for v in range(NVEC)]
            highs = [row.astype(BF16) for row in rows]
            lows = [(row - high.astype(F32)).astype(BF16) for row, high in zip(rows, highs)]
            spread = jnp.concatenate([slot * row for row in highs + lows], axis=0)
            hot = (perm_ref[0:1, at] >> 11).astype(F32).astype(BF16) == numbers(DEV)
            hot = jnp.where(hot, one, none)
            part = lax.dot_general(hot, spread, NT, preferred_element_type=F32)
            parts.append(part + pltpu.roll(part, NVEC * CAP, 1))
        for v in range(NVEC):
            values = jnp.concatenate([p[:, v * CAP : (v + 1) * CAP] for p in parts], axis=1)
            put(jnp.round(values * inverse), group * 2 + v, 4)
    out_ref[...] = stage[...].astype(jnp.int32).astype(jnp.int16)


def bricks_kernel(
    got_ref, packed_ref, kappa_ref, out_ref, halo_ref, sums, wheres, at_cells, hots
):
    for r in range(ROWS):
        for g in range(2):
            total = None
            for c in range(4):
                at = ((r * 2 + g) * 4 + c) * SLAB
                one = got_ref[at : at + SLAB, :].astype(jnp.int32).astype(F32)
                one = jnp.where(iota((SLAB, 128), 0) < 12, one * step_at(one[15:16]), one)
                total = one if total is None else total + one
            wheres[g, r * SLAB : (r + 1) * SLAB, :] = total
    sums[...] = wheres[0] + wheres[1]
    for g in range(2):
        place = wheres[g] - 1.0
        cell = jnp.floor(place * (1.0 / NZ))
        at_cells[g] = cell
        wheres[g] = place - cell * NZ
    sub = iota((8, 128), 0)
    z_row = iota((NZ, 128), 0).astype(F32)
    for j in range(3):
        for r in range(ROWS):
            for g in range(2):
                lanes = slice((r * 2 + g) * 128, (r * 2 + g + 1) * 128)
                at = r * SLAB + j * 4 + g * 2
                pair = jnp.where(sub < 4, sums[at : at + 1, :], sums[at + 1 : at + 2, :])
                high = pair.astype(BF16).astype(F32)
                low = pair - high
                p = r * SLAB + 12 + j
                cell = at_cells[g, p : p + 1, :]
                z_at = wheres[g, p : p + 1, :]
                wanted = [cell == (x * CY + sub % CY).astype(F32) for x in range(CX)]
                rows = jnp.concatenate(
                    [jnp.where(w, part, 0.0) for part in (high, low) for w in wanted], axis=0
                )
                hots[0, 0:64, lanes] = rows.astype(BF16)
                hots[1, :, lanes] = jnp.where(z_at == z_row, 1.0, 0.0).astype(BF16)
        both = lax.dot_general(hots[0, 0:64, :], hots[1], NT, preferred_element_type=F32)
        out_ref[j * 32 : (j + 1) * 32, :] = both[0:32] + both[32:64]
    my_row = lax.axis_index("row")
    half = CX * CY // NVEC
    for j, r in ((0, jnp.maximum(my_row - 1, 0)), (2, jnp.minimum(my_row + 1, ROWS - 1))):
        block = packed_ref[r, :, PTS:].astype(F32)
        for q in range(half):
            for v in range(NVEC):
                at = FIELD + j * CX * CY + v * half + q
                out_ref[at : at + 1, :] = block[v : v + 1, q * NZ : (q + 1) * NZ]
    for x in range(CX):
        at = FIELD + CX * CY + x * CY
        out_ref[at : at + CY, :] = kappa_ref[x]
    level, inverse = level_of(out_ref[0:FIELD, :])

    def store(at, values):
        halo_ref[at : at + values.shape[0], :] = (
            jnp.round(values).astype(jnp.int32).astype(jnp.int16)
        )

    store(0, out_ref[8 : FIELD - 8, :] * inverse)
    store(HALO, out_ref[FIELD + 2 * CY : FIELD + 10 * CY, :] * KAPPA_STEPS)
    store(HALO + 8 * CY, jnp.broadcast_to(level, (16, 128)))


def prior_kernel(own_ref, even_ref, odd_ref, out_ref):
    my_row, my_col = lax.axis_index("row"), lax.axis_index("col")
    wide = 3 * CX
    inside_x = [
        jnp.where(my_row > 0, 1.0, 0.0),
        jnp.float32(1.0),
        jnp.where(my_row < ROWS - 1, 1.0, 0.0),
    ]
    inside_y = [
        jnp.where(my_col > 0, 1.0, 0.0),
        jnp.float32(1.0),
        jnp.where(my_col < COLS - 1, 1.0, 0.0),
    ]
    y_at = iota((8, NZ), 0) % CY
    z_at = iota((8, NZ), 1)
    none = jnp.zeros((8, NZ), F32)
    us, ks = [], []
    even, odd = (ref[...].astype(jnp.int32).astype(F32) for ref in (even_ref, odd_ref))
    at_even = jnp.broadcast_to(my_col % 2, (MESSAGE, NZ)) == 0
    before, after = jnp.where(at_even, odd, even), jnp.where(at_even, even, odd)
    for b, got in enumerate((before, None, after)):
        if got is None:
            field = [own_ref[8 * x : 8 * x + 8, :] for x in range(wide)]
            rows = [own_ref[FIELD + CY * x : FIELD + CY * (x + 1), :] for x in range(wide)]
            kappas = [6.0 + jnp.concatenate([row, row], axis=0) for row in rows]
        else:
            values = got[0:HALO] * (step_at(got[HALO + 8 * CY : HALO + 8 * CY + 1]) * inside_y[b])
            field = [values[8 * x : 8 * x + 8] for x in range(wide - 2)]
            field = [none] + field + [none]
            values = got[HALO : HALO + 8 * CY] * (1.0 / KAPPA_STEPS) + 6.0
            rows = [values[CY * x : CY * (x + 1)] for x in range(8)]
            kappas = [none] * 2 + [jnp.concatenate([row, row], axis=0) for row in rows] + [none] * 2
        us.append(field)
        ks.append(kappas)
    for step in range(1, 5):
        new = [[None] * wide for _ in range(3)]
        for b in range(3):
            if step == 4 and b != 1:
                continue
            edge = step if b == 1 else step + 1
            for x in range(edge, wide - edge):
                u = us[b][x]
                lower = pltpu.roll(us[b - 1][x], 5, 0) if b > 0 and us[b - 1][x] is not None else 0.0
                upper = pltpu.roll(us[b + 1][x], 3, 0) if b < 2 and us[b + 1][x] is not None else 0.0
                beside = us[b][x - 1] + us[b][x + 1]
                beside = beside + jnp.where(y_at == 0, lower, pltpu.roll(u, 1, 0))
                beside = beside + jnp.where(y_at == CY - 1, upper, pltpu.roll(u, 7, 0))
                beside = beside + jnp.where(z_at == 0, 0.0, pltpu.roll(u, 1, 1))
                beside = beside + jnp.where(z_at == NZ - 1, 0.0, pltpu.roll(u, NZ - 1, 1))
                result = (ks[b][x] * u - beside) * 0.125
                if step < 4:
                    if b != 1 and x // CX != 1:
                        result = result * (inside_y[b] * inside_x[x // CX])
                    elif b != 1:
                        result = result * inside_y[b]
                    elif x // CX != 1:
                        result = result * inside_x[x // CX]
                new[b][x] = result
        us = new
    for x in range(CX):
        for v in range(NVEC):
            out_ref[v, x] = us[1][CX + x][v * CY : (v + 1) * CY]


def swapped(array, axis, first):
    pairs = [(i, i + 1) for i in range(first, lax.axis_size(axis) - 1, 2)]
    return lax.ppermute(array, axis, pairs + [(b, a) for a, b in pairs])


def cost(flops, size):
    return pl.CostEstimate(flops=flops, bytes_accessed=size, transcendentals=0)


def in_hbm(*arrays):
    return [pltpu.with_memory_space_constraint(a, pltpu.HBM) for a in arrays]


def in_vmem(*arrays):
    return [pltpu.with_memory_space_constraint(a, pltpu.VMEM) for a in arrays]


def params(mib):
    return pltpu.CompilerParams(vmem_limit_bytes=mib * MIB)


def per_device(
    vectors, lr_left, lr_right, tile_rank, leaf_values, leaf_places, cluster_perm, kappa
):
    vmem = pl.BlockSpec(memory_space=pltpu.VMEM)
    hbm = pl.BlockSpec(memory_space=pltpu.HBM)
    points = COLS * PTS
    terms = TILE_ROWS * TILE_COLS * KMAX
    packed_shape = (ROWS, NVEC, PTS + PTS // NVEC)
    packed, kappa_own, perm, ranks = pl.pallas_call(
        pack_kernel,
        out_shape=(
            pltpu.VMEM(packed_shape, BF16),
            pltpu.VMEM((CX, CY, NZ), F32),
            pltpu.VMEM((1, points), jnp.int32),
            pltpu.VMEM((1, TILE_ROWS * TILE_COLS), jnp.int32),
        ),
        in_specs=[hbm] * 4,
        out_specs=(vmem,) * 4,
        scratch_shapes=[pltpu.VMEM((NVEC, PTS), BF16), pltpu.SemaphoreType.DMA((4,))],
        compiler_params=params(8),
        name="pack",
    )(*in_hbm(vectors[:, 0], kappa, cluster_perm, tile_rank[0]))
    packed = lax.all_to_all(packed, "row", 0, 0, tiled=True)
    rank, place, right = pl.pallas_call(
        slots_kernel,
        out_shape=(
            pltpu.VMEM((1, points), F32),
            pltpu.VMEM((DEV, 128), F32),
            pltpu.VMEM((terms, TS), BF16),
        ),
        in_specs=[vmem, hbm],
        out_specs=(vmem,) * 3,
        scratch_shapes=[pltpu.SemaphoreType.DMA],
        compiler_params=params(16),
        cost_estimate=cost(1 << 31, 1 << 20),
        name="slots",
    )(perm, *in_hbm(lr_right.reshape(terms, TS)))
    send = pl.pallas_call(
        send_kernel,
        out_shape=jax.ShapeDtypeStruct((DEV * SLAB, 128), jnp.int16),
        in_specs=[hbm] * 3 + [vmem] * 6,
        out_specs=vmem,
        scratch_shapes=[
            pltpu.VMEM((terms, TS), BF16),
            pltpu.VMEM((NLEAF, LEAF, LEAF), BF16),
            pltpu.VMEM((16, TS), F32),
            pltpu.VMEM((16, TS), F32),
            pltpu.VMEM((DEV * SLAB, 128), F32),
            pltpu.SMEM((2, NLEAF), jnp.int32),
            pltpu.SemaphoreType.DMA((1 + 2 * PIECES,)),
        ],
        compiler_params=params(32),
        cost_estimate=cost(1 << 31, 8 << 20),
        name="partial_sums",
    )(
        *in_hbm(leaf_places[0, 0].T, lr_left.reshape(terms, TS), leaf_values[0, 0]),
        *in_vmem(packed, ranks, perm, rank, place, right),
    )
    got = lax.all_to_all(send.reshape(DEV, SLAB, 128), ("row", "col"), 0, 0, tiled=True)
    own, halo = pl.pallas_call(
        bricks_kernel,
        out_shape=(
            pltpu.VMEM((FIELD + 3 * CX * CY, NZ), F32),
            pltpu.VMEM((MESSAGE, NZ), jnp.int16),
        ),
        in_specs=[vmem] * 3,
        out_specs=(vmem,) * 2,
        scratch_shapes=[
            pltpu.VMEM((ROWS * SLAB, 128), F32),
            pltpu.VMEM((2, ROWS * SLAB, 128), F32),
            pltpu.VMEM((2, ROWS * SLAB, 128), F32),
            pltpu.VMEM((2, NZ, 4096), BF16),
        ],
        compiler_params=params(16),
        cost_estimate=cost(1 << 30, 1 << 20),
        name="bricks",
    )(got.reshape(DEV * SLAB, 128), packed, kappa_own)
    odd = swapped(halo, "col", 1)
    even = swapped(halo, "col", 0)
    return pl.pallas_call(
        prior_kernel,
        out_shape=jax.ShapeDtypeStruct((NVEC, CX, CY, NZ), F32),
        in_specs=[vmem] * 3,
        out_specs=vmem,
        compiler_params=params(8),
        cost_estimate=cost(1 << 24, 1 << 20),
        name="prior",
    )(own, even, odd)


def solution(mesh):
    in_specs = (
        P(None, "col", "row"),
        P("row", "col", None, None, None),
        P("row", "col", None, None, None),
        P("row", "col", None),
        P("row", "col", None, None, None),
        P("row", "col", None, None),
        P("row", None),
        P("row", "col", None),
    )
    out_specs = P(None, "row", "col", None)
    return jax.shard_map(
        per_device, mesh=mesh, in_specs=in_specs, out_specs=out_specs, check_vma=False
    )
```

```python
import jax
import jax.numpy as jnp
from jax import lax
from jax.experimental import pallas as pl
from jax.experimental.pallas import tpu as pltpu
from jax.sharding import PartitionSpec as P

NVEC = 2
CX = 4
CY = 4
NZ = 128
TILE_ROWS = 4
TILE_COLS = 8
KMAX = 8
LEAF = 512
NLEAF = 8
PTS = 2048
ROWS = 16
COLS = 8
TS = 4096
CAP = 32
DEV = ROWS * COLS
PIECES = 2
LEAF_PIECES = ((0, 2), (2, 4), (4, 6), (6, 8))
SLAB = 16
F32 = jnp.float32
BF16 = jnp.bfloat16
NT = (((1,), (1,)), ((), ()))
MIB = 1 << 20
LEVELS = 64.0
STEPS = 32000.0
KAPPA_STEPS = 8000.0
FIELD = 3 * CX * NVEC * CY
HALO = FIELD - 2 * NVEC * CY
MESSAGE = HALO + 8 * CY + 16


def iota(shape, dim):
    return lax.broadcasted_iota(jnp.int32, shape, dim)


def pack_kernel(
    vectors_hbm, kappa_hbm, perm_hbm, rank_hbm, out_ref, kappa_ref, perm_ref, rank_ref, vectors, sems
):
    pairs = (
        (vectors_hbm, vectors),
        (kappa_hbm, kappa_ref),
        (perm_hbm, perm_ref),
        (rank_hbm, rank_ref),
    )
    copies = [pltpu.make_async_copy(a, b, sems.at[i]) for i, (a, b) in enumerate(pairs)]
    for copy in copies:
        copy.start()
    copies[0].wait()
    for s in range(ROWS):
        out_ref[s, :, 0:PTS] = vectors[...]
    copies[1].wait()
    rows = [kappa_ref[q // CY, q % CY : q % CY + 1, :] for q in range(CX * CY)]
    half = CX * CY // NVEC
    for q in range(half):
        pair = jnp.concatenate([rows[q], rows[half + q]], axis=0).astype(BF16)
        for s in range(ROWS):
            out_ref[s, :, PTS + q * NZ : PTS + (q + 1) * NZ] = pair
    copies[2].wait()
    copies[3].wait()


def slots_kernel(perm_ref, right_hbm, rank_ref, place_ref, right, sem):
    copy = pltpu.make_async_copy(right_hbm, right, sem)
    copy.start()
    chunk = 256
    upto = jnp.where(iota((chunk, chunk), 0) <= iota((chunk, chunk), 1), 1.0, 0.0).astype(BF16)
    brick = iota((DEV, chunk), 0)
    carry = jnp.zeros((COLS * DEV, 1), F32)
    for j in range(PTS // chunk):
        lanes = [slice(k * PTS + j * chunk, k * PTS + (j + 1) * chunk) for k in range(COLS)]
        masks = [(perm_ref[0:1, at] >> 11) == brick for at in lanes]
        hot = jnp.concatenate([jnp.where(m, 1.0, 0.0).astype(BF16) for m in masks], axis=0)
        total = jnp.dot(hot, upto, preferred_element_type=F32) + carry
        for k in range(COLS):
            at = jnp.where(masks[k], total[k * DEV : (k + 1) * DEV], 0.0)
            rank_ref[0:1, lanes[k]] = jnp.sum(at, axis=0, keepdims=True) - 1.0
        carry = total[:, chunk - 1 : chunk]
    col = lax.axis_index("col")
    start = pl.multiple_of(col * PTS, PTS)
    own = perm_ref[0:1, pl.ds(start, PTS)]
    slot = rank_ref[0:1, pl.ds(start, PTS)] + ((col % 4) * CAP).astype(F32)
    here = jnp.where(slot == iota((128, PTS), 0).astype(F32), 1.0, 0.0).astype(BF16)
    hot = jnp.where((own >> 11) == iota((DEV, PTS), 0), 1.0, 0.0).astype(BF16)
    inside = own & (PTS - 1)
    place = jnp.zeros((DEV, 128), F32)
    for part in (inside & ~(NZ - 1), (inside & (NZ - 1)) + 1):
        spread = here * part.astype(F32).astype(BF16)
        place = place + lax.dot_general(hot, spread, NT, preferred_element_type=F32)
    place_ref[...] = place
    copy.wait()


def level_of(values):
    largest = jnp.max(jnp.abs(values), axis=0, keepdims=True)
    largest = jnp.broadcast_to(jnp.max(largest, axis=1, keepdims=True), (8, 128))
    level = jnp.ceil(jnp.maximum(jnp.log2(largest), -100.0) * LEVELS)
    return level[0:1], (STEPS * jnp.exp2(level * (-1.0 / LEVELS)))[0:1]


def step_at(level):
    return jnp.exp2(level * (1.0 / LEVELS)) * (1.0 / STEPS)


def send_kernel(
    leaf_at_hbm,
    left_hbm,
    leaf_hbm,
    x_ref,
    tile_rank_ref,
    perm_ref,
    rank_ref,
    place_ref,
    right,
    out_ref,
    left,
    leaves,
    x_rows,
    sums,
    stage,
    leaf_at,
    sems,
):
    pairs = [(leaf_at_hbm, leaf_at)]
    wide = TS // PIECES
    for i in range(PIECES):
        at = pl.ds(i * wide, wide)
        pairs.append((left_hbm.at[:, at], left.at[:, at]))
    for first, last in LEAF_PIECES:
        at = pl.ds(first, last - first)
        pairs.append((leaf_hbm.at[at], leaves.at[at]))
    copies = [pltpu.make_async_copy(a, b, sems.at[i]) for i, (a, b) in enumerate(pairs)]
    for copy in copies:
        copy.start()

    def put(values, first_row, step):
        values = values.astype(jnp.int32)
        none = jnp.zeros((COLS, 128), jnp.int32)
        stage[pl.ds(first_row, COLS, stride=SLAB), :] = none
        stage[pl.ds(first_row + COLS * SLAB, DEV - COLS, stride=SLAB), :] = values[: DEV - COLS]
        stage[pl.ds(first_row + step, DEV, stride=SLAB), :] = values
        at = first_row + 2 * step
        stage[pl.ds(at, DEV - COLS, stride=SLAB), :] = values[COLS:]
        stage[pl.ds(at + (DEV - COLS) * SLAB, COLS, stride=SLAB), :] = none

    half = TS // PTS
    for s in range(ROWS):
        b, h = divmod(s, half)
        block = x_ref[s, :, 0:PTS].astype(F32)
        x_rows[b : b + 1, h * PTS : (h + 1) * PTS] = block[0:1]
        x_rows[8 + b : 9 + b, h * PTS : (h + 1) * PTS] = block[1:2]
    terms = TILE_ROWS * TILE_COLS * KMAX
    lane = iota((16, terms), 1)
    sub = iota((16, terms), 0)
    widen = jnp.where(
        iota((TILE_ROWS * TILE_COLS, terms), 1) // KMAX
        == iota((TILE_ROWS * TILE_COLS, terms), 0),
        1.0,
        0.0,
    ).astype(BF16)
    ranks = jnp.broadcast_to(tile_rank_ref[...].astype(F32), (16, TILE_ROWS * TILE_COLS))
    rank_lane = jnp.dot(ranks.astype(BF16), widen, preferred_element_type=F32)
    keep = (sub % 8 == (lane // KMAX) % TILE_COLS) & ((lane % KMAX).astype(F32) < rank_lane)
    x_all = x_rows[...].astype(BF16)
    projected = lax.dot_general(x_all, right[...], NT, preferred_element_type=F32)
    projected = jnp.where(keep, projected, 0.0)
    first = jnp.sum(projected[0:8], axis=0, keepdims=True)
    second = jnp.sum(projected[8:16], axis=0, keepdims=True)
    by_row = jnp.where(sub < 8, first, second)
    by_row = jnp.where(sub % 8 == lane // (TILE_COLS * KMAX), by_row, 0.0).astype(BF16)
    for i in range(PIECES):
        copies[1 + i].wait()
        at = (slice(None), slice(i * wide, (i + 1) * wide))
        sums[at] = jnp.dot(by_row, left[at], preferred_element_type=F32)
    copies[0].wait()
    per_tile = TS // LEAF
    for l in range(NLEAF):
        for n, (first, _) in enumerate(LEAF_PIECES):
            if l == first:
                copies[1 + PIECES + n].wait()
        i, j = leaf_at[0, l], leaf_at[1, l]
        from_lane = pl.multiple_of((j % per_tile) * LEAF, LEAF)
        to_lane = pl.multiple_of((i % per_tile) * LEAF, LEAF)
        picked = jnp.concatenate(
            [x_rows[pl.ds(8 * v + j // per_tile, 1), pl.ds(from_lane, LEAF)] for v in range(NVEC)],
            axis=0,
        ).astype(BF16)
        near = lax.dot_general(picked, leaves[l], NT, preferred_element_type=F32)
        for v in range(NVEC):
            at = (pl.ds(8 * v + i // per_tile, 1), pl.ds(to_lane, LEAF))
            sums[at] = sums[at] + near[v : v + 1]
    put(place_ref[...], 12, 1)
    level, inverse = level_of(sums[...])
    stage[pl.ds(15, DEV, stride=SLAB), :] = jnp.broadcast_to(level.astype(jnp.int32), (DEV, 128))
    one, none = jnp.ones((), BF16), jnp.zeros((), BF16)

    def numbers(count):
        return iota((count, PTS), 0).astype(F32).astype(BF16)

    for group in range(2):
        parts = []
        for kk in range(4):
            k = group * 4 + kk
            a, h = divmod(k, half)
            at = slice(k * PTS, (k + 1) * PTS)
            slot = rank_ref[0:1, at].astype(BF16) == numbers(CAP)
            slot = jnp.where(slot, one, none)
            rows = [sums[8 * v + a : 8 * v + a + 1, h * PTS : (h + 1) * PTS] for v in range(NVEC)]
            highs = [row.astype(BF16) for row in rows]
            lows = [(row - high.astype(F32)).astype(BF16) for row, high in zip(rows, highs)]
            spread = jnp.concatenate([slot * row for row in highs + lows], axis=0)
            hot = (perm_ref[0:1, at] >> 11).astype(F32).astype(BF16) == numbers(DEV)
            hot = jnp.where(hot, one, none)
            part = lax.dot_general(hot, spread, NT, preferred_element_type=F32)
            parts.append(part + pltpu.roll(part, NVEC * CAP, 1))
        for v in range(NVEC):
            values = jnp.concatenate([p[:, v * CAP : (v + 1) * CAP] for p in parts], axis=1)
            put(jnp.round(values * inverse), group * 2 + v, 4)
    out_ref[...] = stage[...].astype(jnp.int16)


def bricks_kernel(
    got_ref, packed_ref, kappa_ref, out_ref, halo_ref, sums, wheres, at_cells
):
    for r in range(ROWS):
        for g in range(2):
            total = None
            for c in range(4):
                at = ((r * 2 + g) * 4 + c) * SLAB
                one = got_ref[at : at + SLAB, :].astype(jnp.int32).astype(F32)
                one = jnp.where(iota((SLAB, 128), 0) < 12, one * step_at(one[15:16]), one)
                total = one if total is None else total + one
            wheres[g, r * SLAB : (r + 1) * SLAB, :] = total
    sums[...] = wheres[0] + wheres[1]
    for g in range(2):
        place = wheres[g] - 1.0
        cell = jnp.floor(place * (1.0 / NZ))
        at_cells[g] = cell
        wheres[g] = place - cell * NZ
    sub = iota((8, 128), 0)
    z_row = iota((NZ, 128), 0).astype(F32).astype(BF16)
    one, none = jnp.ones((), BF16), jnp.zeros((), BF16)
    for j in range(3):
        both = jnp.zeros((64, NZ), F32)
        for some in range(0, ROWS, 4):
            cells, heights = [], []
            for r, g in ((r, g) for r in range(some, some + 4) for g in range(2)):
                at = r * SLAB + j * 4 + g * 2
                pair = jnp.where(sub < 4, sums[at : at + 1, :], sums[at + 1 : at + 2, :])
                high = pair.astype(BF16).astype(F32)
                low = pair - high
                p = r * SLAB + 12 + j
                cell = at_cells[g, p : p + 1, :]
                wanted = [cell == (x * CY + sub % CY).astype(F32) for x in range(CX)]
                rows = [jnp.where(w, part, 0.0) for part in (high, low) for w in wanted]
                cells.append(jnp.concatenate(rows, axis=0).astype(BF16))
                z_at = wheres[g, p : p + 1, :].astype(BF16)
                heights.append(jnp.where(z_at == z_row, one, none))
            both = both + lax.dot_general(
                jnp.concatenate(cells, axis=1),
                jnp.concatenate(heights, axis=1),
                NT,
                preferred_element_type=F32,
            )
        out_ref[j * 32 : (j + 1) * 32, :] = both[0:32] + both[32:64]
    my_row = lax.axis_index("row")
    half = CX * CY // NVEC
    for j, r in ((0, jnp.maximum(my_row - 1, 0)), (2, jnp.minimum(my_row + 1, ROWS - 1))):
        block = packed_ref[r, :, PTS:].astype(F32)
        for q in range(half):
            for v in range(NVEC):
                at = FIELD + j * CX * CY + v * half + q
                out_ref[at : at + 1, :] = block[v : v + 1, q * NZ : (q + 1) * NZ]
    for x in range(CX):
        at = FIELD + CX * CY + x * CY
        out_ref[at : at + CY, :] = kappa_ref[x]
    level, inverse = level_of(out_ref[0:FIELD, :])

    def store(at, values):
        halo_ref[at : at + values.shape[0], :] = (
            jnp.round(values).astype(jnp.int32).astype(jnp.int16)
        )

    store(0, out_ref[8 : FIELD - 8, :] * inverse)
    store(HALO, out_ref[FIELD + 2 * CY : FIELD + 10 * CY, :] * KAPPA_STEPS)
    store(HALO + 8 * CY, jnp.broadcast_to(level, (16, 128)))


def prior_kernel(own_ref, even_ref, odd_ref, out_ref):
    my_row, my_col = lax.axis_index("row"), lax.axis_index("col")
    wide = 3 * CX
    inside_x = [
        jnp.where(my_row > 0, 1.0, 0.0),
        jnp.float32(1.0),
        jnp.where(my_row < ROWS - 1, 1.0, 0.0),
    ]
    inside_y = [
        jnp.where(my_col > 0, 1.0, 0.0),
        jnp.float32(1.0),
        jnp.where(my_col < COLS - 1, 1.0, 0.0),
    ]
    y_at = iota((8, NZ), 0) % CY
    z_at = iota((8, NZ), 1)
    none = jnp.zeros((8, NZ), F32)
    us, ks = [], []
    even, odd = (ref[...].astype(jnp.int32).astype(F32) for ref in (even_ref, odd_ref))
    at_even = jnp.broadcast_to(my_col % 2, (MESSAGE, NZ)) == 0
    before, after = jnp.where(at_even, odd, even), jnp.where(at_even, even, odd)
    for b, got in enumerate((before, None, after)):
        if got is None:
            field = [own_ref[8 * x : 8 * x + 8, :] for x in range(wide)]
            rows = [own_ref[FIELD + CY * x : FIELD + CY * (x + 1), :] for x in range(wide)]
            kappas = [6.0 + jnp.concatenate([row, row], axis=0) for row in rows]
        else:
            values = got[0:HALO] * (step_at(got[HALO + 8 * CY : HALO + 8 * CY + 1]) * inside_y[b])
            field = [values[8 * x : 8 * x + 8] for x in range(wide - 2)]
            field = [none] + field + [none]
            values = got[HALO : HALO + 8 * CY] * (1.0 / KAPPA_STEPS) + 6.0
            rows = [values[CY * x : CY * (x + 1)] for x in range(8)]
            kappas = [none] * 2 + [jnp.concatenate([row, row], axis=0) for row in rows] + [none] * 2
        us.append(field)
        ks.append(kappas)
    for step in range(1, 5):
        new = [[None] * wide for _ in range(3)]
        for b in range(3):
            if step == 4 and b != 1:
                continue
            edge = step if b == 1 else step + 1
            for x in range(edge, wide - edge):
                u = us[b][x]
                lower = pltpu.roll(us[b - 1][x], 5, 0) if b > 0 and us[b - 1][x] is not None else 0.0
                upper = pltpu.roll(us[b + 1][x], 3, 0) if b < 2 and us[b + 1][x] is not None else 0.0
                beside = us[b][x - 1] + us[b][x + 1]
                beside = beside + jnp.where(y_at == 0, lower, pltpu.roll(u, 1, 0))
                beside = beside + jnp.where(y_at == CY - 1, upper, pltpu.roll(u, 7, 0))
                beside = beside + jnp.where(z_at == 0, 0.0, pltpu.roll(u, 1, 1))
                beside = beside + jnp.where(z_at == NZ - 1, 0.0, pltpu.roll(u, NZ - 1, 1))
                result = (ks[b][x] * u - beside) * 0.125
                if step < 4:
                    if b != 1 and x // CX != 1:
                        result = result * (inside_y[b] * inside_x[x // CX])
                    elif b != 1:
                        result = result * inside_y[b]
                    elif x // CX != 1:
                        result = result * inside_x[x // CX]
                new[b][x] = result
        us = new
    for x in range(CX):
        for v in range(NVEC):
            out_ref[v, x] = us[1][CX + x][v * CY : (v + 1) * CY]


def swapped(array, axis, first):
    pairs = [(i, i + 1) for i in range(first, lax.axis_size(axis) - 1, 2)]
    return lax.ppermute(array, axis, pairs + [(b, a) for a, b in pairs])


def cost(flops, size):
    return pl.CostEstimate(flops=flops, bytes_accessed=size, transcendentals=0)


def in_hbm(*arrays):
    return [pltpu.with_memory_space_constraint(a, pltpu.HBM) for a in arrays]


def in_vmem(*arrays):
    return [pltpu.with_memory_space_constraint(a, pltpu.VMEM) for a in arrays]


def params(mib):
    return pltpu.CompilerParams(vmem_limit_bytes=mib * MIB)


def per_device(
    vectors, lr_left, lr_right, tile_rank, leaf_values, leaf_places, cluster_perm, kappa
):
    vmem = pl.BlockSpec(memory_space=pltpu.VMEM)
    hbm = pl.BlockSpec(memory_space=pltpu.HBM)
    points = COLS * PTS
    terms = TILE_ROWS * TILE_COLS * KMAX
    packed_shape = (ROWS, NVEC, PTS + PTS // NVEC)
    packed, kappa_own, perm, ranks = pl.pallas_call(
        pack_kernel,
        out_shape=(
            pltpu.VMEM(packed_shape, BF16),
            pltpu.VMEM((CX, CY, NZ), F32),
            pltpu.VMEM((1, points), jnp.int32),
            pltpu.VMEM((1, TILE_ROWS * TILE_COLS), jnp.int32),
        ),
        in_specs=[hbm] * 4,
        out_specs=(vmem,) * 4,
        scratch_shapes=[pltpu.VMEM((NVEC, PTS), BF16), pltpu.SemaphoreType.DMA((4,))],
        compiler_params=params(8),
        name="pack",
    )(*in_hbm(vectors[:, 0], kappa, cluster_perm, tile_rank[0]))
    packed = lax.all_to_all(packed, "row", 0, 0, tiled=True)
    rank, place, right = pl.pallas_call(
        slots_kernel,
        out_shape=(
            pltpu.VMEM((1, points), F32),
            pltpu.VMEM((DEV, 128), F32),
            pltpu.VMEM((terms, TS), BF16),
        ),
        in_specs=[vmem, hbm],
        out_specs=(vmem,) * 3,
        scratch_shapes=[pltpu.SemaphoreType.DMA],
        compiler_params=params(16),
        cost_estimate=cost(1 << 31, 1 << 20),
        name="slots",
    )(perm, *in_hbm(lr_right.reshape(terms, TS)))
    send = pl.pallas_call(
        send_kernel,
        out_shape=jax.ShapeDtypeStruct((DEV * SLAB, 128), jnp.int16),
        in_specs=[hbm] * 3 + [vmem] * 6,
        out_specs=vmem,
        scratch_shapes=[
            pltpu.VMEM((terms, TS), BF16),
            pltpu.VMEM((NLEAF, LEAF, LEAF), BF16),
            pltpu.VMEM((16, TS), F32),
            pltpu.VMEM((16, TS), F32),
            pltpu.VMEM((DEV * SLAB, 128), jnp.int32),
            pltpu.SMEM((2, NLEAF), jnp.int32),
            pltpu.SemaphoreType.DMA((1 + PIECES + len(LEAF_PIECES),)),
        ],
        compiler_params=params(32),
        cost_estimate=cost(1 << 31, 8 << 20),
        name="partial_sums",
    )(
        *in_hbm(leaf_places[0, 0].T, lr_left.reshape(terms, TS), leaf_values[0, 0]),
        *in_vmem(packed, ranks, perm, rank, place, right),
    )
    got = lax.all_to_all(send.reshape(DEV, SLAB, 128), ("row", "col"), 0, 0, tiled=True)
    own, halo = pl.pallas_call(
        bricks_kernel,
        out_shape=(
            pltpu.VMEM((FIELD + 3 * CX * CY, NZ), F32),
            pltpu.VMEM((MESSAGE, NZ), jnp.int16),
        ),
        in_specs=[vmem] * 3,
        out_specs=(vmem,) * 2,
        scratch_shapes=[
            pltpu.VMEM((ROWS * SLAB, 128), F32),
            pltpu.VMEM((2, ROWS * SLAB, 128), F32),
            pltpu.VMEM((2, ROWS * SLAB, 128), F32),
        ],
        compiler_params=params(16),
        cost_estimate=cost(1 << 30, 1 << 20),
        name="bricks",
    )(got.reshape(DEV * SLAB, 128), packed, kappa_own)
    odd = swapped(halo, "col", 1)
    even = swapped(halo, "col", 0)
    return pl.pallas_call(
        prior_kernel,
        out_shape=jax.ShapeDtypeStruct((NVEC, CX, CY, NZ), F32),
        in_specs=[vmem] * 3,
        out_specs=vmem,
        compiler_params=params(8),
        cost_estimate=cost(1 << 24, 1 << 20),
        name="prior",
    )(own, even, odd)


def solution(mesh):
    in_specs = (
        P(None, "col", "row"),
        P("row", "col", None, None, None),
        P("row", "col", None, None, None),
        P("row", "col", None),
        P("row", "col", None, None, None),
        P("row", "col", None, None),
        P("row", None),
        P("row", "col", None),
    )
    out_specs = P(None, "row", "col", None)
    return jax.shard_map(
        per_device, mesh=mesh, in_specs=in_specs, out_specs=out_specs, check_vma=False
    )
```

```python
import jax
import jax.numpy as jnp
from jax import lax
from jax.experimental import pallas as pl
from jax.experimental.pallas import tpu as pltpu
from jax.sharding import PartitionSpec as P

NVEC = 2
CX = 4
CY = 4
NZ = 128
TILE_ROWS = 4
TILE_COLS = 8
KMAX = 8
LEAF = 512
NLEAF = 8
PTS = 2048
ROWS = 16
COLS = 8
TS = 4096
CAP = 32
DEV = ROWS * COLS
PIECES = 2
LEAF_PIECES = ((0, 2), (2, 4), (4, 6), (6, 8))
SLAB = 8
F32 = jnp.float32
BF16 = jnp.bfloat16
NT = (((1,), (1,)), ((), ()))
MIB = 1 << 20
LEVELS = 64.0
STEPS = 32000.0
KAPPA_STEPS = 8000.0
FIELD = 3 * CX * NVEC * CY
HALO = FIELD - 2 * NVEC * CY
MESSAGE = HALO + 8 * CY + 16


def iota(shape, dim):
    return lax.broadcasted_iota(jnp.int32, shape, dim)


def pack_kernel(
    vectors_hbm, kappa_hbm, out_ref, kappa_ref, vectors, sems
):
    pairs = ((vectors_hbm, vectors), (kappa_hbm, kappa_ref))
    copies = [pltpu.make_async_copy(a, b, sems.at[i]) for i, (a, b) in enumerate(pairs)]
    for copy in copies:
        copy.start()
    copies[0].wait()
    for s in range(ROWS):
        out_ref[s, :, 0:PTS] = vectors[...]
    copies[1].wait()
    rows = [kappa_ref[q // CY, q % CY : q % CY + 1, :] for q in range(CX * CY)]
    half = CX * CY // NVEC
    for q in range(half):
        pair = jnp.concatenate([rows[q], rows[half + q]], axis=0).astype(BF16)
        for s in range(ROWS):
            out_ref[s, :, PTS + q * NZ : PTS + (q + 1) * NZ] = pair


def slots_kernel(
    perm_hbm, tile_hbm, right_hbm, perm_ref, tile_ref, rank_ref, place_ref, right, sems
):
    pairs = ((perm_hbm, perm_ref), (tile_hbm, tile_ref), (right_hbm, right))
    copies = [pltpu.make_async_copy(a, b, sems.at[i]) for i, (a, b) in enumerate(pairs)]
    for copy in copies:
        copy.start()
    copies[0].wait()
    chunk = 256
    upto = jnp.where(iota((chunk, chunk), 0) <= iota((chunk, chunk), 1), 1.0, 0.0).astype(BF16)
    brick = iota((DEV, chunk), 0)
    carry = jnp.zeros((COLS * DEV, 1), F32)
    for j in range(PTS // chunk):
        lanes = [slice(k * PTS + j * chunk, k * PTS + (j + 1) * chunk) for k in range(COLS)]
        masks = [(perm_ref[0:1, at] >> 11) == brick for at in lanes]
        hot = jnp.concatenate([jnp.where(m, 1.0, 0.0).astype(BF16) for m in masks], axis=0)
        total = jnp.dot(hot, upto, preferred_element_type=F32) + carry
        for k in range(COLS):
            at = jnp.where(masks[k], total[k * DEV : (k + 1) * DEV], 0.0)
            rank_ref[0:1, lanes[k]] = jnp.sum(at, axis=0, keepdims=True) - 1.0
        carry = total[:, chunk - 1 : chunk]
    col = lax.axis_index("col")
    start = pl.multiple_of(col * PTS, PTS)
    own = perm_ref[0:1, pl.ds(start, PTS)]
    slot = rank_ref[0:1, pl.ds(start, PTS)] + ((col % 4) * CAP).astype(F32)
    here = jnp.where(slot == iota((128, PTS), 0).astype(F32), 1.0, 0.0).astype(BF16)
    hot = jnp.where((own >> 11) == iota((DEV, PTS), 0), 1.0, 0.0).astype(BF16)
    inside = own & (PTS - 1)
    place = jnp.zeros((DEV, 128), F32)
    for part in (inside & ~(NZ - 1), (inside & (NZ - 1)) + 1):
        spread = here * part.astype(F32).astype(BF16)
        place = place + lax.dot_general(hot, spread, NT, preferred_element_type=F32)
    place_ref[...] = place.astype(jnp.int32)
    copies[1].wait()
    copies[2].wait()


def level_of(values):
    largest = jnp.max(jnp.abs(values), axis=0, keepdims=True)
    largest = jnp.broadcast_to(jnp.max(largest, axis=1, keepdims=True), (8, 128))
    level = jnp.ceil(jnp.maximum(jnp.log2(largest), -100.0) * LEVELS)
    return level[0:1], (STEPS * jnp.exp2(level * (-1.0 / LEVELS)))[0:1]


def step_at(level):
    return jnp.exp2(level * (1.0 / LEVELS)) * (1.0 / STEPS)


def send_kernel(
    leaf_at_hbm,
    left_hbm,
    leaf_hbm,
    x_ref,
    tile_rank_ref,
    perm_ref,
    rank_ref,
    place_ref,
    right,
    out_ref,
    left,
    leaves,
    x_rows,
    sums,
    leaf_at,
    sems,
):
    pairs = [(leaf_at_hbm, leaf_at)]
    wide = TS // PIECES
    for i in range(PIECES):
        at = pl.ds(i * wide, wide)
        pairs.append((left_hbm.at[:, at], left.at[:, at]))
    for first, last in LEAF_PIECES:
        at = pl.ds(first, last - first)
        pairs.append((leaf_hbm.at[at], leaves.at[at]))
    copies = [pltpu.make_async_copy(a, b, sems.at[i]) for i, (a, b) in enumerate(pairs)]
    for copy in copies:
        copy.start()

    def beside(values):
        none = jnp.zeros((COLS, 128), jnp.int32)
        last = DEV - COLS
        return [
            jnp.concatenate([none, values[:last]], axis=0),
            values,
            jnp.concatenate([values[COLS:], none], axis=0),
        ]

    def pack(low, high):
        return (high << 16) | (low & 0xFFFF)

    half = TS // PTS
    for s in range(ROWS):
        b, h = divmod(s, half)
        block = x_ref[s, :, 0:PTS].astype(F32)
        x_rows[b : b + 1, h * PTS : (h + 1) * PTS] = block[0:1]
        x_rows[8 + b : 9 + b, h * PTS : (h + 1) * PTS] = block[1:2]
    terms = TILE_ROWS * TILE_COLS * KMAX
    lane = iota((16, terms), 1)
    sub = iota((16, terms), 0)
    widen = jnp.where(
        iota((TILE_ROWS * TILE_COLS, terms), 1) // KMAX
        == iota((TILE_ROWS * TILE_COLS, terms), 0),
        1.0,
        0.0,
    ).astype(BF16)
    ranks = jnp.broadcast_to(tile_rank_ref[...].astype(F32), (16, TILE_ROWS * TILE_COLS))
    rank_lane = jnp.dot(ranks.astype(BF16), widen, preferred_element_type=F32)
    keep = (sub % 8 == (lane // KMAX) % TILE_COLS) & ((lane % KMAX).astype(F32) < rank_lane)
    x_all = x_rows[...].astype(BF16)
    projected = lax.dot_general(x_all, right[...], NT, preferred_element_type=F32)
    projected = jnp.where(keep, projected, 0.0)
    first = jnp.sum(projected[0:8], axis=0, keepdims=True)
    second = jnp.sum(projected[8:16], axis=0, keepdims=True)
    by_row = jnp.where(sub < 8, first, second)
    by_row = jnp.where(sub % 8 == lane // (TILE_COLS * KMAX), by_row, 0.0).astype(BF16)
    for i in range(PIECES):
        copies[1 + i].wait()
        at = (slice(None), slice(i * wide, (i + 1) * wide))
        sums[at] = jnp.dot(by_row, left[at], preferred_element_type=F32)
    copies[0].wait()
    per_tile = TS // LEAF
    for l in range(NLEAF):
        for n, (first, _) in enumerate(LEAF_PIECES):
            if l == first:
                copies[1 + PIECES + n].wait()
        i, j = leaf_at[0, l], leaf_at[1, l]
        from_lane = pl.multiple_of((j % per_tile) * LEAF, LEAF)
        to_lane = pl.multiple_of((i % per_tile) * LEAF, LEAF)
        picked = jnp.concatenate(
            [x_rows[pl.ds(8 * v + j // per_tile, 1), pl.ds(from_lane, LEAF)] for v in range(NVEC)],
            axis=0,
        ).astype(BF16)
        near = lax.dot_general(picked, leaves[l], NT, preferred_element_type=F32)
        for v in range(NVEC):
            at = (pl.ds(8 * v + i // per_tile, 1), pl.ds(to_lane, LEAF))
            sums[at] = sums[at] + near[v : v + 1]
    places = beside(place_ref[...])
    level, inverse = level_of(sums[...])
    out_ref[pl.ds(6, DEV, stride=SLAB), :] = pack(places[0], places[1])
    out_ref[pl.ds(7, DEV, stride=SLAB), :] = pack(
        places[2], jnp.broadcast_to(level.astype(jnp.int32), (DEV, 128))
    )
    one, none = jnp.ones((), BF16), jnp.zeros((), BF16)

    def numbers(count):
        return iota((count, PTS), 0).astype(F32).astype(BF16)

    for group in range(2):
        parts = []
        for kk in range(4):
            k = group * 4 + kk
            a, h = divmod(k, half)
            at = slice(k * PTS, (k + 1) * PTS)
            slot = rank_ref[0:1, at].astype(BF16) == numbers(CAP)
            slot = jnp.where(slot, one, none)
            rows = [sums[8 * v + a : 8 * v + a + 1, h * PTS : (h + 1) * PTS] for v in range(NVEC)]
            highs = [row.astype(BF16) for row in rows]
            lows = [(row - high.astype(F32)).astype(BF16) for row, high in zip(rows, highs)]
            spread = jnp.concatenate([slot * row for row in highs + lows], axis=0)
            hot = (perm_ref[0:1, at] >> 11).astype(F32).astype(BF16) == numbers(DEV)
            hot = jnp.where(hot, one, none)
            part = lax.dot_general(hot, spread, NT, preferred_element_type=F32)
            parts.append(part + pltpu.roll(part, NVEC * CAP, 1))
        words = pack(
            *(
                jnp.round(
                    jnp.concatenate([p[:, v * CAP : (v + 1) * CAP] for p in parts], axis=1) * inverse
                ).astype(jnp.int32)
                for v in range(NVEC)
            )
        )
        for j, moved in enumerate(beside(words)):
            out_ref[pl.ds(j * 2 + group, DEV, stride=SLAB), :] = moved


def bricks_kernel(
    got_ref, packed_ref, kappa_ref, out_ref, halo_ref, sums, wheres, at_cells
):
    valued = iota((SLAB, 128), 0) < 6
    for r in range(ROWS):
        at = slice(r * SLAB, (r + 1) * SLAB)
        halves = []
        for g in range(2):
            totals = [None, None]
            for c in range(4):
                start = ((r * 2 + g) * 4 + c) * SLAB
                words = got_ref[start : start + SLAB, :]
                pair = [((words << 16) >> 16).astype(F32), (words >> 16).astype(F32)]
                size = jnp.where(valued, step_at(pair[1][7:8]), 1.0)
                pair = [one * size for one in pair]
                totals = [b if a is None else a + b for a, b in zip(totals, pair)]
            for v in range(NVEC):
                wheres[v, g, at, :] = totals[v]
            halves.append(totals)
        for v in range(NVEC):
            sums[v, at, :] = halves[0][v] + halves[1][v]
    for v in range(NVEC):
        for g in range(2):
            place = wheres[v, g] - 1.0
            cell = jnp.floor(place * (1.0 / NZ))
            at_cells[v, g] = cell
            wheres[v, g] = place - cell * NZ
    sub = iota((8, 128), 0)
    z_row = iota((NZ, 128), 0).astype(F32).astype(BF16)
    one, none = jnp.ones((), BF16), jnp.zeros((), BF16)
    for j in range(3):
        both = jnp.zeros((64, NZ), F32)
        for some in range(0, ROWS, 4):
            cells, heights = [], []
            for r, g in ((r, g) for r in range(some, some + 4) for g in range(2)):
                at = r * SLAB + j * 2 + g
                pair = jnp.where(sub < 4, sums[0, at : at + 1, :], sums[1, at : at + 1, :])
                high = pair.astype(BF16).astype(F32)
                low = pair - high
                v, p = j % 2, r * SLAB + 6 + j // 2
                cell = at_cells[v, g, p : p + 1, :]
                wanted = [cell == (x * CY + sub % CY).astype(F32) for x in range(CX)]
                rows = [jnp.where(w, part, 0.0) for part in (high, low) for w in wanted]
                cells.append(jnp.concatenate(rows, axis=0).astype(BF16))
                z_at = wheres[v, g, p : p + 1, :].astype(BF16)
                heights.append(jnp.where(z_at == z_row, one, none))
            both = both + lax.dot_general(
                jnp.concatenate(cells, axis=1),
                jnp.concatenate(heights, axis=1),
                NT,
                preferred_element_type=F32,
            )
        out_ref[j * 32 : (j + 1) * 32, :] = both[0:32] + both[32:64]
    my_row = lax.axis_index("row")
    half = CX * CY // NVEC
    for j, r in ((0, jnp.maximum(my_row - 1, 0)), (2, jnp.minimum(my_row + 1, ROWS - 1))):
        block = packed_ref[r, :, PTS:].astype(F32)
        for q in range(half):
            for v in range(NVEC):
                at = FIELD + j * CX * CY + v * half + q
                out_ref[at : at + 1, :] = block[v : v + 1, q * NZ : (q + 1) * NZ]
    for x in range(CX):
        at = FIELD + CX * CY + x * CY
        out_ref[at : at + CY, :] = kappa_ref[x]
    level, inverse = level_of(out_ref[0:FIELD, :])

    def store(at, values):
        halo_ref[at : at + values.shape[0], :] = (
            jnp.round(values).astype(jnp.int32).astype(jnp.int16)
        )

    store(0, out_ref[8 : FIELD - 8, :] * inverse)
    store(HALO, out_ref[FIELD + 2 * CY : FIELD + 10 * CY, :] * KAPPA_STEPS)
    store(HALO + 8 * CY, jnp.broadcast_to(level, (16, 128)))


def prior_kernel(own_ref, even_ref, odd_ref, out_ref):
    my_row, my_col = lax.axis_index("row"), lax.axis_index("col")
    wide = 3 * CX
    inside_x = [
        jnp.where(my_row > 0, 1.0, 0.0),
        jnp.float32(1.0),
        jnp.where(my_row < ROWS - 1, 1.0, 0.0),
    ]
    inside_y = [
        jnp.where(my_col > 0, 1.0, 0.0),
        jnp.float32(1.0),
        jnp.where(my_col < COLS - 1, 1.0, 0.0),
    ]
    y_at = iota((8, NZ), 0) % CY
    z_at = iota((8, NZ), 1)
    none = jnp.zeros((8, NZ), F32)
    us, ks = [], []
    even, odd = (ref[...].astype(jnp.int32).astype(F32) for ref in (even_ref, odd_ref))
    at_even = jnp.broadcast_to(my_col % 2, (MESSAGE, NZ)) == 0
    before, after = jnp.where(at_even, odd, even), jnp.where(at_even, even, odd)
    for b, got in enumerate((before, None, after)):
        if got is None:
            field = [own_ref[8 * x : 8 * x + 8, :] for x in range(wide)]
            rows = [own_ref[FIELD + CY * x : FIELD + CY * (x + 1), :] for x in range(wide)]
            kappas = [6.0 + jnp.concatenate([row, row], axis=0) for row in rows]
        else:
            values = got[0:HALO] * (step_at(got[HALO + 8 * CY : HALO + 8 * CY + 1]) * inside_y[b])
            field = [values[8 * x : 8 * x + 8] for x in range(wide - 2)]
            field = [none] + field + [none]
            values = got[HALO : HALO + 8 * CY] * (1.0 / KAPPA_STEPS) + 6.0
            rows = [values[CY * x : CY * (x + 1)] for x in range(8)]
            kappas = [none] * 2 + [jnp.concatenate([row, row], axis=0) for row in rows] + [none] * 2
        us.append(field)
        ks.append(kappas)
    for step in range(1, 5):
        new = [[None] * wide for _ in range(3)]
        for b in range(3):
            if step == 4 and b != 1:
                continue
            edge = step if b == 1 else step + 1
            for x in range(edge, wide - edge):
                u = us[b][x]
                lower = pltpu.roll(us[b - 1][x], 5, 0) if b > 0 and us[b - 1][x] is not None else 0.0
                upper = pltpu.roll(us[b + 1][x], 3, 0) if b < 2 and us[b + 1][x] is not None else 0.0
                beside = us[b][x - 1] + us[b][x + 1]
                beside = beside + jnp.where(y_at == 0, lower, pltpu.roll(u, 1, 0))
                beside = beside + jnp.where(y_at == CY - 1, upper, pltpu.roll(u, 7, 0))
                beside = beside + jnp.where(z_at == 0, 0.0, pltpu.roll(u, 1, 1))
                beside = beside + jnp.where(z_at == NZ - 1, 0.0, pltpu.roll(u, NZ - 1, 1))
                result = (ks[b][x] * u - beside) * 0.125
                if step < 4:
                    if b != 1 and x // CX != 1:
                        result = result * (inside_y[b] * inside_x[x // CX])
                    elif b != 1:
                        result = result * inside_y[b]
                    elif x // CX != 1:
                        result = result * inside_x[x // CX]
                new[b][x] = result
        us = new
    for x in range(CX):
        for v in range(NVEC):
            out_ref[v, x] = us[1][CX + x][v * CY : (v + 1) * CY]


def swapped(array, axis, first):
    pairs = [(i, i + 1) for i in range(first, lax.axis_size(axis) - 1, 2)]
    return lax.ppermute(array, axis, pairs + [(b, a) for a, b in pairs])


def cost(flops, size):
    return pl.CostEstimate(flops=flops, bytes_accessed=size, transcendentals=0)


def in_hbm(*arrays):
    return [pltpu.with_memory_space_constraint(a, pltpu.HBM) for a in arrays]


def in_vmem(*arrays):
    return [pltpu.with_memory_space_constraint(a, pltpu.VMEM) for a in arrays]


def params(mib):
    return pltpu.CompilerParams(vmem_limit_bytes=mib * MIB)


def per_device(
    vectors, lr_left, lr_right, tile_rank, leaf_values, leaf_places, cluster_perm, kappa
):
    vmem = pl.BlockSpec(memory_space=pltpu.VMEM)
    hbm = pl.BlockSpec(memory_space=pltpu.HBM)
    points = COLS * PTS
    terms = TILE_ROWS * TILE_COLS * KMAX
    packed_shape = (ROWS, NVEC, PTS + PTS // NVEC)
    packed, kappa_own = pl.pallas_call(
        pack_kernel,
        out_shape=(
            pltpu.VMEM(packed_shape, BF16),
            pltpu.VMEM((CX, CY, NZ), F32),
        ),
        in_specs=[hbm] * 2,
        out_specs=(vmem,) * 2,
        scratch_shapes=[pltpu.VMEM((NVEC, PTS), BF16), pltpu.SemaphoreType.DMA((2,))],
        compiler_params=params(8),
        name="pack",
    )(*in_hbm(vectors[:, 0], kappa))
    packed = lax.all_to_all(packed, "row", 0, 0, tiled=True)
    perm, ranks, rank, place, right = pl.pallas_call(
        slots_kernel,
        out_shape=(
            pltpu.VMEM((1, points), jnp.int32),
            pltpu.VMEM((1, TILE_ROWS * TILE_COLS), jnp.int32),
            pltpu.VMEM((1, points), F32),
            pltpu.VMEM((DEV, 128), jnp.int32),
            pltpu.VMEM((terms, TS), BF16),
        ),
        in_specs=[hbm] * 3,
        out_specs=(vmem,) * 5,
        scratch_shapes=[pltpu.SemaphoreType.DMA((3,))],
        compiler_params=params(16),
        cost_estimate=cost(1 << 31, 1 << 20),
        name="slots",
    )(*in_hbm(cluster_perm, tile_rank[0], lr_right.reshape(terms, TS)))
    send = pl.pallas_call(
        send_kernel,
        out_shape=jax.ShapeDtypeStruct((DEV * SLAB, 128), jnp.int32),
        in_specs=[hbm] * 3 + [vmem] * 6,
        out_specs=vmem,
        scratch_shapes=[
            pltpu.VMEM((terms, TS), BF16),
            pltpu.VMEM((NLEAF, LEAF, LEAF), BF16),
            pltpu.VMEM((16, TS), F32),
            pltpu.VMEM((16, TS), F32),
            pltpu.SMEM((2, NLEAF), jnp.int32),
            pltpu.SemaphoreType.DMA((1 + PIECES + len(LEAF_PIECES),)),
        ],
        compiler_params=params(32),
        cost_estimate=cost(1 << 31, 8 << 20),
        name="partial_sums",
    )(
        *in_hbm(leaf_places[0, 0].T, lr_left.reshape(terms, TS), leaf_values[0, 0]),
        *in_vmem(packed, ranks, perm, rank, place, right),
    )
    got = lax.all_to_all(send.reshape(DEV, SLAB, 128), ("row", "col"), 0, 0, tiled=True)
    own, halo = pl.pallas_call(
        bricks_kernel,
        out_shape=(
            pltpu.VMEM((FIELD + 3 * CX * CY, NZ), F32),
            pltpu.VMEM((MESSAGE, NZ), jnp.int16),
        ),
        in_specs=[vmem] * 3,
        out_specs=(vmem,) * 2,
        scratch_shapes=[
            pltpu.VMEM((NVEC, ROWS * SLAB, 128), F32),
            pltpu.VMEM((NVEC, 2, ROWS * SLAB, 128), F32),
            pltpu.VMEM((NVEC, 2, ROWS * SLAB, 128), F32),
        ],
        compiler_params=params(16),
        cost_estimate=cost(1 << 30, 1 << 20),
        name="bricks",
    )(got.reshape(DEV * SLAB, 128), packed, kappa_own)
    odd = swapped(halo, "col", 1)
    even = swapped(halo, "col", 0)
    return pl.pallas_call(
        prior_kernel,
        out_shape=jax.ShapeDtypeStruct((NVEC, CX, CY, NZ), F32),
        in_specs=[vmem] * 3,
        out_specs=vmem,
        compiler_params=params(8),
        cost_estimate=cost(1 << 24, 1 << 20),
        name="prior",
    )(own, even, odd)


def solution(mesh):
    in_specs = (
        P(None, "col", "row"),
        P("row", "col", None, None, None),
        P("row", "col", None, None, None),
        P("row", "col", None),
        P("row", "col", None, None, None),
        P("row", "col", None, None),
        P("row", None),
        P("row", "col", None),
    )
    out_specs = P(None, "row", "col", None)
    return jax.shard_map(
        per_device, mesh=mesh, in_specs=in_specs, out_specs=out_specs, check_vma=False
    )
```

```python
import jax
import jax.numpy as jnp
from jax import lax
from jax.experimental import pallas as pl
from jax.experimental.pallas import tpu as pltpu
from jax.sharding import PartitionSpec as P

NVEC = 2
CX = 4
CY = 4
NZ = 128
TILE_ROWS = 4
TILE_COLS = 8
KMAX = 8
LEAF = 512
NLEAF = 8
PTS = 2048
ROWS = 16
COLS = 8
TS = 4096
CAP = 32
DEV = ROWS * COLS
PIECES = 2
LEAF_PIECES = ((0, 2), (2, 4), (4, 6), (6, 8))
SLAB = 7
F32 = jnp.float32
BF16 = jnp.bfloat16
NT = (((1,), (1,)), ((), ()))
MIB = 1 << 20
LEVELS = 64.0
STEPS = 32000.0
KAPPA_STEPS = 8000.0
FIELD = 3 * CX * NVEC * CY
HALO = FIELD - 2 * NVEC * CY
MESSAGE = HALO + 8 * CY + 16


def iota(shape, dim):
    return lax.broadcasted_iota(jnp.int32, shape, dim)


def pack_kernel(
    vectors_hbm, kappa_hbm, out_ref, kappa_ref, vectors, sems
):
    pairs = ((vectors_hbm, vectors), (kappa_hbm, kappa_ref))
    copies = [pltpu.make_async_copy(a, b, sems.at[i]) for i, (a, b) in enumerate(pairs)]
    for copy in copies:
        copy.start()
    copies[0].wait()
    for s in range(ROWS):
        out_ref[s, :, 0:PTS] = vectors[...]
    copies[1].wait()
    rows = [kappa_ref[q // CY, q % CY : q % CY + 1, :] for q in range(CX * CY)]
    half = CX * CY // NVEC
    for q in range(half):
        pair = jnp.concatenate([rows[q], rows[half + q]], axis=0).astype(BF16)
        for s in range(ROWS):
            out_ref[s, :, PTS + q * NZ : PTS + (q + 1) * NZ] = pair


def beside(values):
    none = jnp.zeros((COLS, values.shape[1]), jnp.int32)
    last = DEV - COLS
    return [
        jnp.concatenate([none, values[:last]], axis=0),
        values,
        jnp.concatenate([values[COLS:], none], axis=0),
    ]


def slots_kernel(
    perm_hbm, tile_hbm, right_hbm, perm_ref, tile_ref, rank_ref, place_ref, right, sems
):
    pairs = ((perm_hbm, perm_ref), (tile_hbm, tile_ref), (right_hbm, right))
    copies = [pltpu.make_async_copy(a, b, sems.at[i]) for i, (a, b) in enumerate(pairs)]
    for copy in copies:
        copy.start()
    copies[0].wait()
    chunk = 256
    upto = jnp.where(iota((chunk, chunk), 0) <= iota((chunk, chunk), 1), 1.0, 0.0).astype(BF16)
    brick = iota((DEV, chunk), 0)
    carry = jnp.zeros((COLS * DEV, 1), F32)
    for j in range(PTS // chunk):
        lanes = [slice(k * PTS + j * chunk, k * PTS + (j + 1) * chunk) for k in range(COLS)]
        masks = [(perm_ref[0:1, at] >> 11) == brick for at in lanes]
        hot = jnp.concatenate([jnp.where(m, 1.0, 0.0).astype(BF16) for m in masks], axis=0)
        total = jnp.dot(hot, upto, preferred_element_type=F32) + carry
        for k in range(COLS):
            at = jnp.where(masks[k], total[k * DEV : (k + 1) * DEV], 0.0)
            rank_ref[0:1, lanes[k]] = jnp.sum(at, axis=0, keepdims=True) - 1.0
        carry = total[:, chunk - 1 : chunk]
    col = lax.axis_index("col")
    start = pl.multiple_of(col * PTS, PTS)
    own = perm_ref[0:1, pl.ds(start, PTS)]
    slot = rank_ref[0:1, pl.ds(start, PTS)]
    here = jnp.where(slot == iota((CAP, PTS), 0).astype(F32), 1.0, 0.0).astype(BF16)
    hot = jnp.where((own >> 11) == iota((DEV, PTS), 0), 1.0, 0.0).astype(BF16)
    inside = own & (PTS - 1)
    place = jnp.zeros((DEV, CAP), F32)
    for part in (inside & ~(NZ - 1), (inside & (NZ - 1)) + 1):
        spread = here * part.astype(F32).astype(BF16)
        place = place + lax.dot_general(hot, spread, NT, preferred_element_type=F32)
    place = place.astype(jnp.int32)
    place_ref[...] = jnp.concatenate(beside(place) + [jnp.zeros((DEV, CAP), jnp.int32)], axis=1)
    copies[1].wait()
    copies[2].wait()


def level_of(values):
    largest = jnp.max(jnp.abs(values), axis=0, keepdims=True)
    largest = jnp.broadcast_to(jnp.max(largest, axis=1, keepdims=True), (8, 128))
    level = jnp.ceil(jnp.maximum(jnp.log2(largest), -100.0) * LEVELS)
    return level[0:1], (STEPS * jnp.exp2(level * (-1.0 / LEVELS)))[0:1]


def step_at(level):
    return jnp.exp2(level * (1.0 / LEVELS)) * (1.0 / STEPS)


def send_kernel(
    leaf_at_hbm,
    left_hbm,
    leaf_hbm,
    x_ref,
    tile_rank_ref,
    perm_ref,
    rank_ref,
    place_ref,
    right,
    out_ref,
    left,
    leaves,
    x_rows,
    sums,
    leaf_at,
    sems,
):
    pairs = [(leaf_at_hbm, leaf_at)]
    wide = TS // PIECES
    for i in range(PIECES):
        at = pl.ds(i * wide, wide)
        pairs.append((left_hbm.at[:, at], left.at[:, at]))
    for first, last in LEAF_PIECES:
        at = pl.ds(first, last - first)
        pairs.append((leaf_hbm.at[at], leaves.at[at]))
    copies = [pltpu.make_async_copy(a, b, sems.at[i]) for i, (a, b) in enumerate(pairs)]
    for copy in copies:
        copy.start()

    def pack(low, high):
        return (high << 16) | (low & 0xFFFF)

    half = TS // PTS
    for s in range(ROWS):
        b, h = divmod(s, half)
        block = x_ref[s, :, 0:PTS].astype(F32)
        x_rows[b : b + 1, h * PTS : (h + 1) * PTS] = block[0:1]
        x_rows[8 + b : 9 + b, h * PTS : (h + 1) * PTS] = block[1:2]
    terms = TILE_ROWS * TILE_COLS * KMAX
    lane = iota((16, terms), 1)
    sub = iota((16, terms), 0)
    widen = jnp.where(
        iota((TILE_ROWS * TILE_COLS, terms), 1) // KMAX
        == iota((TILE_ROWS * TILE_COLS, terms), 0),
        1.0,
        0.0,
    ).astype(BF16)
    ranks = jnp.broadcast_to(tile_rank_ref[...].astype(F32), (16, TILE_ROWS * TILE_COLS))
    rank_lane = jnp.dot(ranks.astype(BF16), widen, preferred_element_type=F32)
    keep = (sub % 8 == (lane // KMAX) % TILE_COLS) & ((lane % KMAX).astype(F32) < rank_lane)
    x_all = x_rows[...].astype(BF16)
    projected = lax.dot_general(x_all, right[...], NT, preferred_element_type=F32)
    projected = jnp.where(keep, projected, 0.0)
    first = jnp.sum(projected[0:8], axis=0, keepdims=True)
    second = jnp.sum(projected[8:16], axis=0, keepdims=True)
    by_row = jnp.where(sub < 8, first, second)
    by_row = jnp.where(sub % 8 == lane // (TILE_COLS * KMAX), by_row, 0.0).astype(BF16)
    for i in range(PIECES):
        copies[1 + i].wait()
        at = (slice(None), slice(i * wide, (i + 1) * wide))
        sums[at] = jnp.dot(by_row, left[at], preferred_element_type=F32)
    copies[0].wait()
    per_tile = TS // LEAF
    for l in range(NLEAF):
        for n, (first, _) in enumerate(LEAF_PIECES):
            if l == first:
                copies[1 + PIECES + n].wait()
        i, j = leaf_at[0, l], leaf_at[1, l]
        from_lane = pl.multiple_of((j % per_tile) * LEAF, LEAF)
        to_lane = pl.multiple_of((i % per_tile) * LEAF, LEAF)
        picked = jnp.concatenate(
            [x_rows[pl.ds(8 * v + j // per_tile, 1), pl.ds(from_lane, LEAF)] for v in range(NVEC)],
            axis=0,
        ).astype(BF16)
        near = lax.dot_general(picked, leaves[l], NT, preferred_element_type=F32)
        for v in range(NVEC):
            at = (pl.ds(8 * v + i // per_tile, 1), pl.ds(to_lane, LEAF))
            sums[at] = sums[at] + near[v : v + 1]
    level, inverse = level_of(sums[...])
    out_ref[pl.ds(6, DEV, stride=SLAB), :] = jnp.where(
        iota((DEV, 128), 1) < 3 * CAP, place_ref[...], level.astype(jnp.int32)
    )
    one, none = jnp.ones((), BF16), jnp.zeros((), BF16)

    def numbers(count):
        return iota((count, PTS), 0).astype(F32).astype(BF16)

    for group in range(2):
        parts = []
        for kk in range(4):
            k = group * 4 + kk
            a, h = divmod(k, half)
            at = slice(k * PTS, (k + 1) * PTS)
            slot = rank_ref[0:1, at].astype(BF16) == numbers(CAP)
            slot = jnp.where(slot, one, none)
            rows = [sums[8 * v + a : 8 * v + a + 1, h * PTS : (h + 1) * PTS] for v in range(NVEC)]
            highs = [row.astype(BF16) for row in rows]
            lows = [(row - high.astype(F32)).astype(BF16) for row, high in zip(rows, highs)]
            spread = jnp.concatenate([slot * row for row in highs + lows], axis=0)
            hot = (perm_ref[0:1, at] >> 11).astype(F32).astype(BF16) == numbers(DEV)
            hot = jnp.where(hot, one, none)
            part = lax.dot_general(hot, spread, NT, preferred_element_type=F32)
            parts.append(part + pltpu.roll(part, NVEC * CAP, 1))
        words = pack(
            *(
                jnp.round(
                    jnp.concatenate([p[:, v * CAP : (v + 1) * CAP] for p in parts], axis=1) * inverse
                ).astype(jnp.int32)
                for v in range(NVEC)
            )
        )
        for j, moved in enumerate(beside(words)):
            out_ref[pl.ds(j * 2 + group, DEV, stride=SLAB), :] = moved


def bricks_kernel(
    got_ref, packed_ref, kappa_ref, out_ref, halo_ref, sums, wheres, at_cells
):
    def of_all_rows(c, q):
        return got_ref[pl.ds(c * SLAB + q, ROWS, stride=COLS * SLAB), :]

    last = [of_all_rows(c, 6).astype(F32) for c in range(COLS)]
    sizes = [
        step_at(jnp.broadcast_to(one[:, 3 * CAP : 3 * CAP + 1], (ROWS, 128))) for one in last
    ]
    for q in range(6):
        totals = [jnp.zeros((ROWS, 128), F32)] * NVEC
        for c in range(COLS):
            words = of_all_rows(c, q)
            pair = ((words << 16) >> 16, words >> 16)
            totals = [t + w.astype(F32) * sizes[c] for t, w in zip(totals, pair)]
        for v in range(NVEC):
            sums[v, q * ROWS : (q + 1) * ROWS, :] = totals[v]
    part = iota((ROWS, 128), 1) // CAP
    for g in range(2):
        for j in range(3):
            place = jnp.full((ROWS, 128), -1.0, F32)
            for kk in range(4):
                moved = pltpu.roll(last[g * 4 + kk], (kk - j) * CAP % 128, 1)
                place = place + jnp.where(part == kk, moved, 0.0)
            cell = jnp.floor(place * (1.0 / NZ))
            at_cells[g, j * ROWS : (j + 1) * ROWS, :] = cell
            wheres[g, j * ROWS : (j + 1) * ROWS, :] = place - cell * NZ
    sub = iota((8, 128), 0)
    z_row = iota((NZ, 128), 0).astype(F32).astype(BF16)
    one, none = jnp.ones((), BF16), jnp.zeros((), BF16)
    for j in range(3):
        both = jnp.zeros((64, NZ), F32)
        for some in range(0, ROWS, 4):
            cells, heights = [], []
            for r, g in ((r, g) for r in range(some, some + 4) for g in range(2)):
                at = (j * 2 + g) * ROWS + r
                pair = jnp.where(sub < 4, sums[0, at : at + 1, :], sums[1, at : at + 1, :])
                high = pair.astype(BF16).astype(F32)
                low = pair - high
                p = j * ROWS + r
                cell = at_cells[g, p : p + 1, :]
                wanted = [cell == (x * CY + sub % CY).astype(F32) for x in range(CX)]
                rows = [jnp.where(w, part, 0.0) for part in (high, low) for w in wanted]
                cells.append(jnp.concatenate(rows, axis=0).astype(BF16))
                z_at = wheres[g, p : p + 1, :].astype(BF16)
                heights.append(jnp.where(z_at == z_row, one, none))
            both = both + lax.dot_general(
                jnp.concatenate(cells, axis=1),
                jnp.concatenate(heights, axis=1),
                NT,
                preferred_element_type=F32,
            )
        out_ref[j * 32 : (j + 1) * 32, :] = both[0:32] + both[32:64]
    my_row = lax.axis_index("row")
    half = CX * CY // NVEC
    for j, r in ((0, jnp.maximum(my_row - 1, 0)), (2, jnp.minimum(my_row + 1, ROWS - 1))):
        block = packed_ref[r, :, PTS:].astype(F32)
        for q in range(half):
            for v in range(NVEC):
                at = FIELD + j * CX * CY + v * half + q
                out_ref[at : at + 1, :] = block[v : v + 1, q * NZ : (q + 1) * NZ]
    for x in range(CX):
        at = FIELD + CX * CY + x * CY
        out_ref[at : at + CY, :] = kappa_ref[x]
    level, inverse = level_of(out_ref[0:FIELD, :])

    def store(at, values):
        halo_ref[at : at + values.shape[0], :] = (
            jnp.round(values).astype(jnp.int32).astype(jnp.int16)
        )

    store(0, out_ref[8 : FIELD - 8, :] * inverse)
    store(HALO, out_ref[FIELD + 2 * CY : FIELD + 10 * CY, :] * KAPPA_STEPS)
    store(HALO + 8 * CY, jnp.broadcast_to(level, (16, 128)))


def prior_kernel(own_ref, even_ref, odd_ref, out_ref):
    my_row, my_col = lax.axis_index("row"), lax.axis_index("col")
    wide = 3 * CX
    inside_x = [
        jnp.where(my_row > 0, 1.0, 0.0),
        jnp.float32(1.0),
        jnp.where(my_row < ROWS - 1, 1.0, 0.0),
    ]
    inside_y = [
        jnp.where(my_col > 0, 1.0, 0.0),
        jnp.float32(1.0),
        jnp.where(my_col < COLS - 1, 1.0, 0.0),
    ]
    y_at = iota((8, NZ), 0) % CY
    z_at = iota((8, NZ), 1)
    none = jnp.zeros((8, NZ), F32)
    us, ks = [], []
    even, odd = (ref[...].astype(jnp.int32).astype(F32) for ref in (even_ref, odd_ref))
    at_even = jnp.broadcast_to(my_col % 2, (MESSAGE, NZ)) == 0
    before, after = jnp.where(at_even, odd, even), jnp.where(at_even, even, odd)
    for b, got in enumerate((before, None, after)):
        if got is None:
            field = [own_ref[8 * x : 8 * x + 8, :] for x in range(wide)]
            rows = [own_ref[FIELD + CY * x : FIELD + CY * (x + 1), :] for x in range(wide)]
            kappas = [6.0 + jnp.concatenate([row, row], axis=0) for row in rows]
        else:
            values = got[0:HALO] * (step_at(got[HALO + 8 * CY : HALO + 8 * CY + 1]) * inside_y[b])
            field = [values[8 * x : 8 * x + 8] for x in range(wide - 2)]
            field = [none] + field + [none]
            values = got[HALO : HALO + 8 * CY] * (1.0 / KAPPA_STEPS) + 6.0
            rows = [values[CY * x : CY * (x + 1)] for x in range(8)]
            kappas = [none] * 2 + [jnp.concatenate([row, row], axis=0) for row in rows] + [none] * 2
        us.append(field)
        ks.append(kappas)
    for step in range(1, 5):
        new = [[None] * wide for _ in range(3)]
        for b in range(3):
            if step == 4 and b != 1:
                continue
            edge = step if b == 1 else step + 1
            for x in range(edge, wide - edge):
                u = us[b][x]
                lower = pltpu.roll(us[b - 1][x], 5, 0) if b > 0 and us[b - 1][x] is not None else 0.0
                upper = pltpu.roll(us[b + 1][x], 3, 0) if b < 2 and us[b + 1][x] is not None else 0.0
                beside = us[b][x - 1] + us[b][x + 1]
                beside = beside + jnp.where(y_at == 0, lower, pltpu.roll(u, 1, 0))
                beside = beside + jnp.where(y_at == CY - 1, upper, pltpu.roll(u, 7, 0))
                beside = beside + jnp.where(z_at == 0, 0.0, pltpu.roll(u, 1, 1))
                beside = beside + jnp.where(z_at == NZ - 1, 0.0, pltpu.roll(u, NZ - 1, 1))
                result = (ks[b][x] * u - beside) * 0.125
                if step < 4:
                    if b != 1 and x // CX != 1:
                        result = result * (inside_y[b] * inside_x[x // CX])
                    elif b != 1:
                        result = result * inside_y[b]
                    elif x // CX != 1:
                        result = result * inside_x[x // CX]
                new[b][x] = result
        us = new
    for x in range(CX):
        for v in range(NVEC):
            out_ref[v, x] = us[1][CX + x][v * CY : (v + 1) * CY]


def swapped(array, axis, first):
    pairs = [(i, i + 1) for i in range(first, lax.axis_size(axis) - 1, 2)]
    return lax.ppermute(array, axis, pairs + [(b, a) for a, b in pairs])


def cost(flops, size):
    return pl.CostEstimate(flops=flops, bytes_accessed=size, transcendentals=0)


def in_hbm(*arrays):
    return [pltpu.with_memory_space_constraint(a, pltpu.HBM) for a in arrays]


def in_vmem(*arrays):
    return [pltpu.with_memory_space_constraint(a, pltpu.VMEM) for a in arrays]


def params(mib):
    return pltpu.CompilerParams(vmem_limit_bytes=mib * MIB)


def per_device(
    vectors, lr_left, lr_right, tile_rank, leaf_values, leaf_places, cluster_perm, kappa
):
    vmem = pl.BlockSpec(memory_space=pltpu.VMEM)
    hbm = pl.BlockSpec(memory_space=pltpu.HBM)
    points = COLS * PTS
    terms = TILE_ROWS * TILE_COLS * KMAX
    packed_shape = (ROWS, NVEC, PTS + PTS // NVEC)
    packed, kappa_own = pl.pallas_call(
        pack_kernel,
        out_shape=(
            pltpu.VMEM(packed_shape, BF16),
            pltpu.VMEM((CX, CY, NZ), F32),
        ),
        in_specs=[hbm] * 2,
        out_specs=(vmem,) * 2,
        scratch_shapes=[pltpu.VMEM((NVEC, PTS), BF16), pltpu.SemaphoreType.DMA((2,))],
        compiler_params=params(8),
        name="pack",
    )(*in_hbm(vectors[:, 0], kappa))
    packed = lax.all_to_all(packed, "row", 0, 0, tiled=True)
    perm, ranks, rank, place, right = pl.pallas_call(
        slots_kernel,
        out_shape=(
            pltpu.VMEM((1, points), jnp.int32),
            pltpu.VMEM((1, TILE_ROWS * TILE_COLS), jnp.int32),
            pltpu.VMEM((1, points), F32),
            pltpu.VMEM((DEV, 128), jnp.int32),
            pltpu.VMEM((terms, TS), BF16),
        ),
        in_specs=[hbm] * 3,
        out_specs=(vmem,) * 5,
        scratch_shapes=[pltpu.SemaphoreType.DMA((3,))],
        compiler_params=params(16),
        cost_estimate=cost(1 << 31, 1 << 20),
        name="slots",
    )(*in_hbm(cluster_perm, tile_rank[0], lr_right.reshape(terms, TS)))
    send = pl.pallas_call(
        send_kernel,
        out_shape=jax.ShapeDtypeStruct((DEV * SLAB, 128), jnp.int32),
        in_specs=[hbm] * 3 + [vmem] * 6,
        out_specs=vmem,
        scratch_shapes=[
            pltpu.VMEM((terms, TS), BF16),
            pltpu.VMEM((NLEAF, LEAF, LEAF), BF16),
            pltpu.VMEM((16, TS), F32),
            pltpu.VMEM((16, TS), F32),
            pltpu.SMEM((2, NLEAF), jnp.int32),
            pltpu.SemaphoreType.DMA((1 + PIECES + len(LEAF_PIECES),)),
        ],
        compiler_params=params(32),
        cost_estimate=cost(1 << 31, 8 << 20),
        name="partial_sums",
    )(
        *in_hbm(leaf_places[0, 0].T, lr_left.reshape(terms, TS), leaf_values[0, 0]),
        *in_vmem(packed, ranks, perm, rank, place, right),
    )
    got = lax.all_to_all(send.reshape(DEV, SLAB, 1, 128), ("row", "col"), 0, 0, tiled=True)
    own, halo = pl.pallas_call(
        bricks_kernel,
        out_shape=(
            pltpu.VMEM((FIELD + 3 * CX * CY, NZ), F32),
            pltpu.VMEM((MESSAGE, NZ), jnp.int16),
        ),
        in_specs=[vmem] * 3,
        out_specs=(vmem,) * 2,
        scratch_shapes=[
            pltpu.VMEM((NVEC, 6 * ROWS, 128), F32),
            pltpu.VMEM((2, 3 * ROWS, 128), F32),
            pltpu.VMEM((2, 3 * ROWS, 128), F32),
        ],
        compiler_params=params(16),
        cost_estimate=cost(1 << 30, 1 << 20),
        name="bricks",
    )(got.reshape(DEV * SLAB, 128), packed, kappa_own)
    odd = swapped(halo, "col", 1)
    even = swapped(halo, "col", 0)
    return pl.pallas_call(
        prior_kernel,
        out_shape=jax.ShapeDtypeStruct((NVEC, CX, CY, NZ), F32),
        in_specs=[vmem] * 3,
        out_specs=vmem,
        compiler_params=params(8),
        cost_estimate=cost(1 << 24, 1 << 20),
        name="prior",
    )(own, even, odd)


def solution(mesh):
    in_specs = (
        P(None, "col", "row"),
        P("row", "col", None, None, None),
        P("row", "col", None, None, None),
        P("row", "col", None),
        P("row", "col", None, None, None),
        P("row", "col", None, None),
        P("row", None),
        P("row", "col", None),
    )
    out_specs = P(None, "row", "col", None)
    return jax.shard_map(
        per_device, mesh=mesh, in_specs=in_specs, out_specs=out_specs, check_vma=False
    )
```

```python
import jax
import jax.numpy as jnp
from jax import lax
from jax.experimental import pallas as pl
from jax.experimental.pallas import tpu as pltpu
from jax.sharding import PartitionSpec as P

NVEC = 2
CX = 4
CY = 4
NZ = 128
TILE_ROWS = 4
TILE_COLS = 8
KMAX = 8
LEAF = 512
NLEAF = 8
PTS = 2048
ROWS = 16
COLS = 8
TS = 4096
CAP = 32
DEV = ROWS * COLS
PIECES = 2
LEAF_PIECES = ((0, 2), (2, 4), (4, 6), (6, 8))
SLAB = 7
F32 = jnp.float32
BF16 = jnp.bfloat16
NT = (((1,), (1,)), ((), ()))
MIB = 1 << 20
LEVELS = 64.0
STEPS = 32000.0
KAPPA_STEPS = 8000.0
FIELD = 3 * CX * NVEC * CY
HALO = FIELD - 2 * NVEC * CY
MESSAGE = HALO + 8 * CY + 16


def iota(shape, dim):
    return lax.broadcasted_iota(jnp.int32, shape, dim)


def pack_kernel(
    vectors_hbm, kappa_hbm, out_ref, kappa_ref, vectors, sems
):
    pairs = ((vectors_hbm, vectors), (kappa_hbm, kappa_ref))
    copies = [pltpu.make_async_copy(a, b, sems.at[i]) for i, (a, b) in enumerate(pairs)]
    for copy in copies:
        copy.start()
    copies[0].wait()
    for s in range(ROWS):
        out_ref[s, :, 0:PTS] = vectors[...]
    copies[1].wait()
    rows = [kappa_ref[q // CY, q % CY : q % CY + 1, :] for q in range(CX * CY)]
    half = CX * CY // NVEC
    for q in range(half):
        pair = jnp.concatenate([rows[q], rows[half + q]], axis=0).astype(BF16)
        for s in range(ROWS):
            out_ref[s, :, PTS + q * NZ : PTS + (q + 1) * NZ] = pair


def beside(values):
    none = jnp.zeros((COLS, values.shape[1]), jnp.int32)
    last = DEV - COLS
    return [
        jnp.concatenate([none, values[:last]], axis=0),
        values,
        jnp.concatenate([values[COLS:], none], axis=0),
    ]


def slots_kernel(
    perm_hbm, tile_hbm, right_hbm, perm_ref, tile_ref, rank_ref, place_ref, right, sems
):
    pairs = ((perm_hbm, perm_ref), (tile_hbm, tile_ref), (right_hbm, right))
    copies = [pltpu.make_async_copy(a, b, sems.at[i]) for i, (a, b) in enumerate(pairs)]
    for copy in copies:
        copy.start()
    copies[0].wait()
    chunk = 256
    upto = jnp.where(iota((chunk, chunk), 0) <= iota((chunk, chunk), 1), 1.0, 0.0).astype(BF16)
    brick = iota((DEV, chunk), 0)
    carry = jnp.zeros((COLS * DEV, 1), F32)
    for j in range(PTS // chunk):
        lanes = [slice(k * PTS + j * chunk, k * PTS + (j + 1) * chunk) for k in range(COLS)]
        masks = [(perm_ref[0:1, at] >> 11) == brick for at in lanes]
        hot = jnp.concatenate([jnp.where(m, 1.0, 0.0).astype(BF16) for m in masks], axis=0)
        total = jnp.dot(hot, upto, preferred_element_type=F32) + carry
        for k in range(COLS):
            at = jnp.where(masks[k], total[k * DEV : (k + 1) * DEV], 0.0)
            rank_ref[0:1, lanes[k]] = jnp.sum(at, axis=0, keepdims=True) - 1.0
        carry = total[:, chunk - 1 : chunk]
    col = lax.axis_index("col")
    start = pl.multiple_of(col * PTS, PTS)
    own = perm_ref[0:1, pl.ds(start, PTS)]
    slot = rank_ref[0:1, pl.ds(start, PTS)]
    here = jnp.where(slot == iota((CAP, PTS), 0).astype(F32), 1.0, 0.0).astype(BF16)
    hot = jnp.where((own >> 11) == iota((DEV, PTS), 0), 1.0, 0.0).astype(BF16)
    inside = own & (PTS - 1)
    place = jnp.zeros((DEV, CAP), F32)
    for part in (inside & ~(NZ - 1), (inside & (NZ - 1)) + 1):
        spread = here * part.astype(F32).astype(BF16)
        place = place + lax.dot_general(hot, spread, NT, preferred_element_type=F32)
    place = place.astype(jnp.int32)
    place_ref[...] = jnp.concatenate(beside(place) + [jnp.zeros((DEV, CAP), jnp.int32)], axis=1)
    copies[1].wait()
    copies[2].wait()


def level_of(values):
    largest = jnp.max(jnp.abs(values), axis=0, keepdims=True)
    largest = jnp.broadcast_to(jnp.max(largest, axis=1, keepdims=True), (8, 128))
    level = jnp.ceil(jnp.maximum(jnp.log2(largest), -100.0) * LEVELS)
    return level[0:1], (STEPS * jnp.exp2(level * (-1.0 / LEVELS)))[0:1]


def step_at(level):
    return jnp.exp2(level * (1.0 / LEVELS)) * (1.0 / STEPS)


def send_kernel(
    leaf_at_hbm,
    left_hbm,
    leaf_hbm,
    x_ref,
    tile_rank_ref,
    perm_ref,
    rank_ref,
    place_ref,
    right,
    out_ref,
    left,
    leaves,
    x_rows,
    sums,
    leaf_at,
    sems,
):
    pairs = [(leaf_at_hbm, leaf_at)]
    wide = TS // PIECES
    for i in range(PIECES):
        at = pl.ds(i * wide, wide)
        pairs.append((left_hbm.at[:, at], left.at[:, at]))
    for first, last in LEAF_PIECES:
        at = pl.ds(first, last - first)
        pairs.append((leaf_hbm.at[at], leaves.at[at]))
    copies = [pltpu.make_async_copy(a, b, sems.at[i]) for i, (a, b) in enumerate(pairs)]
    for copy in copies:
        copy.start()

    def pack(low, high):
        return (high << 16) | (low & 0xFFFF)

    half = TS // PTS
    for s in range(ROWS):
        b, h = divmod(s, half)
        block = x_ref[s, :, 0:PTS].astype(F32)
        x_rows[b : b + 1, h * PTS : (h + 1) * PTS] = block[0:1]
        x_rows[8 + b : 9 + b, h * PTS : (h + 1) * PTS] = block[1:2]
    terms = TILE_ROWS * TILE_COLS * KMAX
    lane = iota((16, terms), 1)
    sub = iota((16, terms), 0)
    widen = jnp.where(
        iota((TILE_ROWS * TILE_COLS, terms), 1) // KMAX
        == iota((TILE_ROWS * TILE_COLS, terms), 0),
        1.0,
        0.0,
    ).astype(BF16)
    ranks = jnp.broadcast_to(tile_rank_ref[...].astype(F32), (16, TILE_ROWS * TILE_COLS))
    rank_lane = jnp.dot(ranks.astype(BF16), widen, preferred_element_type=F32)
    keep = (sub % 8 == (lane // KMAX) % TILE_COLS) & ((lane % KMAX).astype(F32) < rank_lane)
    x_all = x_rows[...].astype(BF16)
    projected = lax.dot_general(x_all, right[...], NT, preferred_element_type=F32)
    projected = jnp.where(keep, projected, 0.0)
    first = jnp.sum(projected[0:8], axis=0, keepdims=True)
    second = jnp.sum(projected[8:16], axis=0, keepdims=True)
    by_row = jnp.where(sub < 8, first, second)
    by_row = jnp.where(sub % 8 == lane // (TILE_COLS * KMAX), by_row, 0.0).astype(BF16)
    for i in range(PIECES):
        copies[1 + i].wait()
        at = (slice(None), slice(i * wide, (i + 1) * wide))
        sums[at] = jnp.dot(by_row, left[at], preferred_element_type=F32)
    copies[0].wait()
    per_tile = TS // LEAF
    for l in range(NLEAF):
        for n, (first, _) in enumerate(LEAF_PIECES):
            if l == first:
                copies[1 + PIECES + n].wait()
        i, j = leaf_at[0, l], leaf_at[1, l]
        from_lane = pl.multiple_of((j % per_tile) * LEAF, LEAF)
        to_lane = pl.multiple_of((i % per_tile) * LEAF, LEAF)
        picked = jnp.concatenate(
            [x_rows[pl.ds(8 * v + j // per_tile, 1), pl.ds(from_lane, LEAF)] for v in range(NVEC)],
            axis=0,
        ).astype(BF16)
        near = lax.dot_general(picked, leaves[l], NT, preferred_element_type=F32)
        for v in range(NVEC):
            at = (pl.ds(8 * v + i // per_tile, 1), pl.ds(to_lane, LEAF))
            sums[at] = sums[at] + near[v : v + 1]
    level, inverse = level_of(sums[...])
    out_ref[pl.ds(6, DEV, stride=SLAB), :] = jnp.where(
        iota((DEV, 128), 1) < 3 * CAP, place_ref[...], level.astype(jnp.int32)
    )
    one, none = jnp.ones((), BF16), jnp.zeros((), BF16)

    def numbers(count):
        return iota((count, PTS), 0).astype(F32).astype(BF16)

    for group in range(2):
        parts = []
        for kk in range(4):
            k = group * 4 + kk
            a, h = divmod(k, half)
            at = slice(k * PTS, (k + 1) * PTS)
            slot = rank_ref[0:1, at].astype(BF16) == numbers(CAP)
            slot = jnp.where(slot, one, none)
            rows = [sums[8 * v + a : 8 * v + a + 1, h * PTS : (h + 1) * PTS] for v in range(NVEC)]
            highs = [row.astype(BF16) for row in rows]
            lows = [(row - high.astype(F32)).astype(BF16) for row, high in zip(rows, highs)]
            spread = jnp.concatenate([slot * row for row in highs + lows], axis=0)
            hot = (perm_ref[0:1, at] >> 11).astype(F32).astype(BF16) == numbers(DEV)
            hot = jnp.where(hot, one, none)
            part = lax.dot_general(hot, spread, NT, preferred_element_type=F32)
            parts.append(part + pltpu.roll(part, NVEC * CAP, 1))
        words = pack(
            *(
                jnp.round(
                    jnp.concatenate([p[:, v * CAP : (v + 1) * CAP] for p in parts], axis=1) * inverse
                ).astype(jnp.int32)
                for v in range(NVEC)
            )
        )
        for j, moved in enumerate(beside(words)):
            out_ref[pl.ds(j * 2 + group, DEV, stride=SLAB), :] = moved


def bricks_kernel(
    got_ref, packed_ref, kappa_ref, out_ref, halo_ref, sums, wheres, at_cells
):
    def of_all_rows(c, q):
        return got_ref[pl.ds(c * SLAB + q, ROWS, stride=COLS * SLAB), :]

    last = [of_all_rows(c, 6).astype(F32) for c in range(COLS)]
    sizes = [
        step_at(jnp.broadcast_to(one[:, 3 * CAP : 3 * CAP + 1], (ROWS, 128))) for one in last
    ]
    for q in range(6):
        totals = [jnp.zeros((ROWS, 128), F32)] * NVEC
        for c in range(COLS):
            words = of_all_rows(c, q)
            pair = ((words << 16) >> 16, words >> 16)
            totals = [t + w.astype(F32) * sizes[c] for t, w in zip(totals, pair)]
        for v in range(NVEC):
            sums[v, q * ROWS : (q + 1) * ROWS, :] = totals[v]
    level, inverse = level_of(jnp.maximum(jnp.abs(sums[0]), jnp.abs(sums[1])))
    part = iota((ROWS, 128), 1) // CAP
    for g in range(2):
        for j in range(3):
            place = jnp.full((ROWS, 128), -1.0, F32)
            for kk in range(4):
                moved = pltpu.roll(last[g * 4 + kk], (kk - j) * CAP % 128, 1)
                place = place + jnp.where(part == kk, moved, 0.0)
            cell = jnp.floor(place * (1.0 / NZ))
            at_cells[g, j * ROWS : (j + 1) * ROWS, :] = cell
            wheres[g, j * ROWS : (j + 1) * ROWS, :] = place - cell * NZ
    sub = iota((8, 128), 0)
    z_row = iota((NZ, 128), 0).astype(F32).astype(BF16)
    one, none = jnp.ones((), BF16), jnp.zeros((), BF16)
    for j in range(3):
        both = jnp.zeros((64, NZ), F32)
        for some in range(0, ROWS, 4):
            cells, heights = [], []
            for r, g in ((r, g) for r in range(some, some + 4) for g in range(2)):
                at = (j * 2 + g) * ROWS + r
                pair = jnp.where(sub < 4, sums[0, at : at + 1, :], sums[1, at : at + 1, :])
                p = j * ROWS + r
                cell = at_cells[g, p : p + 1, :]
                wanted = [cell == (x * CY + sub % CY).astype(F32) for x in range(CX)]
                rows = jnp.concatenate([jnp.where(w, pair, 0.0) for w in wanted], axis=0)
                high = rows.astype(BF16)
                low = (rows - high.astype(F32)).astype(BF16)
                cells.append(jnp.concatenate([high, low], axis=0))
                z_at = wheres[g, p : p + 1, :].astype(BF16)
                heights.append(jnp.where(z_at == z_row, one, none))
            both = both + lax.dot_general(
                jnp.concatenate(cells, axis=1),
                jnp.concatenate(heights, axis=1),
                NT,
                preferred_element_type=F32,
            )
        out_ref[j * 32 : (j + 1) * 32, :] = both[0:32] + both[32:64]
    my_row = lax.axis_index("row")
    half = CX * CY // NVEC
    for j, r in ((0, jnp.maximum(my_row - 1, 0)), (2, jnp.minimum(my_row + 1, ROWS - 1))):
        block = packed_ref[r, :, PTS:].astype(F32)
        for q in range(half):
            for v in range(NVEC):
                at = FIELD + j * CX * CY + v * half + q
                out_ref[at : at + 1, :] = block[v : v + 1, q * NZ : (q + 1) * NZ]
    for x in range(CX):
        at = FIELD + CX * CY + x * CY
        out_ref[at : at + CY, :] = kappa_ref[x]

    def store(at, values):
        halo_ref[at : at + values.shape[0], :] = (
            jnp.round(values).astype(jnp.int32).astype(jnp.int16)
        )

    store(0, out_ref[8 : FIELD - 8, :] * inverse)
    store(HALO, out_ref[FIELD + 2 * CY : FIELD + 10 * CY, :] * KAPPA_STEPS)
    store(HALO + 8 * CY, jnp.broadcast_to(level, (16, 128)))


def prior_kernel(own_ref, even_ref, odd_ref, out_ref):
    my_row, my_col = lax.axis_index("row"), lax.axis_index("col")
    wide = 3 * CX
    inside_x = [
        jnp.where(my_row > 0, 1.0, 0.0),
        jnp.float32(1.0),
        jnp.where(my_row < ROWS - 1, 1.0, 0.0),
    ]
    inside_y = [
        jnp.where(my_col > 0, 1.0, 0.0),
        jnp.float32(1.0),
        jnp.where(my_col < COLS - 1, 1.0, 0.0),
    ]
    y_at = iota((8, NZ), 0) % CY
    z_at = iota((8, NZ), 1)
    none = jnp.zeros((8, NZ), F32)
    us, ks = [], []
    even, odd = (ref[...].astype(jnp.int32).astype(F32) for ref in (even_ref, odd_ref))
    at_even = jnp.broadcast_to(my_col % 2, (MESSAGE, NZ)) == 0
    before, after = jnp.where(at_even, odd, even), jnp.where(at_even, even, odd)
    for b, got in enumerate((before, None, after)):
        if got is None:
            field = [own_ref[8 * x : 8 * x + 8, :] for x in range(wide)]
            rows = [own_ref[FIELD + CY * x : FIELD + CY * (x + 1), :] for x in range(wide)]
            kappas = [6.0 + jnp.concatenate([row, row], axis=0) for row in rows]
        else:
            values = got[0:HALO] * (step_at(got[HALO + 8 * CY : HALO + 8 * CY + 1]) * inside_y[b])
            field = [values[8 * x : 8 * x + 8] for x in range(wide - 2)]
            field = [none] + field + [none]
            values = got[HALO : HALO + 8 * CY] * (1.0 / KAPPA_STEPS) + 6.0
            rows = [values[CY * x : CY * (x + 1)] for x in range(8)]
            kappas = [none] * 2 + [jnp.concatenate([row, row], axis=0) for row in rows] + [none] * 2
        us.append(field)
        ks.append(kappas)
    for step in range(1, 5):
        new = [[None] * wide for _ in range(3)]
        for b in range(3):
            if step == 4 and b != 1:
                continue
            edge = step if b == 1 else step + 1
            for x in range(edge, wide - edge):
                u = us[b][x]
                lower = pltpu.roll(us[b - 1][x], 5, 0) if b > 0 and us[b - 1][x] is not None else 0.0
                upper = pltpu.roll(us[b + 1][x], 3, 0) if b < 2 and us[b + 1][x] is not None else 0.0
                beside = us[b][x - 1] + us[b][x + 1]
                beside = beside + jnp.where(y_at == 0, lower, pltpu.roll(u, 1, 0))
                beside = beside + jnp.where(y_at == CY - 1, upper, pltpu.roll(u, 7, 0))
                beside = beside + jnp.where(z_at == 0, 0.0, pltpu.roll(u, 1, 1))
                beside = beside + jnp.where(z_at == NZ - 1, 0.0, pltpu.roll(u, NZ - 1, 1))
                result = (ks[b][x] * u - beside) * 0.125
                if step < 4:
                    if b != 1 and x // CX != 1:
                        result = result * (inside_y[b] * inside_x[x // CX])
                    elif b != 1:
                        result = result * inside_y[b]
                    elif x // CX != 1:
                        result = result * inside_x[x // CX]
                new[b][x] = result
        us = new
    for x in range(CX):
        for v in range(NVEC):
            out_ref[v, x] = us[1][CX + x][v * CY : (v + 1) * CY]


def swapped(array, axis, first):
    pairs = [(i, i + 1) for i in range(first, lax.axis_size(axis) - 1, 2)]
    return lax.ppermute(array, axis, pairs + [(b, a) for a, b in pairs])


def cost(flops, size):
    return pl.CostEstimate(flops=flops, bytes_accessed=size, transcendentals=0)


def in_hbm(*arrays):
    return [pltpu.with_memory_space_constraint(a, pltpu.HBM) for a in arrays]


def in_vmem(*arrays):
    return [pltpu.with_memory_space_constraint(a, pltpu.VMEM) for a in arrays]


def params(mib):
    return pltpu.CompilerParams(vmem_limit_bytes=mib * MIB)


def per_device(
    vectors, lr_left, lr_right, tile_rank, leaf_values, leaf_places, cluster_perm, kappa
):
    vmem = pl.BlockSpec(memory_space=pltpu.VMEM)
    hbm = pl.BlockSpec(memory_space=pltpu.HBM)
    points = COLS * PTS
    terms = TILE_ROWS * TILE_COLS * KMAX
    packed_shape = (ROWS, NVEC, PTS + PTS // NVEC)
    packed, kappa_own = pl.pallas_call(
        pack_kernel,
        out_shape=(
            pltpu.VMEM(packed_shape, BF16),
            pltpu.VMEM((CX, CY, NZ), F32),
        ),
        in_specs=[hbm] * 2,
        out_specs=(vmem,) * 2,
        scratch_shapes=[pltpu.VMEM((NVEC, PTS), BF16), pltpu.SemaphoreType.DMA((2,))],
        compiler_params=params(8),
        name="pack",
    )(*in_hbm(vectors[:, 0], kappa))
    packed = lax.all_to_all(packed, "row", 0, 0, tiled=True)
    perm, ranks, rank, place, right = pl.pallas_call(
        slots_kernel,
        out_shape=(
            pltpu.VMEM((1, points), jnp.int32),
            pltpu.VMEM((1, TILE_ROWS * TILE_COLS), jnp.int32),
            pltpu.VMEM((1, points), F32),
            pltpu.VMEM((DEV, 128), jnp.int32),
            pltpu.VMEM((terms, TS), BF16),
        ),
        in_specs=[hbm] * 3,
        out_specs=(vmem,) * 5,
        scratch_shapes=[pltpu.SemaphoreType.DMA((3,))],
        compiler_params=params(16),
        cost_estimate=cost(1 << 31, 1 << 20),
        name="slots",
    )(*in_hbm(cluster_perm, tile_rank[0], lr_right.reshape(terms, TS)))
    send = pl.pallas_call(
        send_kernel,
        out_shape=jax.ShapeDtypeStruct((DEV * SLAB, 128), jnp.int32),
        in_specs=[hbm] * 3 + [vmem] * 6,
        out_specs=vmem,
        scratch_shapes=[
            pltpu.VMEM((terms, TS), BF16),
            pltpu.VMEM((NLEAF, LEAF, LEAF), BF16),
            pltpu.VMEM((16, TS), F32),
            pltpu.VMEM((16, TS), F32),
            pltpu.SMEM((2, NLEAF), jnp.int32),
            pltpu.SemaphoreType.DMA((1 + PIECES + len(LEAF_PIECES),)),
        ],
        compiler_params=params(32),
        cost_estimate=cost(1 << 31, 8 << 20),
        name="partial_sums",
    )(
        *in_hbm(leaf_places[0, 0].T, lr_left.reshape(terms, TS), leaf_values[0, 0]),
        *in_vmem(packed, ranks, perm, rank, place, right),
    )
    got = lax.all_to_all(send.reshape(DEV, SLAB, 1, 128), ("row", "col"), 0, 0, tiled=True)
    own, halo = pl.pallas_call(
        bricks_kernel,
        out_shape=(
            pltpu.VMEM((FIELD + 3 * CX * CY, NZ), F32),
            pltpu.VMEM((MESSAGE, NZ), jnp.int16),
        ),
        in_specs=[vmem] * 3,
        out_specs=(vmem,) * 2,
        scratch_shapes=[
            pltpu.VMEM((NVEC, 6 * ROWS, 128), F32),
            pltpu.VMEM((2, 3 * ROWS, 128), F32),
            pltpu.VMEM((2, 3 * ROWS, 128), F32),
        ],
        compiler_params=params(16),
        cost_estimate=cost(1 << 30, 1 << 20),
        name="bricks",
    )(got.reshape(DEV * SLAB, 128), packed, kappa_own)
    odd = swapped(halo, "col", 1)
    even = swapped(halo, "col", 0)
    return pl.pallas_call(
        prior_kernel,
        out_shape=jax.ShapeDtypeStruct((NVEC, CX, CY, NZ), F32),
        in_specs=[vmem] * 3,
        out_specs=vmem,
        compiler_params=params(8),
        cost_estimate=cost(1 << 24, 1 << 20),
        name="prior",
    )(own, even, odd)


def solution(mesh):
    in_specs = (
        P(None, "col", "row"),
        P("row", "col", None, None, None),
        P("row", "col", None, None, None),
        P("row", "col", None),
        P("row", "col", None, None, None),
        P("row", "col", None, None),
        P("row", None),
        P("row", "col", None),
    )
    out_specs = P(None, "row", "col", None)
    return jax.shard_map(
        per_device, mesh=mesh, in_specs=in_specs, out_specs=out_specs, check_vma=False
    )
```
